32 devices in a mesh: groups: 2 (over x), dom: 16 (over z, y, core).
Axes of the slice: x: 2, y: 2, z: 4, core: 2. Of those that a mesh axis runs over, the one named last changes fastest.
Arguments:
- start_block: bfloat16 [32, 262144], P(None, ('groups', 'dom')), parts along dimension 1
- tiles: bfloat16 [10240, 128, 128], P(('groups', 'dom')), parts along dimension 0
- tile_src: int32 [10240], P(('groups', 'dom')), parts along dimension 0, may hold values from 0 to 111, as said below
- tile_dst: int32 [10240], P(('groups', 'dom')), parts along dimension 0, may hold values from 0 to 63
- slot_count: int32 [32], P(('groups', 'dom')), parts along dimension 0, may hold values from 112 to 320, as said below
- send_rows: int32 [32, 4, 1536], P(('groups', 'dom')), parts along dimension 0, may hold values from 0 to 8191
Outputs:
- subspace: float32 [32, 262144], P(None, ('groups', 'dom')), parts along dimension 1
The draws below stay inside these ranges and needn't reach their ends.
There are 2 independent parts, one for each index of `groups`. The reference program is written for one: setup_inputs(seed, part) draws one part's arguments, and reference() takes and returns one part's arrays. A program takes and returns all parts, laid end to end along the dimension named above; each array names one. Nothing has to cross between parts.
Inputs may be any that keep to these rules, and one draw needn't show every extreme that they name: `tile_src`: slot t < 64 of every partition has source tile t and target tile t; slot 64 + g for g < 48 has source tile 64 + g, the g-th tile of received boundary rows; the other slots may name any local or received tile. Slots at local positions from slot_count on are ignored. Some partition uses all 320 slots. `send_rows`: indices may repeat.
All inputs are finite; a program needn't handle non-finite values.
Results may differ from the reference program's by a relative error of at most 0.0025.
Values may be sent and summed in bfloat16 or wider, within the bound.
No kernel may reach another device: no remote copies, remote signals or barrier semaphores. Data moves between devices by JAX's collectives and lax.ppermute only.
A program may use at most 64 MiB of HBM per device.

```python
import math
import jax
import jax.numpy as jnp
import numpy as np
from jax import lax

K = 32
TS = 128
TL = 64
NROUND = 4
ITERS = 3
S_DEV = 8192
SLOTS = 320
BR = 1536
NG = 48
STATES = 131072
TILES = 5120
N_DOM = 16


def slot_layout(key):
    layout_key = jax.random.fold_in(key, 101)
    key_src, key_dst, key_load, key_heavy = jax.random.split(layout_key, 4)
    partitions = TILES // SLOTS
    slot_index = jnp.arange(SLOTS, dtype=jnp.int32)[None, :]
    random_src = jax.random.randint(key_src, (partitions, SLOTS), 0, TL + NG, dtype=jnp.int32)
    random_dst = jax.random.randint(key_dst, (partitions, SLOTS), 0, TL, dtype=jnp.int32)
    sources = jnp.where(slot_index < TL + NG, slot_index, random_src)
    targets = jnp.where(slot_index < TL, slot_index, random_dst)
    loads = jax.random.randint(key_load, (partitions,), TL + NG, 2 * TL + NG, dtype=jnp.int32)
    heavy = jax.random.randint(key_heavy, (), 0, partitions, dtype=jnp.int32)
    loads = jnp.where(jnp.arange(partitions, dtype=jnp.int32) == heavy, SLOTS, loads)
    return (sources.reshape(-1), targets.reshape(-1), loads)


def draw_tile_src(key, part):
    return slot_layout(key)[0]


def draw_tile_dst(key, part):
    return slot_layout(key)[1]


def draw_slot_count(key, part):
    return slot_layout(key)[2]


def draw_tiles(key, part):
    sources, targets, loads = slot_layout(key)
    value_key = jax.random.fold_in(key, 202)
    key_diag, key_off = jax.random.split(value_key, 2)
    partitions = TILES // SLOTS
    uniform_part = jax.random.uniform(key_off, (TILES, TS, TS), jnp.float32)
    diagonal = jnp.exp(jax.random.uniform(key_diag, (TILES, 1, TS), jnp.float32, math.log(0.5), math.log(2.0)))
    spread = jnp.exp(math.log(0.5) + uniform_part * math.log(4.0)) * (12.0 / (TS - 1))
    slot_index = jnp.tile(jnp.arange(SLOTS, dtype=jnp.int32), partitions)
    others = jnp.repeat(loads - TL, SLOTS).astype(jnp.float32)
    weight = jnp.where(slot_index < TL, 0.5, TL / others)[:, None, None]
    identity = jnp.eye(TS, dtype=jnp.float32)[None, :, :]
    values = weight * diagonal * (identity + spread * (1.0 - identity))
    return values.astype(jnp.bfloat16)


def draw_start_block(key, part):
    block_key = jax.random.fold_in(key, 303)
    key_base, key_cols, key_states, key_common = jax.random.split(block_key, 4)
    ramp_factor = 1.0 + 2.0 * jnp.arange(STATES, dtype=jnp.float32) / (STATES - 1)
    columns = jnp.exp(jax.random.uniform(key_cols, (K, 1), jnp.float32, 0.0, math.log(10.0)))
    states = jnp.exp(jax.random.uniform(key_states, (1, STATES), jnp.float32, 0.0, math.log(10.0)))
    base = jnp.clip(jax.random.normal(key_base, (K, STATES), jnp.float32), -4.0, 4.0)
    base = base + jax.random.uniform(key_common, (1, STATES), jnp.float32, 0.5, 1.5)
    return (0.1 * base * columns * states * ramp_factor[None, :]).astype(jnp.bfloat16)


def plant(values, stream_key, least, largest):
    longest = values.shape.index(max(values.shape))
    spots = []
    for shift in (0, 1):
        where = [jax.random.randint(jax.random.fold_in(stream_key, axis), (), 0, length) for axis, length in enumerate(values.shape)]
        where[longest] = (where[longest] + shift) % values.shape[longest]
        spots.append(tuple(where))
    return values.at[spots[0]].set(least).at[spots[1]].set(largest)


def setup_inputs(seed: int = 0, part: int = 0) -> dict:
    keys = jax.random.split(jax.random.key(seed), 7)
    part_keys = jax.random.split(jax.random.fold_in(keys[6], part), 7)
    start_block = draw_start_block(jax.random.fold_in(jax.random.fold_in(keys[6], part), 71), part)
    tiles = draw_tiles(jax.random.fold_in(jax.random.fold_in(keys[6], part), 71), part)
    tile_src = draw_tile_src(jax.random.fold_in(jax.random.fold_in(keys[6], part), 71), part)
    tile_dst = draw_tile_dst(jax.random.fold_in(jax.random.fold_in(keys[6], part), 71), part)
    slot_count = draw_slot_count(jax.random.fold_in(jax.random.fold_in(keys[6], part), 71), part)
    send_rows = plant(jax.random.randint(part_keys[5], (N_DOM, NROUND, BR), 0, S_DEV), jax.random.fold_in(part_keys[5], 1), 0, S_DEV - 1).astype(jnp.int32)
    return dict(start_block=start_block, tiles=tiles, tile_src=tile_src, tile_dst=tile_dst, slot_count=slot_count, send_rows=send_rows)


def partition_product(operands):
    source, tiles_part, src_part, dst_part, used_slots = operands
    pieces = source.reshape(K, -1, TS).transpose(1, 0, 2)
    chosen = pieces[src_part].astype(jnp.float32)
    partials = jnp.einsum('ski,sij->skj', chosen, tiles_part.astype(jnp.float32))
    live_mask = jnp.arange(SLOTS) < used_slots
    onehot = ((dst_part[:, None] == jnp.arange(TL)[None, :]) & live_mask[:, None]).astype(jnp.float32)
    summed = jnp.einsum('st,skj->ktj', onehot, partials, precision=lax.Precision.HIGHEST)
    return summed.reshape(K, S_DEV)

def reference(start_block, tiles, tile_src, tile_dst, slot_count, send_rows):
    partitions = STATES // S_DEV
    top_bit = int(partitions).bit_length() - 2
    colour_bits = [0, 1, 2, top_bit]
    owners = np.arange(partitions)
    tiles_part = tiles.reshape(partitions, SLOTS, TS, TS)
    src_part = tile_src.reshape(partitions, SLOTS)
    dst_part = tile_dst.reshape(partitions, SLOTS)
    current = start_block
    subspace = None
    for sweep_index in range(ITERS):
        local_block = current.reshape(K, partitions, S_DEV).transpose(1, 0, 2)
        ghosts = []
        for colour in range(NROUND):
            partners = owners ^ 1 << colour_bits[colour]
            partner_blocks = local_block[partners]
            positions = send_rows[partners, colour, :]
            positions = jnp.broadcast_to(positions[:, None, :], (partitions, K, BR))
            ghosts.append(jnp.take_along_axis(partner_blocks, positions, axis=2))
        source = jnp.concatenate([local_block] + ghosts, axis=2)
        product = lax.map(partition_product, (source, tiles_part, src_part, dst_part, slot_count))
        product = product.transpose(1, 0, 2).reshape(K, STATES)
        gram_sum = jnp.dot(product, product.T, precision=lax.Precision.HIGHEST) / STATES
        lower_factor = jnp.linalg.cholesky(gram_sum)
        inverse = lax.linalg.triangular_solve(lower_factor, jnp.eye(K, dtype=jnp.float32), left_side=True, lower=True)
        subspace = jnp.dot(inverse, product, precision=lax.Precision.HIGHEST)
        current = subspace.astype(jnp.bfloat16)
    return subspace
```

```python
import jax
import jax.numpy as jnp
from jax import lax
from jax.sharding import PartitionSpec as P

ITERS = 3


def swapped(x, axis, bit):
    return lax.ppermute(x, axis, [(i, i ^ 1 << bit) for i in range(lax.axis_size(axis))])


def summed_over_dom(x):
    size = lax.axis_size("dom")
    step = 1
    while step < size:
        span = min(4, size // step)
        others = [
            lax.ppermute(x, "dom", [(i, i ^ step * k) for i in range(size)])
            for k in range(1, span)
        ]
        for other in others:
            x = x + other
        step *= span
    return x


def on_device(start_block, tiles, tile_src, tile_dst, slot_count, send_rows):
    top_bit = lax.axis_size("dom").bit_length() - 2
    colour_bits = (0, 1, 2, top_bit)
    columns = start_block.shape[0]
    states_dev = start_block.shape[1]
    tile_size = tiles.shape[1]
    local_tiles = states_dev // tile_size
    total_states = states_dev * lax.axis_size("dom")
    live_count = slot_count[0]
    send_lists = send_rows[0]
    current = start_block
    received = []
    for colour in range(len(colour_bits)):
        chosen = jnp.take(current, send_lists[colour], axis=1)
        received.append(swapped(chosen, "dom", colour_bits[colour]))
    ghosts = jnp.concatenate(received, axis=1)
    subspace = None
    for sweep_index in range(ITERS):
        final_turn = sweep_index == ITERS - 1
        slot_pieces = (
            jnp.concatenate([current, ghosts], axis=1)
            .reshape(columns, -1, tile_size)
            .transpose(1, 0, 2)
        )
        slot_chosen = slot_pieces[tile_src]
        partials = jnp.einsum(
            "ski,sij->skj", slot_chosen, tiles, preferred_element_type=jnp.float32
        )
        slot_ids = jnp.arange(tile_src.shape[0], dtype=jnp.int32)
        live_mask = slot_ids < live_count
        onehot = (
            (tile_dst[:, None] == jnp.arange(local_tiles, dtype=jnp.int32)[None, :])
            & live_mask[:, None]
        ).astype(jnp.float32)
        summed = jnp.einsum("st,skj->ktj", onehot, partials, precision=lax.Precision.HIGHEST)
        product = summed.reshape(columns, states_dev)
        partial_gram = jnp.dot(product, product.T, precision=lax.Precision.HIGHEST) / total_states
        gram_sum = summed_over_dom(partial_gram)
        lower_factor = jnp.linalg.cholesky(gram_sum)
        inverse = lax.linalg.triangular_solve(
            lower_factor, jnp.eye(columns, dtype=jnp.float32), left_side=True, lower=True
        )
        subspace = jnp.dot(inverse, product, precision=lax.Precision.HIGHEST)
        if not final_turn:
            current = subspace.astype(jnp.bfloat16)
            later_received = []
            for later_colour in range(len(colour_bits)):
                later_chosen = jnp.take(current, send_lists[later_colour], axis=1)
                later_received.append(swapped(later_chosen, "dom", colour_bits[later_colour]))
            ghosts = jnp.concatenate(later_received, axis=1)
    return subspace


def solution(mesh):
    return jax.shard_map(
        on_device,
        mesh=mesh,
        in_specs=(
            P(None, ("groups", "dom")),
            P(("groups", "dom"), None, None),
            P(("groups", "dom")),
            P(("groups", "dom")),
            P(("groups", "dom")),
            P(("groups", "dom"), None, None),
        ),
        out_specs=P(None, ("groups", "dom")),
        check_vma=False,
    )
```

```python
import functools

import jax
import jax.numpy as jnp
from jax import lax
from jax.experimental import pallas as pl
from jax.experimental.pallas import tpu as pltpu
from jax.sharding import PartitionSpec as P

ITERS = 3
LANES = 128
PACK = 4
CHUNK = 1024
F32 = jnp.float32
BF16 = jnp.bfloat16
VMEM = pl.BlockSpec(memory_space=pltpu.VMEM)
SMEM = pl.BlockSpec(memory_space=pltpu.SMEM)
PARAMS = pltpu.CompilerParams(vmem_limit_bytes=32 << 20)


def in_vmem(x):
    return pltpu.with_memory_space_constraint(x, pltpu.VMEM)


def vmem_out(shape, dtype):
    return pltpu.VMEM(shape, dtype)


def swapped(x, mask):
    size = lax.axis_size("dom")
    return lax.ppermute(x, "dom", [(i, i ^ mask) for i in range(size)])


def split3(x):
    high = x.astype(BF16)
    rest = x - high.astype(F32)
    mid = rest.astype(BF16)
    low = (rest - mid.astype(F32)).astype(BF16)
    return high, mid, low


def stack3(x):
    return jnp.concatenate(split3(x), axis=0)


def inverse_factor(gram):
    n = gram.shape[0]
    row = lax.broadcasted_iota(jnp.int32, (n, n), 0)
    col = lax.broadcasted_iota(jnp.int32, (n, n), 1)
    eye = (row == col).astype(F32)
    both = jnp.concatenate([gram, eye, jnp.zeros((n, LANES - 2 * n), F32)], axis=1)
    rows = lax.broadcasted_iota(jnp.int32, (n, LANES), 0)
    scale = jnp.zeros((n, LANES), F32)
    for j in range(n):
        pivot = both[j : j + 1, j : j + 1]
        factor = jnp.broadcast_to(both[:, j : j + 1] / pivot, (n, LANES))
        scale = jnp.where(rows == j, jnp.broadcast_to(1.0 / jnp.sqrt(pivot), (n, LANES)), scale)
        both = both - jnp.where(rows > j, factor, 0.0) * both[j : j + 1, :]
    return (both * scale)[:, n : 2 * n]


def apply_matrix(inverse):
    high, mid, low = (t.astype(F32) for t in split3(inverse))
    zero = jnp.zeros_like(high)
    full = jnp.concatenate(
        [
            jnp.concatenate([high, high, high], axis=1),
            jnp.concatenate([mid, mid, zero], axis=1),
            jnp.concatenate([low, zero, zero], axis=1),
        ],
        axis=0,
    )
    return full.astype(BF16)


def applied(matrix, stacked):
    n = matrix.shape[0] // 3
    terms = jnp.dot(matrix, stacked, preferred_element_type=F32)
    return terms[:n] + (terms[n : 2 * n] + terms[2 * n :])


def gram_of(parts, total_states):
    (a, b), (c, d) = parts[:2], parts[2:]
    return ((a + b) + (c + d)) / total_states


def transposed_into(source, rows_ref):
    for g in range(rows_ref.shape[0] // LANES):
        pieces = [
            source[:, (PACK * g + b) * LANES : (PACK * g + b + 1) * LANES].astype(F32)
            for b in range(PACK)
        ]
        rows_ref[g * LANES : (g + 1) * LANES, :] = jnp.concatenate(pieces, axis=0).T


def gathered_into(unroll, row_ref, part_ref, rows_ref, picked, outs):
    count = picked.shape[0]
    columns = outs[0].shape[0]

    def pick(i, carry):
        for u in range(unroll):
            m = i * unroll + u
            picked[pl.ds(m, 1), :] = rows_ref[pl.ds(row_ref[m], 1), :]
        return carry

    lax.fori_loop(0, count // unroll, pick, 0)
    tiles_out = outs[0].shape[1] // LANES
    for g in range(count // LANES):
        y = picked[g * LANES : (g + 1) * LANES, :].T
        part = jnp.broadcast_to(part_ref[g : g + 1, :], (columns, LANES))
        value = y[:columns]
        for b in range(1, PACK):
            value = jnp.where(part == b, y[b * columns : (b + 1) * columns], value)
        out, t = outs[g // tiles_out], g % tiles_out
        out[:, t * LANES : (t + 1) * LANES] = value.astype(out.dtype)


def gather_kernel(unroll, row_ref, part_ref, rows_ref, *rest):
    gathered_into(unroll, row_ref, part_ref, rows_ref, rest[-1], rest[:-1])


def gather_colours(rows, row_list, part_list, count, dtype):
    indices = row_list.shape[0]
    columns = LANES // PACK
    return pl.pallas_call(
        functools.partial(gather_kernel, 64),
        out_shape=[vmem_out((columns, indices // count), dtype)] * count,
        in_specs=[SMEM, VMEM, VMEM],
        out_specs=[VMEM] * count,
        scratch_shapes=[pltpu.VMEM((indices, LANES), F32)],
        compiler_params=PARAMS,
        cost_estimate=pl.CostEstimate(flops=0, bytes_accessed=8 << 20, transcendentals=0),
        name="gather_rows",
    )(row_list, in_vmem(part_list), in_vmem(rows))


def start_rows_kernel(block_ref, rows_ref):
    transposed_into(block_ref, rows_ref)


def start_rows(block):
    return pl.pallas_call(
        start_rows_kernel,
        out_shape=vmem_out((block.shape[1] // PACK, LANES), F32),
        in_specs=[VMEM],
        out_specs=VMEM,
        compiler_params=PARAMS,
        name="start_rows",
    )(in_vmem(block))


def own_slots(block_ref, tiles_ref, own_ref):
    tile_size = tiles_ref.shape[1]
    for t in range(own_ref.shape[1] // tile_size):
        at = slice(t * tile_size, (t + 1) * tile_size)
        own_ref[:, at] = jnp.dot(block_ref[:, at], tiles_ref[t], preferred_element_type=F32)


def first_own_kernel(block_ref, tiles_ref, own_ref):
    own_slots(block_ref, tiles_ref, own_ref)


def first_own(block, tiles):
    return pl.pallas_call(
        first_own_kernel,
        out_shape=vmem_out(block.shape, F32),
        in_specs=[VMEM] * 2,
        out_specs=VMEM,
        compiler_params=PARAMS,
        name="first_own",
    )(in_vmem(block), in_vmem(tiles))


def later_own_kernel(total_states, *refs):
    grams, stacked, tiles_ref = refs[:4], refs[4], refs[5]
    block_ref, matrix_ref, own_ref = refs[6:]
    matrix = apply_matrix(inverse_factor(gram_of([r[...] for r in grams], total_states)))
    matrix_ref[...] = matrix
    for c in range(0, block_ref.shape[1], CHUNK):
        block_ref[:, c : c + CHUNK] = applied(matrix, stacked[:, c : c + CHUNK]).astype(BF16)
    own_slots(block_ref, tiles_ref, own_ref)


def later_own(grams, stacked, tiles, total_states):
    columns, states = stacked.shape[0] // 3, stacked.shape[1]
    return pl.pallas_call(
        functools.partial(later_own_kernel, total_states),
        out_shape=[
            vmem_out((columns, states), BF16),
            vmem_out((3 * columns, 3 * columns), BF16),
            vmem_out((columns, states), F32),
        ],
        in_specs=[VMEM] * 6,
        out_specs=[VMEM] * 3,
        compiler_params=PARAMS,
        name="later_own",
    )(*[in_vmem(g) for g in grams], in_vmem(stacked), in_vmem(tiles))


def product_kernel(colours, group, with_rows, *refs):
    src_ref, dst_ref, count_ref, block_ref, own_ref = refs[:5]
    ghosts, refs = refs[5 : 5 + colours], refs[5 + colours :]
    matrix_ref = None
    if ghosts[0].dtype == F32:
        matrix_ref, refs = refs[0], refs[1:]
    tiles_ref, refs = refs[0], refs[1:]
    stacked_ref, gram_ref, refs = refs[0], refs[1], refs[2:]
    if with_rows:
        rows_ref, refs = refs[0], refs[1:]
    source, total = refs
    columns, states = block_ref.shape
    slots, tile_size, _ = tiles_ref.shape
    first = states // tile_size
    live = count_ref[0]

    source[:, :states] = block_ref[...]
    at = states
    for ghost in ghosts:
        width = ghost.shape[1]
        value = ghost[...]
        if matrix_ref is not None:
            value = applied(matrix_ref[...], stack3(value)).astype(BF16)
        source[:, at : at + width] = value
        at += width
    source[:, at:] = jnp.zeros((columns, tile_size), BF16)
    nothing = at // tile_size
    total[...] = own_ref[...]

    def tile_at(s):
        index = jnp.where(s < live, src_ref[s], nothing)
        return source[:, pl.ds(pl.multiple_of(index * tile_size, tile_size), tile_size)]

    zero = jnp.zeros((columns, tile_size), BF16)

    def body(i, carry):
        base = first + i * group
        terms = []
        for u in range(0, group, 2):
            pair = jnp.concatenate(
                [
                    jnp.concatenate([tile_at(base + u), zero], axis=1),
                    jnp.concatenate([zero, tile_at(base + u + 1)], axis=1),
                ],
                axis=0,
            )
            weights = tiles_ref[pl.ds(base + u, 2)].reshape(2 * tile_size, tile_size)
            both = jnp.dot(pair, weights, preferred_element_type=F32)
            terms += [both[:columns], both[columns:]]
        for u in range(group):
            where = pl.multiple_of(dst_ref[base + u] * tile_size, tile_size)
            total[:, pl.ds(where, tile_size)] += terms[u]
        return carry

    lax.fori_loop(0, (live - first + group - 1) // group, body, 0)

    gram = jnp.zeros((3 * columns, 3 * columns), F32)
    for c in range(0, states, CHUNK):
        part = stack3(total[:, c : c + CHUNK])
        stacked_ref[:, c : c + CHUNK] = part
        gram += lax.dot_general(part, part, (((1,), (1,)), ((), ())), preferred_element_type=F32)
    blocks = [
        gram[a * columns : (a + 1) * columns, b * columns : (b + 1) * columns]
        for a in range(3)
        for b in range(3)
    ]
    small = blocks[8] + (blocks[5] + blocks[7])
    middle = blocks[4] + (blocks[2] + blocks[6])
    gram_ref[...] = blocks[0] + ((blocks[1] + blocks[3]) + (middle + small))
    if with_rows:
        transposed_into(total, rows_ref)


def product(src, dst, count, block, own, ghosts, matrix, tiles, with_rows):
    columns, states = block.shape
    slots, tile_size, _ = tiles.shape
    rest = slots - states // tile_size
    group = 64
    while rest % group:
        group //= 2
    outs = [vmem_out((3 * columns, states), BF16), vmem_out((columns, columns), F32)]
    if with_rows:
        outs.append(vmem_out((states // PACK, LANES), F32))
    operands = [block, own, *ghosts] + ([] if matrix is None else [matrix]) + [tiles]
    width = states + sum(g.shape[1] for g in ghosts) + tile_size
    return pl.pallas_call(
        functools.partial(product_kernel, len(ghosts), group, with_rows),
        out_shape=outs,
        in_specs=[SMEM] * 3 + [VMEM] * len(operands),
        out_specs=[VMEM] * len(outs),
        scratch_shapes=[pltpu.VMEM((columns, width), BF16), pltpu.VMEM((columns, states), F32)],
        compiler_params=PARAMS,
        name="product",
    )(src, dst, count, *[in_vmem(x) for x in operands])


def final_kernel(total_states, *refs):
    grams, stacked, out_ref = refs[:4], refs[4], refs[5]
    matrix = apply_matrix(inverse_factor(gram_of([r[...] for r in grams], total_states)))
    for c in range(0, out_ref.shape[1], CHUNK):
        out_ref[:, c : c + CHUNK] = applied(matrix, stacked[:, c : c + CHUNK])


def final(grams, stacked, total_states):
    columns, states = stacked.shape[0] // 3, stacked.shape[1]
    return pl.pallas_call(
        functools.partial(final_kernel, total_states),
        out_shape=jax.ShapeDtypeStruct((columns, states), F32),
        in_specs=[VMEM] * 5,
        out_specs=VMEM,
        compiler_params=PARAMS,
        name="final",
    )(*[in_vmem(g) for g in grams], in_vmem(stacked))


def dom_rounds(size):
    rounds, step = [], 1
    while step < size:
        span = min(4, size // step)
        rounds.append([step * k for k in range(1, span)])
        step *= span
    return rounds[::-1]


def gram_parts(gram, rounds):
    parts = [gram]
    for masks in rounds:
        if len(parts) > 1:
            gram = (parts[0] + parts[1]) + (parts[2] + parts[3])
        parts = [gram] + [swapped(gram, mask) for mask in masks]
        parts += [jnp.zeros_like(gram)] * (4 - len(parts))
    return parts


def on_device(start_block, tiles, tile_src, tile_dst, slot_count, send_rows):
    size = lax.axis_size("dom")
    masks = [1, 2, 4, 1 << (size.bit_length() - 2)]
    columns, states = start_block.shape
    total_states = states * size
    rounds = dom_rounds(size)
    lists = send_rows[0]
    pack_states = PACK * LANES
    row_lists = lists // pack_states * LANES + lists % LANES
    part_lists = lists // LANES % PACK
    far = (3, 2)
    near = (1, 0)

    def lists_of(colours):
        rows = jnp.concatenate([row_lists[c] for c in colours])
        parts = jnp.concatenate([part_lists[c] for c in colours]).reshape(-1, LANES)
        return rows, parts

    listed = [lists_of(far), lists_of(near)]

    def exchanged(rows, dtype):
        ghosts = [None] * len(masks)
        for colours, (row_list, part_list) in zip((far, near), listed):
            picked = gather_colours(rows, row_list, part_list, len(colours), dtype)
            for colour, x in zip(colours, picked):
                ghosts[colour] = swapped(x, masks[colour])
        return ghosts

    ghosts = exchanged(start_rows(start_block), BF16)
    block, matrix = start_block, None
    own = first_own(start_block, tiles)
    for turn in range(ITERS):
        last = turn == ITERS - 1
        stacked, gram, *rows = product(
            tile_src, tile_dst, slot_count, block, own, ghosts, matrix, tiles, not last
        )
        parts = gram_parts(gram, rounds)
        if last:
            return final(parts, stacked, total_states)
        ghosts = exchanged(rows[0], F32)
        block, matrix, own = later_own(parts, stacked, tiles, total_states)


def solution(mesh):
    return jax.shard_map(
        on_device,
        mesh=mesh,
        in_specs=(
            P(None, ("groups", "dom")),
            P(("groups", "dom"), None, None),
            P(("groups", "dom")),
            P(("groups", "dom")),
            P(("groups", "dom")),
            P(("groups", "dom"), None, None),
        ),
        out_specs=P(None, ("groups", "dom")),
        check_vma=False,
    )
```

```python
import functools

import jax
import jax.numpy as jnp
from jax import lax
from jax.experimental import pallas as pl
from jax.experimental.pallas import tpu as pltpu
from jax.sharding import PartitionSpec as P

ITERS = 3
LANES = 128
PACK = 4
CHUNK = 1024
SUBLANES = 8
STEP = 4
COPIES = 8
F32 = jnp.float32
BF16 = jnp.bfloat16
VMEM = pl.BlockSpec(memory_space=pltpu.VMEM)
SMEM = pl.BlockSpec(memory_space=pltpu.SMEM)
PARAMS = pltpu.CompilerParams(vmem_limit_bytes=32 << 20)


def in_vmem(x):
    return pltpu.with_memory_space_constraint(x, pltpu.VMEM)


def vmem_out(shape, dtype):
    return pltpu.VMEM(shape, dtype)


def swapped(x, mask):
    size = lax.axis_size("dom")
    return lax.ppermute(x, "dom", [(i, i ^ mask) for i in range(size)])


def split3(x):
    high = x.astype(BF16)
    rest = x - high.astype(F32)
    mid = rest.astype(BF16)
    low = (rest - mid.astype(F32)).astype(BF16)
    return high, mid, low


def stack3(x):
    return jnp.concatenate(split3(x), axis=0)


def inverse_factor(gram):
    n = gram.shape[0]
    row = lax.broadcasted_iota(jnp.int32, (n, n), 0)
    col = lax.broadcasted_iota(jnp.int32, (n, n), 1)
    eye = (row == col).astype(F32)
    both = jnp.concatenate([gram, eye, jnp.zeros((n, LANES - 2 * n), F32)], axis=1)
    full = (SUBLANES, LANES)
    parts = [both[q : q + SUBLANES] for q in range(0, n, SUBLANES)]
    sub = lax.broadcasted_iota(jnp.int32, full, 0)
    scales = [jnp.zeros(full, F32) for _ in parts]
    for j in range(0, n, STEP):
        home, at = j // SUBLANES, j % SUBLANES
        live = range(home, len(parts))
        cols = [
            {q: jnp.broadcast_to(parts[q][:, j + a : j + a + 1], full) for q in live}
            for a in range(STEP)
        ]
        rows = [jnp.broadcast_to(parts[home][at + a : at + a + 1], full) for a in range(STEP)]
        entry = {
            (a, b): jnp.broadcast_to(cols[b][home][at + a : at + a + 1], full)
            for a in range(STEP)
            for b in range(a + 1)
        }
        for a in range(STEP):
            over = 1.0 / entry[a, a]
            ratio = {c: entry[c, a] * over for c in range(a + 1, STEP)}
            for c in range(a + 1, STEP):
                for d in range(a + 1, c + 1):
                    entry[c, d] = entry[c, d] - ratio[c] * entry[d, a]
            for c in range(a + 1, STEP):
                rows[c] = rows[c] - ratio[c] * rows[a]
                for q in live:
                    cols[c][q] = cols[c][q] - ratio[c] * cols[a][q]
            root = 1.0 / jnp.sqrt(entry[a, a])
            scales[home] = jnp.where(sub == at + a, root, scales[home])
            for q in live:
                factor = cols[a][q] * over
                if q == home:
                    factor = jnp.where(sub > at + a, factor, 0.0)
                parts[q] = parts[q] - factor * rows[a]
    done = jnp.concatenate([p * s for p, s in zip(parts, scales)], axis=0)
    return done[:, n : 2 * n]


def apply_matrix(inverse):
    high, mid, low = (t.astype(F32) for t in split3(inverse))
    zero = jnp.zeros_like(high)
    full = jnp.concatenate(
        [
            jnp.concatenate([high, high, high], axis=1),
            jnp.concatenate([mid, mid, zero], axis=1),
            jnp.concatenate([low, zero, zero], axis=1),
        ],
        axis=0,
    )
    return full.astype(BF16)


def applied(matrix, stacked):
    n = matrix.shape[0] // 3
    terms = jnp.dot(matrix, stacked, preferred_element_type=F32)
    return terms[:n] + (terms[n : 2 * n] + terms[2 * n :])


def gram_of(parts, total_states):
    return paired_sum(parts) / total_states


def transposed_into(source, rows_ref):
    for g in range(rows_ref.shape[0] // LANES):
        pieces = [
            source[:, (PACK * g + b) * LANES : (PACK * g + b + 1) * LANES].astype(F32)
            for b in range(PACK)
        ]
        rows_ref[g * LANES : (g + 1) * LANES, :] = jnp.concatenate(pieces, axis=0).T


def gathered_into(unroll, row_ref, part_ref, rows_ref, picked, outs):
    count = picked.shape[0]
    columns = outs[0].shape[0]

    def pick(i, carry):
        for u in range(unroll):
            m = i * unroll + u
            picked[pl.ds(m, 1), :] = rows_ref[pl.ds(row_ref[m], 1), :]
        return carry

    lax.fori_loop(0, count // unroll, pick, 0)
    tiles_out = outs[0].shape[1] // LANES
    for g in range(count // LANES):
        y = picked[g * LANES : (g + 1) * LANES, :].T
        part = jnp.broadcast_to(part_ref[g : g + 1, :], (columns, LANES))
        value = y[:columns]
        for b in range(1, PACK):
            value = jnp.where(part == b, y[b * columns : (b + 1) * columns], value)
        out, t = outs[g // tiles_out], g % tiles_out
        out[:, t * LANES : (t + 1) * LANES] = value.astype(out.dtype)


def gather_kernel(row_ref, part_ref, rows_ref, *rest):
    gathered_into(64, row_ref, part_ref, rows_ref, rest[-1], rest[:-1])


def gather_colours(rows, row_list, part_list, count):
    indices = row_list.shape[0]
    columns = LANES // PACK
    return pl.pallas_call(
        gather_kernel,
        out_shape=[vmem_out((columns, indices // count), F32)] * count,
        in_specs=[SMEM, VMEM, VMEM],
        out_specs=[VMEM] * count,
        scratch_shapes=[pltpu.VMEM((indices, LANES), F32)],
        compiler_params=PARAMS,
        cost_estimate=pl.CostEstimate(flops=0, bytes_accessed=8 << 20, transcendentals=0),
        name="gather_rows",
    )(row_list, in_vmem(part_list), in_vmem(rows))


def start_kernel(count, first, make_rows, row_ref, part_ref, source_ref, tiles_ref, *refs):
    outs, kept_ref, refs = refs[:count], refs[count], refs[count + 1 :]
    picked, sems = refs[-2:]
    size = kept_ref.shape[0] // COPIES
    copies = [
        pltpu.make_async_copy(
            tiles_ref.at[pl.ds(first + c * size, size)],
            kept_ref.at[pl.ds(c * size, size)],
            sems.at[c],
        )
        for c in range(COPIES)
    ]
    for copy in copies:
        copy.start()
    rows_ref = source_ref
    if make_rows:
        rows_ref = refs[0]
        transposed_into(source_ref, rows_ref)
    gathered_into(64, row_ref, part_ref, rows_ref, picked, outs)
    for copy in copies:
        copy.wait()


def start_gather(source, row_list, part_list, count, tiles, first, kept, make_rows):
    indices = row_list.shape[0]
    columns = LANES // PACK
    outs = [vmem_out((columns, indices // count), BF16)] * count
    outs.append(vmem_out((kept, *tiles.shape[1:]), tiles.dtype))
    if make_rows:
        outs.append(vmem_out((source.shape[1] // PACK, LANES), F32))
    return pl.pallas_call(
        functools.partial(start_kernel, count, first, make_rows),
        out_shape=outs,
        in_specs=[SMEM, VMEM, VMEM, pl.BlockSpec(memory_space=pl.ANY)],
        out_specs=[VMEM] * len(outs),
        scratch_shapes=[pltpu.VMEM((indices, LANES), F32), pltpu.SemaphoreType.DMA((COPIES,))],
        compiler_params=PARAMS,
        name="start_gather",
    )(row_list, in_vmem(part_list), in_vmem(source), tiles)


def own_slots(block_ref, tiles_ref, own_ref):
    tile_size = tiles_ref.shape[1]
    for t in range(own_ref.shape[1] // tile_size):
        at = slice(t * tile_size, (t + 1) * tile_size)
        own_ref[:, at] = jnp.dot(block_ref[:, at], tiles_ref[t], preferred_element_type=F32)


def first_own_kernel(block_ref, tiles_ref, own_ref):
    own_slots(block_ref, tiles_ref, own_ref)


def first_own(block, tiles):
    return pl.pallas_call(
        first_own_kernel,
        out_shape=vmem_out(block.shape, F32),
        in_specs=[VMEM] * 2,
        out_specs=VMEM,
        compiler_params=PARAMS,
        name="first_own",
    )(in_vmem(block), in_vmem(tiles))


def later_own_kernel(total_states, *refs):
    grams, stacked, tiles_ref = refs[:4], refs[4], refs[5]
    block_ref, matrix_ref, own_ref = refs[6:]
    matrix = apply_matrix(inverse_factor(gram_of([r[...] for r in grams], total_states)))
    matrix_ref[...] = matrix
    for c in range(0, block_ref.shape[1], CHUNK):
        block_ref[:, c : c + CHUNK] = applied(matrix, stacked[:, c : c + CHUNK]).astype(BF16)
    own_slots(block_ref, tiles_ref, own_ref)


def later_own(grams, stacked, tiles, total_states):
    columns, states = stacked.shape[0] // 3, stacked.shape[1]
    return pl.pallas_call(
        functools.partial(later_own_kernel, total_states),
        out_shape=[
            vmem_out((columns, states), BF16),
            vmem_out((3 * columns, 3 * columns), BF16),
            vmem_out((columns, states), F32),
        ],
        in_specs=[VMEM] * 6,
        out_specs=[VMEM] * 3,
        compiler_params=PARAMS,
        name="later_own",
    )(*[in_vmem(g) for g in grams], in_vmem(stacked), in_vmem(tiles))


def product_kernel(colours, group, with_rows, *refs):
    src_ref, dst_ref, count_ref, block_ref, own_ref = refs[:5]
    ghosts, refs = refs[5 : 5 + colours], refs[5 + colours :]
    matrix_ref = None
    if ghosts[0].dtype == F32:
        matrix_ref, refs = refs[0], refs[1:]
    tiles_ref, refs = refs[0], refs[1:]
    stacked_ref, gram_ref, refs = refs[0], refs[1], refs[2:]
    if with_rows:
        rows_ref, refs = refs[0], refs[1:]
    source, total = refs
    columns, states = block_ref.shape
    tile_size = tiles_ref.shape[1]
    first = states // tile_size
    live = count_ref[0]

    source[:, :states] = block_ref[...]
    at = states
    for ghost in ghosts:
        width = ghost.shape[1]
        value = ghost[...]
        if matrix_ref is not None:
            value = applied(matrix_ref[...], stack3(value)).astype(BF16)
        source[:, at : at + width] = value
        at += width
    source[:, at:] = jnp.zeros((columns, tile_size), BF16)
    nothing = at // tile_size
    total[...] = own_ref[...]

    def tile_at(s):
        index = jnp.where(s < live, src_ref[s], nothing)
        return source[:, pl.ds(pl.multiple_of(index * tile_size, tile_size), tile_size)]

    zero = jnp.zeros((columns, tile_size), BF16)

    def body(i, carry):
        base = first + i * group
        terms = []
        for u in range(0, group, 2):
            pair = jnp.concatenate(
                [
                    jnp.concatenate([tile_at(base + u), zero], axis=1),
                    jnp.concatenate([zero, tile_at(base + u + 1)], axis=1),
                ],
                axis=0,
            )
            weights = tiles_ref[pl.ds(base + u - first, 2)].reshape(2 * tile_size, tile_size)
            both = jnp.dot(pair, weights, preferred_element_type=F32)
            terms += [both[:columns], both[columns:]]
        for u in range(group):
            where = pl.multiple_of(dst_ref[base + u] * tile_size, tile_size)
            total[:, pl.ds(where, tile_size)] += terms[u]
        return carry

    lax.fori_loop(0, (live - first + group - 1) // group, body, 0)

    gram = jnp.zeros((3 * columns, 3 * columns), F32)
    for c in range(0, states, CHUNK):
        part = stack3(total[:, c : c + CHUNK])
        stacked_ref[:, c : c + CHUNK] = part
        gram += lax.dot_general(part, part, (((1,), (1,)), ((), ())), preferred_element_type=F32)
    blocks = [
        gram[a * columns : (a + 1) * columns, b * columns : (b + 1) * columns]
        for a in range(3)
        for b in range(3)
    ]
    small = blocks[8] + (blocks[5] + blocks[7])
    middle = blocks[4] + (blocks[2] + blocks[6])
    gram_ref[...] = blocks[0] + ((blocks[1] + blocks[3]) + (middle + small))
    if with_rows:
        transposed_into(total, rows_ref)


def product(src, dst, count, block, own, ghosts, matrix, tiles, with_rows):
    columns, states = block.shape
    rest, tile_size, _ = tiles.shape
    group = 64
    while rest % group:
        group //= 2
    outs = [vmem_out((3 * columns, states), BF16), vmem_out((columns, columns), F32)]
    if with_rows:
        outs.append(vmem_out((states // PACK, LANES), F32))
    operands = [block, own, *ghosts] + ([] if matrix is None else [matrix]) + [tiles]
    width = states + sum(g.shape[1] for g in ghosts) + tile_size
    return pl.pallas_call(
        functools.partial(product_kernel, len(ghosts), group, with_rows),
        out_shape=outs,
        in_specs=[SMEM] * 3 + [VMEM] * len(operands),
        out_specs=[VMEM] * len(outs),
        scratch_shapes=[pltpu.VMEM((columns, width), BF16), pltpu.VMEM((columns, states), F32)],
        compiler_params=PARAMS,
        name="product",
    )(src, dst, count, *[in_vmem(x) for x in operands])


def final_kernel(total_states, *refs):
    grams, stacked, out_ref = refs[:4], refs[4], refs[5]
    matrix = apply_matrix(inverse_factor(gram_of([r[...] for r in grams], total_states)))
    for c in range(0, out_ref.shape[1], CHUNK):
        out_ref[:, c : c + CHUNK] = applied(matrix, stacked[:, c : c + CHUNK])


def final(grams, stacked, total_states):
    columns, states = stacked.shape[0] // 3, stacked.shape[1]
    return pl.pallas_call(
        functools.partial(final_kernel, total_states),
        out_shape=jax.ShapeDtypeStruct((columns, states), F32),
        in_specs=[VMEM] * 5,
        out_specs=VMEM,
        compiler_params=PARAMS,
        name="final",
    )(*[in_vmem(g) for g in grams], in_vmem(stacked))


def dom_rounds(size):
    rounds, step = [], 1
    while step < size:
        span = min(4, size // step)
        rounds.append([step * k for k in range(1, span)])
        step *= span
    return rounds[::-1]


def paired_sum(parts):
    return (parts[0] + parts[1]) + (parts[2] + parts[3])


def gram_round(gram, masks):
    parts = [gram] + [swapped(gram, mask) for mask in masks]
    return parts + [jnp.zeros_like(gram)] * (4 - len(parts))


def on_device(start_block, tiles, tile_src, tile_dst, slot_count, send_rows):
    size = lax.axis_size("dom")
    masks = [1, 2, 4, 1 << (size.bit_length() - 2)]
    columns, states = start_block.shape
    total_states = states * size
    rounds = dom_rounds(size)
    lists = send_rows[0]
    pack_states = PACK * LANES
    row_lists = lists // pack_states * LANES + lists % LANES
    part_lists = lists // LANES % PACK
    far = (3, 2)
    near = (1, 0)

    def lists_of(colours):
        rows = jnp.concatenate([row_lists[c] for c in colours])
        parts = jnp.concatenate([part_lists[c] for c in colours]).reshape(-1, LANES)
        return rows, parts

    listed = [lists_of(far), lists_of(near)]

    def sent(ghosts, colours, picked):
        for colour, x in zip(colours, picked):
            ghosts[colour] = swapped(x, masks[colour])

    own_count = states // tiles.shape[1]
    ghosts = [None] * len(masks)
    *picked, rest_tiles, start_rows = start_gather(
        start_block, *listed[0], len(far), tiles, own_count, tiles.shape[0] - own_count, True
    )
    sent(ghosts, far, picked)
    *picked, own_tiles = start_gather(
        start_rows, *listed[1], len(near), tiles, 0, own_count, False
    )
    sent(ghosts, near, picked)
    block, matrix = start_block, None
    own = first_own(start_block, own_tiles)
    for turn in range(ITERS):
        last = turn == ITERS - 1
        stacked, gram, *rows = product(
            tile_src, tile_dst, slot_count, block, own, ghosts, matrix, rest_tiles, not last
        )
        for masks_now in rounds[:-1]:
            gram = paired_sum(gram_round(gram, masks_now))
        if last:
            return final(gram_round(gram, rounds[-1]), stacked, total_states)
        ghosts = [None] * len(masks)
        picked = gather_colours(rows[0], *listed[0], len(far))
        gram, near_rows, *picked = lax.optimization_barrier((gram, rows[0], *picked))
        parts = gram_round(gram, rounds[-1])
        sent(ghosts, far, picked)
        picked = gather_colours(near_rows, *listed[1], len(near))
        gathered = lax.optimization_barrier((*parts, *picked))
        parts, picked = gathered[: len(parts)], gathered[len(parts) :]
        sent(ghosts, near, picked)
        block, matrix, own = later_own(parts, stacked, own_tiles, total_states)


def solution(mesh):
    return jax.shard_map(
        on_device,
        mesh=mesh,
        in_specs=(
            P(None, ("groups", "dom")),
            P(("groups", "dom"), None, None),
            P(("groups", "dom")),
            P(("groups", "dom")),
            P(("groups", "dom")),
            P(("groups", "dom"), None, None),
        ),
        out_specs=P(None, ("groups", "dom")),
        check_vma=False,
    )
```

```python
import functools

import jax
import jax.numpy as jnp
from jax import lax
from jax.experimental import pallas as pl
from jax.experimental.pallas import tpu as pltpu
from jax.sharding import PartitionSpec as P

ITERS = 3
LANES = 128
PACK = 4
CHUNK = 1024
SUBLANES = 8
STEP = 4
COPIES = 8
F32 = jnp.float32
BF16 = jnp.bfloat16
VMEM = pl.BlockSpec(memory_space=pltpu.VMEM)
SMEM = pl.BlockSpec(memory_space=pltpu.SMEM)
CHEAP = pl.CostEstimate(flops=0, bytes_accessed=1024, transcendentals=0)
PARAMS = pltpu.CompilerParams(vmem_limit_bytes=32 << 20)


def in_vmem(x):
    return pltpu.with_memory_space_constraint(x, pltpu.VMEM)


def in_hbm(x):
    return pltpu.with_memory_space_constraint(x, pltpu.HBM)


def vmem_out(shape, dtype):
    return pltpu.VMEM(shape, dtype)


def swapped(x, mask):
    size = lax.axis_size("dom")
    return lax.ppermute(x, "dom", [(i, i ^ mask) for i in range(size)])


def split3(x):
    high = x.astype(BF16)
    rest = x - high.astype(F32)
    mid = rest.astype(BF16)
    low = (rest - mid.astype(F32)).astype(BF16)
    return high, mid, low


def stack3(x):
    return jnp.concatenate(split3(x), axis=0)


def inverse_factor(gram):
    n = gram.shape[0]
    row = lax.broadcasted_iota(jnp.int32, (n, n), 0)
    col = lax.broadcasted_iota(jnp.int32, (n, n), 1)
    eye = (row == col).astype(F32)
    both = jnp.concatenate([gram, eye, jnp.zeros((n, LANES - 2 * n), F32)], axis=1)
    full = (SUBLANES, LANES)
    parts = [both[q : q + SUBLANES] for q in range(0, n, SUBLANES)]
    sub = lax.broadcasted_iota(jnp.int32, full, 0)
    scales = [jnp.zeros(full, F32) for _ in parts]
    for j in range(0, n, STEP):
        home, at = j // SUBLANES, j % SUBLANES
        live = range(home, len(parts))
        cols = [
            {q: jnp.broadcast_to(parts[q][:, j + a : j + a + 1], full) for q in live}
            for a in range(STEP)
        ]
        rows = [jnp.broadcast_to(parts[home][at + a : at + a + 1], full) for a in range(STEP)]
        entry = {
            (a, b): jnp.broadcast_to(cols[b][home][at + a : at + a + 1], full)
            for a in range(STEP)
            for b in range(a + 1)
        }
        for a in range(STEP):
            over = 1.0 / entry[a, a]
            ratio = {c: entry[c, a] * over for c in range(a + 1, STEP)}
            for c in range(a + 1, STEP):
                for d in range(a + 1, c + 1):
                    entry[c, d] = entry[c, d] - ratio[c] * entry[d, a]
            for c in range(a + 1, STEP):
                rows[c] = rows[c] - ratio[c] * rows[a]
                for q in live:
                    cols[c][q] = cols[c][q] - ratio[c] * cols[a][q]
            root = 1.0 / jnp.sqrt(entry[a, a])
            scales[home] = jnp.where(sub == at + a, root, scales[home])
            for q in live:
                factor = cols[a][q] * over
                if q == home:
                    factor = jnp.where(sub > at + a, factor, 0.0)
                parts[q] = parts[q] - factor * rows[a]
    done = jnp.concatenate([p * s for p, s in zip(parts, scales)], axis=0)
    return done[:, n : 2 * n]


def apply_matrix(inverse):
    high, mid, low = (t.astype(F32) for t in split3(inverse))
    zero = jnp.zeros_like(high)
    full = jnp.concatenate(
        [
            jnp.concatenate([high, high, high], axis=1),
            jnp.concatenate([mid, mid, zero], axis=1),
            jnp.concatenate([low, zero, zero], axis=1),
        ],
        axis=0,
    )
    return full.astype(BF16)


def applied(matrix, stacked):
    n = matrix.shape[0] // 3
    terms = jnp.dot(matrix, stacked, preferred_element_type=F32)
    return terms[:n] + (terms[n : 2 * n] + terms[2 * n :])


def gram_of(parts, total_states):
    return paired_sum(parts) / total_states


def transposed_into(source, rows_ref):
    for g in range(rows_ref.shape[0] // LANES):
        pieces = [
            source[:, (PACK * g + b) * LANES : (PACK * g + b + 1) * LANES].astype(F32)
            for b in range(PACK)
        ]
        rows_ref[g * LANES : (g + 1) * LANES, :] = jnp.concatenate(pieces, axis=0).T


def gathered_into(unroll, row_ref, part_ref, rows_ref, picked, outs):
    count = picked.shape[0]
    columns = outs[0].shape[0]

    def pick(i, carry):
        for u in range(unroll):
            m = i * unroll + u
            picked[pl.ds(m, 1), :] = rows_ref[pl.ds(row_ref[m], 1), :]
        return carry

    lax.fori_loop(0, count // unroll, pick, 0)
    tiles_out = outs[0].shape[1] // LANES
    for g in range(count // LANES):
        y = picked[g * LANES : (g + 1) * LANES, :].T
        part = jnp.broadcast_to(part_ref[g : g + 1, :], (columns, LANES))
        value = y[:columns]
        for b in range(1, PACK):
            value = jnp.where(part == b, y[b * columns : (b + 1) * columns], value)
        out, t = outs[g // tiles_out], g % tiles_out
        out[:, t * LANES : (t + 1) * LANES] = value.astype(out.dtype)


def gather_kernel(row_ref, part_ref, rows_ref, *rest):
    gathered_into(64, row_ref, part_ref, rows_ref, rest[-1], rest[:-1])


def gather_colours(rows, row_list, part_list, count):
    indices = row_list.shape[0]
    columns = LANES // PACK
    return pl.pallas_call(
        gather_kernel,
        out_shape=[vmem_out((columns, indices // count), F32)] * count,
        in_specs=[SMEM, VMEM, VMEM],
        out_specs=[VMEM] * count,
        scratch_shapes=[pltpu.VMEM((indices, LANES), F32)],
        compiler_params=PARAMS,
        cost_estimate=CHEAP,
        name="gather_rows",
    )(row_list, in_vmem(part_list), in_vmem(rows))


def start_kernel(count, first, make_rows, row_ref, part_ref, source_ref, tiles_ref, *refs):
    outs, kept_ref, refs = refs[:count], refs[count], refs[count + 1 :]
    picked, sems = refs[-2:]
    size = kept_ref.shape[0] // COPIES
    copies = [
        pltpu.make_async_copy(
            tiles_ref.at[pl.ds(first + c * size, size)],
            kept_ref.at[pl.ds(c * size, size)],
            sems.at[c],
        )
        for c in range(COPIES)
    ]
    for copy in copies:
        copy.start()
    rows_ref = source_ref
    if make_rows:
        rows_ref = refs[0]
        transposed_into(source_ref, rows_ref)
    gathered_into(64, row_ref, part_ref, rows_ref, picked, outs)
    for copy in copies:
        copy.wait()


def start_gather(source, row_list, part_list, count, tiles, first, kept, make_rows):
    indices = row_list.shape[0]
    columns = LANES // PACK
    outs = [vmem_out((columns, indices // count), BF16)] * count
    outs.append(vmem_out((kept, *tiles.shape[1:]), tiles.dtype))
    if make_rows:
        outs.append(vmem_out((source.shape[1] // PACK, LANES), F32))
    return pl.pallas_call(
        functools.partial(start_kernel, count, first, make_rows),
        out_shape=outs,
        in_specs=[SMEM, VMEM, VMEM, pl.BlockSpec(memory_space=pltpu.HBM)],
        out_specs=[VMEM] * len(outs),
        scratch_shapes=[pltpu.VMEM((indices, LANES), F32), pltpu.SemaphoreType.DMA((COPIES,))],
        compiler_params=PARAMS,
        cost_estimate=CHEAP,
        name="start_gather",
    )(row_list, in_vmem(part_list), source if make_rows else in_vmem(source), in_hbm(tiles))


def own_slots(block_ref, tiles_ref, own_ref):
    tile_size = tiles_ref.shape[1]
    for t in range(own_ref.shape[1] // tile_size):
        at = slice(t * tile_size, (t + 1) * tile_size)
        own_ref[:, at] = jnp.dot(block_ref[:, at], tiles_ref[t], preferred_element_type=F32)


def first_own_kernel(block_ref, tiles_ref, own_ref):
    own_slots(block_ref, tiles_ref, own_ref)


def first_own(block, tiles):
    return pl.pallas_call(
        first_own_kernel,
        out_shape=vmem_out(block.shape, F32),
        in_specs=[VMEM] * 2,
        out_specs=VMEM,
        compiler_params=PARAMS,
        cost_estimate=CHEAP,
        name="first_own",
    )(in_vmem(block), in_vmem(tiles))


def later_own_kernel(total_states, *refs):
    grams, stacked, tiles_ref = refs[:4], refs[4], refs[5]
    block_ref, matrix_ref, own_ref = refs[6:]
    matrix = apply_matrix(inverse_factor(gram_of([r[...] for r in grams], total_states)))
    matrix_ref[...] = matrix
    for c in range(0, block_ref.shape[1], CHUNK):
        block_ref[:, c : c + CHUNK] = applied(matrix, stacked[:, c : c + CHUNK]).astype(BF16)
    own_slots(block_ref, tiles_ref, own_ref)


def later_own(grams, stacked, tiles, total_states):
    columns, states = stacked.shape[0] // 3, stacked.shape[1]
    return pl.pallas_call(
        functools.partial(later_own_kernel, total_states),
        out_shape=[
            vmem_out((columns, states), BF16),
            vmem_out((3 * columns, 3 * columns), BF16),
            vmem_out((columns, states), F32),
        ],
        in_specs=[VMEM] * 6,
        out_specs=[VMEM] * 3,
        compiler_params=PARAMS,
        cost_estimate=CHEAP,
        name="later_own",
    )(*[in_vmem(g) for g in grams], in_vmem(stacked), in_vmem(tiles))


def product_kernel(colours, group, with_rows, *refs):
    src_ref, dst_ref, count_ref, block_ref, own_ref = refs[:5]
    ghosts, refs = refs[5 : 5 + colours], refs[5 + colours :]
    matrix_ref = None
    if ghosts[0].dtype == F32:
        matrix_ref, refs = refs[0], refs[1:]
    tiles_ref, refs = refs[0], refs[1:]
    stacked_ref, gram_ref, refs = refs[0], refs[1], refs[2:]
    if with_rows:
        rows_ref, refs = refs[0], refs[1:]
    source, total = refs
    columns, states = block_ref.shape
    tile_size = tiles_ref.shape[1]
    first = states // tile_size
    live = count_ref[0]

    source[:, :states] = block_ref[...]
    at = states
    for ghost in ghosts:
        width = ghost.shape[1]
        value = ghost[...]
        if matrix_ref is not None:
            value = applied(matrix_ref[...], stack3(value)).astype(BF16)
        source[:, at : at + width] = value
        at += width
    source[:, at:] = jnp.zeros((columns, tile_size), BF16)
    nothing = at // tile_size
    total[...] = own_ref[...]

    def tile_at(s):
        index = jnp.where(s < live, src_ref[s], nothing)
        return source[:, pl.ds(pl.multiple_of(index * tile_size, tile_size), tile_size)]

    zero = jnp.zeros((columns, tile_size), BF16)

    def body(i, carry):
        base = first + i * group
        terms = []
        for u in range(0, group, 2):
            pair = jnp.concatenate(
                [
                    jnp.concatenate([tile_at(base + u), zero], axis=1),
                    jnp.concatenate([zero, tile_at(base + u + 1)], axis=1),
                ],
                axis=0,
            )
            weights = tiles_ref[pl.ds(base + u - first, 2)].reshape(2 * tile_size, tile_size)
            both = jnp.dot(pair, weights, preferred_element_type=F32)
            terms += [both[:columns], both[columns:]]
        for u in range(group):
            where = pl.multiple_of(dst_ref[base + u] * tile_size, tile_size)
            total[:, pl.ds(where, tile_size)] += terms[u]
        return carry

    lax.fori_loop(0, (live - first + group - 1) // group, body, 0)

    gram = jnp.zeros((3 * columns, 3 * columns), F32)
    for c in range(0, states, CHUNK):
        part = stack3(total[:, c : c + CHUNK])
        stacked_ref[:, c : c + CHUNK] = part
        gram += lax.dot_general(part, part, (((1,), (1,)), ((), ())), preferred_element_type=F32)
    blocks = [
        gram[a * columns : (a + 1) * columns, b * columns : (b + 1) * columns]
        for a in range(3)
        for b in range(3)
    ]
    small = blocks[8] + (blocks[5] + blocks[7])
    middle = blocks[4] + (blocks[2] + blocks[6])
    gram_ref[...] = blocks[0] + ((blocks[1] + blocks[3]) + (middle + small))
    if with_rows:
        transposed_into(total, rows_ref)


def product(src, dst, count, block, own, ghosts, matrix, tiles, with_rows):
    columns, states = block.shape
    rest, tile_size, _ = tiles.shape
    group = 64
    while rest % group:
        group //= 2
    outs = [vmem_out((3 * columns, states), BF16), vmem_out((columns, columns), F32)]
    if with_rows:
        outs.append(vmem_out((states // PACK, LANES), F32))
    operands = [block, own, *ghosts] + ([] if matrix is None else [matrix]) + [tiles]
    width = states + sum(g.shape[1] for g in ghosts) + tile_size
    return pl.pallas_call(
        functools.partial(product_kernel, len(ghosts), group, with_rows),
        out_shape=outs,
        in_specs=[SMEM] * 3 + [VMEM] * len(operands),
        out_specs=[VMEM] * len(outs),
        scratch_shapes=[pltpu.VMEM((columns, width), BF16), pltpu.VMEM((columns, states), F32)],
        compiler_params=PARAMS,
        cost_estimate=CHEAP,
        name="product",
    )(src, dst, count, *[in_vmem(x) for x in operands])


def final_kernel(total_states, *refs):
    grams, stacked, out_ref = refs[:4], refs[4], refs[5]
    matrix = apply_matrix(inverse_factor(gram_of([r[...] for r in grams], total_states)))
    for c in range(0, out_ref.shape[1], CHUNK):
        out_ref[:, c : c + CHUNK] = applied(matrix, stacked[:, c : c + CHUNK])


def final(grams, stacked, total_states):
    columns, states = stacked.shape[0] // 3, stacked.shape[1]
    return pl.pallas_call(
        functools.partial(final_kernel, total_states),
        out_shape=jax.ShapeDtypeStruct((columns, states), F32),
        in_specs=[VMEM] * 5,
        out_specs=VMEM,
        compiler_params=PARAMS,
        cost_estimate=CHEAP,
        name="final",
    )(*[in_vmem(g) for g in grams], in_vmem(stacked))


def dom_rounds(size):
    rounds, step = [], 1
    while step < size:
        span = min(4, size // step)
        rounds.append([step * k for k in range(1, span)])
        step *= span
    return rounds[::-1]


def paired_sum(parts):
    return (parts[0] + parts[1]) + (parts[2] + parts[3])


def gram_round(gram, masks):
    parts = [gram] + [swapped(gram, mask) for mask in masks]
    return parts + [jnp.zeros_like(gram)] * (4 - len(parts))


def on_device(start_block, tiles, tile_src, tile_dst, slot_count, send_rows):
    size = lax.axis_size("dom")
    masks = [1, 2, 4, 1 << (size.bit_length() - 2)]
    columns, states = start_block.shape
    total_states = states * size
    rounds = dom_rounds(size)
    lists = send_rows[0]
    pack_states = PACK * LANES
    row_lists = lists // pack_states * LANES + lists % LANES
    part_lists = lists // LANES % PACK
    far = (3, 2)
    near = (1, 0)

    def lists_of(colours):
        rows = jnp.concatenate([row_lists[c] for c in colours])
        parts = jnp.concatenate([part_lists[c] for c in colours]).reshape(-1, LANES)
        return rows, parts

    listed = [lists_of(far), lists_of(near)]

    def sent(ghosts, colours, picked):
        for colour, x in zip(colours, picked):
            ghosts[colour] = swapped(x, masks[colour])

    own_count = states // tiles.shape[1]
    ghosts = [None] * len(masks)
    *picked, rest_tiles, start_rows = start_gather(
        start_block, *listed[0], len(far), tiles, own_count, tiles.shape[0] - own_count, True
    )
    sent(ghosts, far, picked)
    *picked, own_tiles = start_gather(
        start_rows, *listed[1], len(near), tiles, 0, own_count, False
    )
    sent(ghosts, near, picked)
    block, matrix = start_block, None
    own = first_own(start_block, own_tiles)
    for turn in range(ITERS):
        last = turn == ITERS - 1
        stacked, gram, *rows = product(
            tile_src, tile_dst, slot_count, block, own, ghosts, matrix, rest_tiles, not last
        )
        for masks_now in rounds[:-1]:
            gram = paired_sum(gram_round(gram, masks_now))
        if last:
            return final(gram_round(gram, rounds[-1]), stacked, total_states)
        ghosts = [None] * len(masks)
        picked = gather_colours(rows[0], *listed[0], len(far))
        gram, *picked = lax.optimization_barrier((gram, *picked))
        parts = gram_round(gram, rounds[-1])
        sent(ghosts, far, picked)
        near_rows, *parts = lax.optimization_barrier((rows[0], *parts))
        sent(ghosts, near, gather_colours(near_rows, *listed[1], len(near)))
        block, matrix, own = later_own(parts, stacked, own_tiles, total_states)


def solution(mesh):
    return jax.shard_map(
        on_device,
        mesh=mesh,
        in_specs=(
            P(None, ("groups", "dom")),
            P(("groups", "dom"), None, None),
            P(("groups", "dom")),
            P(("groups", "dom")),
            P(("groups", "dom")),
            P(("groups", "dom"), None, None),
        ),
        out_specs=P(None, ("groups", "dom")),
        check_vma=False,
    )
```

```python
import functools

import jax
import jax.numpy as jnp
from jax import lax
from jax.experimental import pallas as pl
from jax.experimental.pallas import tpu as pltpu
from jax.sharding import PartitionSpec as P

ITERS = 3
LANES = 128
PACK = 4
CHUNK = 1024
SUBLANES = 8
STEP = 4
COPIES = 8
F32 = jnp.float32
BF16 = jnp.bfloat16
VMEM = pl.BlockSpec(memory_space=pltpu.VMEM)
SMEM = pl.BlockSpec(memory_space=pltpu.SMEM)
CHEAP = pl.CostEstimate(flops=0, bytes_accessed=1024, transcendentals=0)
PARAMS = pltpu.CompilerParams(vmem_limit_bytes=32 << 20)


def in_vmem(x):
    return pltpu.with_memory_space_constraint(x, pltpu.VMEM)


def in_hbm(x):
    return pltpu.with_memory_space_constraint(x, pltpu.HBM)


def vmem_out(shape, dtype):
    return pltpu.VMEM(shape, dtype)


def swapped(x, mask):
    size = lax.axis_size("dom")
    return lax.ppermute(x, "dom", [(i, i ^ mask) for i in range(size)])


def split3(x):
    high = x.astype(BF16)
    rest = x - high.astype(F32)
    mid = rest.astype(BF16)
    low = (rest - mid.astype(F32)).astype(BF16)
    return high, mid, low


def stack3(x):
    return jnp.concatenate(split3(x), axis=0)


def inverse_factor(gram):
    n = gram.shape[0]
    row = lax.broadcasted_iota(jnp.int32, (n, n), 0)
    col = lax.broadcasted_iota(jnp.int32, (n, n), 1)
    eye = (row == col).astype(F32)
    both = jnp.concatenate([gram, eye, jnp.zeros((n, LANES - 2 * n), F32)], axis=1)
    full = (SUBLANES, LANES)
    parts = [both[q : q + SUBLANES] for q in range(0, n, SUBLANES)]
    sub = lax.broadcasted_iota(jnp.int32, full, 0)
    scales = [jnp.zeros(full, F32) for _ in parts]
    for j in range(0, n, STEP):
        home, at = j // SUBLANES, j % SUBLANES
        live = range(home, len(parts))
        cols = [
            {q: jnp.broadcast_to(parts[q][:, j + a : j + a + 1], full) for q in live}
            for a in range(STEP)
        ]
        rows = [jnp.broadcast_to(parts[home][at + a : at + a + 1], full) for a in range(STEP)]
        entry = {
            (a, b): jnp.broadcast_to(cols[b][home][at + a : at + a + 1], full)
            for a in range(STEP)
            for b in range(a + 1)
        }
        for a in range(STEP):
            over = 1.0 / entry[a, a]
            ratio = {c: entry[c, a] * over for c in range(a + 1, STEP)}
            for c in range(a + 1, STEP):
                for d in range(a + 1, c + 1):
                    entry[c, d] = entry[c, d] - ratio[c] * entry[d, a]
            for c in range(a + 1, STEP):
                rows[c] = rows[c] - ratio[c] * rows[a]
                for q in live:
                    cols[c][q] = cols[c][q] - ratio[c] * cols[a][q]
            root = 1.0 / jnp.sqrt(entry[a, a])
            scales[home] = jnp.where(sub == at + a, root, scales[home])
            for q in live:
                factor = cols[a][q] * over
                if q == home:
                    factor = jnp.where(sub > at + a, factor, 0.0)
                parts[q] = parts[q] - factor * rows[a]
    done = jnp.concatenate([p * s for p, s in zip(parts, scales)], axis=0)
    return done[:, n : 2 * n]


def apply_matrix(inverse):
    high, mid, low = (t.astype(F32) for t in split3(inverse))
    zero = jnp.zeros_like(high)
    full = jnp.concatenate(
        [
            jnp.concatenate([high, high, high], axis=1),
            jnp.concatenate([mid, mid, zero], axis=1),
            jnp.concatenate([low, zero, zero], axis=1),
        ],
        axis=0,
    )
    return full.astype(BF16)


def applied(matrix, stacked):
    n = matrix.shape[0] // 3
    terms = jnp.dot(matrix, stacked, preferred_element_type=F32)
    return terms[:n] + (terms[n : 2 * n] + terms[2 * n :])


def gram_of(parts, total_states):
    return paired_sum(parts) / total_states


def transposed_into(source, rows_ref):
    for g in range(rows_ref.shape[0] // LANES):
        pieces = [
            source[:, (PACK * g + b) * LANES : (PACK * g + b + 1) * LANES].astype(F32)
            for b in range(PACK)
        ]
        rows_ref[g * LANES : (g + 1) * LANES, :] = jnp.concatenate(pieces, axis=0).T


def gathered_into(unroll, row_ref, part_ref, rows_ref, picked, outs):
    count = picked.shape[0]
    columns = outs[0].shape[0]

    def pick(i, carry):
        for u in range(unroll):
            m = i * unroll + u
            picked[pl.ds(m, 1), :] = rows_ref[pl.ds(row_ref[m], 1), :]
        return carry

    lax.fori_loop(0, count // unroll, pick, 0)
    tiles_out = outs[0].shape[1] // LANES
    for g in range(count // LANES):
        y = picked[g * LANES : (g + 1) * LANES, :].T
        part = jnp.broadcast_to(part_ref[g : g + 1, :], (columns, LANES))
        value = y[:columns]
        for b in range(1, PACK):
            value = jnp.where(part == b, y[b * columns : (b + 1) * columns], value)
        out, t = outs[g // tiles_out], g % tiles_out
        out[:, t * LANES : (t + 1) * LANES] = value.astype(out.dtype)


def gather_kernel(row_ref, part_ref, rows_ref, *rest):
    gathered_into(64, row_ref, part_ref, rows_ref, rest[-1], rest[:-1])


def gather_colours(rows, row_list, part_list, count):
    indices = row_list.shape[0]
    columns = LANES // PACK
    return pl.pallas_call(
        gather_kernel,
        out_shape=[vmem_out((columns, indices // count), F32)] * count,
        in_specs=[SMEM, VMEM, VMEM],
        out_specs=[VMEM] * count,
        scratch_shapes=[pltpu.VMEM((indices, LANES), F32)],
        compiler_params=PARAMS,
        cost_estimate=CHEAP,
        name="gather_rows",
    )(row_list, in_vmem(part_list), in_vmem(rows))


def start_kernel(count, first, make_rows, row_ref, part_ref, source_ref, tiles_ref, *refs):
    outs, kept_ref, refs = refs[:count], refs[count], refs[count + 1 :]
    picked, sems = refs[-2:]
    size = kept_ref.shape[0] // COPIES
    copies = [
        pltpu.make_async_copy(
            tiles_ref.at[pl.ds(first + c * size, size)],
            kept_ref.at[pl.ds(c * size, size)],
            sems.at[c],
        )
        for c in range(COPIES)
    ]
    for copy in copies:
        copy.start()
    rows_ref = source_ref
    if make_rows:
        rows_ref = refs[0]
        transposed_into(source_ref, rows_ref)
    gathered_into(64, row_ref, part_ref, rows_ref, picked, outs)
    for copy in copies:
        copy.wait()


def start_gather(source, row_list, part_list, count, tiles, first, kept, make_rows):
    indices = row_list.shape[0]
    columns = LANES // PACK
    outs = [vmem_out((columns, indices // count), BF16)] * count
    outs.append(vmem_out((kept, *tiles.shape[1:]), tiles.dtype))
    if make_rows:
        outs.append(vmem_out((source.shape[1] // PACK, LANES), F32))
    return pl.pallas_call(
        functools.partial(start_kernel, count, first, make_rows),
        out_shape=outs,
        in_specs=[SMEM, VMEM, VMEM, pl.BlockSpec(memory_space=pltpu.HBM)],
        out_specs=[VMEM] * len(outs),
        scratch_shapes=[pltpu.VMEM((indices, LANES), F32), pltpu.SemaphoreType.DMA((COPIES,))],
        compiler_params=PARAMS,
        cost_estimate=CHEAP,
        name="start_gather",
    )(row_list, in_vmem(part_list), source if make_rows else in_vmem(source), in_hbm(tiles))


def own_slots(block_ref, tiles_ref, own_ref):
    tile_size = tiles_ref.shape[1]
    for t in range(own_ref.shape[1] // tile_size):
        at = slice(t * tile_size, (t + 1) * tile_size)
        own_ref[:, at] = jnp.dot(block_ref[:, at], tiles_ref[t], preferred_element_type=F32)


def first_own_kernel(block_ref, tiles_ref, own_ref):
    own_slots(block_ref, tiles_ref, own_ref)


def first_own(block, tiles):
    return pl.pallas_call(
        first_own_kernel,
        out_shape=vmem_out(block.shape, F32),
        in_specs=[VMEM] * 2,
        out_specs=VMEM,
        compiler_params=PARAMS,
        cost_estimate=CHEAP,
        name="first_own",
    )(in_vmem(block), in_vmem(tiles))


def later_own_kernel(total_states, *refs):
    grams, stacked, tiles_ref = refs[:4], refs[4], refs[5]
    block_ref, matrix_ref, own_ref = refs[6:]
    matrix = apply_matrix(inverse_factor(gram_of([r[...] for r in grams], total_states)))
    matrix_ref[...] = matrix
    for c in range(0, block_ref.shape[1], CHUNK):
        block_ref[:, c : c + CHUNK] = applied(matrix, stacked[:, c : c + CHUNK]).astype(BF16)
    own_slots(block_ref, tiles_ref, own_ref)


def later_own(grams, stacked, tiles, total_states):
    columns, states = stacked.shape[0] // 3, stacked.shape[1]
    return pl.pallas_call(
        functools.partial(later_own_kernel, total_states),
        out_shape=[
            vmem_out((columns, states), BF16),
            vmem_out((3 * columns, 3 * columns), BF16),
            vmem_out((columns, states), F32),
        ],
        in_specs=[VMEM] * 6,
        out_specs=[VMEM] * 3,
        compiler_params=PARAMS,
        cost_estimate=CHEAP,
        name="later_own",
    )(*[in_vmem(g) for g in grams], in_vmem(stacked), in_vmem(tiles))


def product_kernel(colours, group, with_rows, *refs):
    src_ref, dst_ref, count_ref, block_ref, own_ref = refs[:5]
    ghosts, refs = refs[5 : 5 + colours], refs[5 + colours :]
    matrix_ref = None
    if ghosts[0].dtype == F32:
        matrix_ref, refs = refs[0], refs[1:]
    tiles_ref, refs = refs[0], refs[1:]
    stacked_ref, gram_ref, refs = refs[0], refs[1], refs[2:]
    if with_rows:
        rows_ref, refs = refs[0], refs[1:]
    source, total = refs
    columns, states = block_ref.shape
    tile_size = tiles_ref.shape[1]
    first = states // tile_size
    live = count_ref[0]

    source[:, :states] = block_ref[...]
    at = states
    for ghost in ghosts:
        width = ghost.shape[1]
        value = ghost[...]
        if matrix_ref is not None:
            value = applied(matrix_ref[...], stack3(value)).astype(BF16)
        source[:, at : at + width] = value
        at += width
    source[:, at:] = jnp.zeros((columns, tile_size), BF16)
    nothing = at // tile_size
    total[...] = own_ref[...]

    def tile_at(s):
        index = jnp.where(s < live, src_ref[s], nothing)
        return source[:, pl.ds(pl.multiple_of(index * tile_size, tile_size), tile_size)]

    zero = jnp.zeros((columns, tile_size), BF16)

    def body(i, carry):
        base = first + i * group
        terms = []
        for u in range(0, group, 2):
            pair = jnp.concatenate(
                [
                    jnp.concatenate([tile_at(base + u), zero], axis=1),
                    jnp.concatenate([zero, tile_at(base + u + 1)], axis=1),
                ],
                axis=0,
            )
            weights = tiles_ref[pl.ds(base + u - first, 2)].reshape(2 * tile_size, tile_size)
            both = jnp.dot(pair, weights, preferred_element_type=F32)
            terms += [both[:columns], both[columns:]]
        for u in range(group):
            where = pl.multiple_of(dst_ref[base + u] * tile_size, tile_size)
            total[:, pl.ds(where, tile_size)] += terms[u]
        return carry

    lax.fori_loop(0, (live - first + group - 1) // group, body, 0)

    gram = jnp.zeros((3 * columns, 3 * columns), F32)
    for c in range(0, states, CHUNK):
        part = stack3(total[:, c : c + CHUNK])
        stacked_ref[:, c : c + CHUNK] = part
        gram += lax.dot_general(part, part, (((1,), (1,)), ((), ())), preferred_element_type=F32)
    blocks = [
        gram[a * columns : (a + 1) * columns, b * columns : (b + 1) * columns]
        for a in range(3)
        for b in range(3)
    ]
    small = blocks[8] + (blocks[5] + blocks[7])
    middle = blocks[4] + (blocks[2] + blocks[6])
    gram_ref[...] = blocks[0] + ((blocks[1] + blocks[3]) + (middle + small))
    if with_rows:
        transposed_into(total, rows_ref)


def product(src, dst, count, block, own, ghosts, matrix, tiles, with_rows):
    columns, states = block.shape
    rest, tile_size, _ = tiles.shape
    group = 64
    while rest % group:
        group //= 2
    outs = [vmem_out((3 * columns, states), BF16), vmem_out((columns, columns), F32)]
    if with_rows:
        outs.append(vmem_out((states // PACK, LANES), F32))
    operands = [block, own, *ghosts] + ([] if matrix is None else [matrix]) + [tiles]
    width = states + sum(g.shape[1] for g in ghosts) + tile_size
    return pl.pallas_call(
        functools.partial(product_kernel, len(ghosts), group, with_rows),
        out_shape=outs,
        in_specs=[SMEM] * 3 + [VMEM] * len(operands),
        out_specs=[VMEM] * len(outs),
        scratch_shapes=[pltpu.VMEM((columns, width), BF16), pltpu.VMEM((columns, states), F32)],
        compiler_params=PARAMS,
        cost_estimate=CHEAP,
        name="product",
    )(src, dst, count, *[in_vmem(x) for x in operands])


def final_kernel(total_states, *refs):
    grams, stacked, out_ref = refs[:4], refs[4], refs[5]
    matrix = apply_matrix(inverse_factor(gram_of([r[...] for r in grams], total_states)))
    for c in range(0, out_ref.shape[1], CHUNK):
        out_ref[:, c : c + CHUNK] = applied(matrix, stacked[:, c : c + CHUNK])


def final(grams, stacked, total_states):
    columns, states = stacked.shape[0] // 3, stacked.shape[1]
    return pl.pallas_call(
        functools.partial(final_kernel, total_states),
        out_shape=jax.ShapeDtypeStruct((columns, states), F32),
        in_specs=[VMEM] * 5,
        out_specs=VMEM,
        compiler_params=PARAMS,
        cost_estimate=CHEAP,
        name="final",
    )(*[in_vmem(g) for g in grams], in_vmem(stacked))


def dom_rounds(size):
    rounds, step = [], 1
    while step < size:
        span = min(4, size // step)
        rounds.append([step * k for k in range(1, span)])
        step *= span
    return rounds[::-1]


def paired_sum(parts):
    return (parts[0] + parts[1]) + (parts[2] + parts[3])


def gram_round(gram, masks):
    parts = [gram] + [swapped(gram, mask) for mask in masks]
    return parts + [jnp.zeros_like(gram)] * (4 - len(parts))


def on_device(start_block, tiles, tile_src, tile_dst, slot_count, send_rows):
    size = lax.axis_size("dom")
    masks = [1, 2, 4, 1 << (size.bit_length() - 2)]
    columns, states = start_block.shape
    total_states = states * size
    rounds = dom_rounds(size)
    lists = send_rows[0]
    pack_states = PACK * LANES
    row_lists = lists // pack_states * LANES + lists % LANES
    part_lists = lists // LANES % PACK
    far = (3, 0)
    near = (2, 1)

    def lists_of(colours):
        rows = jnp.concatenate([row_lists[c] for c in colours])
        parts = jnp.concatenate([part_lists[c] for c in colours]).reshape(-1, LANES)
        return rows, parts

    listed = [lists_of(far), lists_of(near)]

    def sent(ghosts, colours, picked):
        for colour, x in zip(colours, picked):
            ghosts[colour] = swapped(x, masks[colour])

    own_count = states // tiles.shape[1]
    ghosts = [None] * len(masks)
    *picked, rest_tiles, start_rows = start_gather(
        start_block, *listed[0], len(far), tiles, own_count, tiles.shape[0] - own_count, True
    )
    sent(ghosts, far, picked)
    *picked, own_tiles = start_gather(
        start_rows, *listed[1], len(near), tiles, 0, own_count, False
    )
    sent(ghosts, near, picked)
    block, matrix = start_block, None
    own = first_own(start_block, own_tiles)
    for turn in range(ITERS):
        last = turn == ITERS - 1
        stacked, gram, *rows = product(
            tile_src, tile_dst, slot_count, block, own, ghosts, matrix, rest_tiles, not last
        )
        for masks_now in rounds[:-1]:
            gram = paired_sum(gram_round(gram, masks_now))
        if last:
            return final(gram_round(gram, rounds[-1]), stacked, total_states)
        ghosts = [None] * len(masks)
        picked = gather_colours(rows[0], *listed[0], len(far))
        gram, *picked = lax.optimization_barrier((gram, *picked))
        parts = gram_round(gram, rounds[-1])
        sent(ghosts, far, picked)
        near_rows, *parts = lax.optimization_barrier((rows[0], *parts))
        sent(ghosts, near, gather_colours(near_rows, *listed[1], len(near)))
        block, matrix, own = later_own(parts, stacked, own_tiles, total_states)


def solution(mesh):
    return jax.shard_map(
        on_device,
        mesh=mesh,
        in_specs=(
            P(None, ("groups", "dom")),
            P(("groups", "dom"), None, None),
            P(("groups", "dom")),
            P(("groups", "dom")),
            P(("groups", "dom")),
            P(("groups", "dom"), None, None),
        ),
        out_specs=P(None, ("groups", "dom")),
        check_vma=False,
    )
```

```python
import functools

import jax
import jax.numpy as jnp
from jax import lax
from jax.experimental import pallas as pl
from jax.experimental.pallas import tpu as pltpu
from jax.sharding import PartitionSpec as P

ITERS = 3
LANES = 128
PACK = 4
CHUNK = 1024
SUBLANES = 8
STEP = 4
COPIES = 8
F32 = jnp.float32
BF16 = jnp.bfloat16
VMEM = pl.BlockSpec(memory_space=pltpu.VMEM)
SMEM = pl.BlockSpec(memory_space=pltpu.SMEM)
HBM = pl.BlockSpec(memory_space=pltpu.HBM)
CHEAP = pl.CostEstimate(flops=0, bytes_accessed=1024, transcendentals=0)
PARAMS = pltpu.CompilerParams(vmem_limit_bytes=32 << 20)


def in_vmem(x):
    return pltpu.with_memory_space_constraint(x, pltpu.VMEM)


def in_hbm(x):
    return pltpu.with_memory_space_constraint(x, pltpu.HBM)


def vmem_out(shape, dtype):
    return pltpu.VMEM(shape, dtype)


def swapped(x, mask):
    size = lax.axis_size("dom")
    return lax.ppermute(x, "dom", [(i, i ^ mask) for i in range(size)])


def split3(x):
    high = x.astype(BF16)
    rest = x - high.astype(F32)
    mid = rest.astype(BF16)
    low = (rest - mid.astype(F32)).astype(BF16)
    return high, mid, low


def stack3(x):
    return jnp.concatenate(split3(x), axis=0)


def inverse_factor(gram):
    n = gram.shape[0]
    row = lax.broadcasted_iota(jnp.int32, (n, n), 0)
    col = lax.broadcasted_iota(jnp.int32, (n, n), 1)
    eye = (row == col).astype(F32)
    both = jnp.concatenate([gram, eye, jnp.zeros((n, LANES - 2 * n), F32)], axis=1)
    full = (SUBLANES, LANES)
    parts = [both[q : q + SUBLANES] for q in range(0, n, SUBLANES)]
    sub = lax.broadcasted_iota(jnp.int32, full, 0)
    scales = [jnp.zeros(full, F32) for _ in parts]
    for j in range(0, n, STEP):
        home, at = j // SUBLANES, j % SUBLANES
        live = range(home, len(parts))
        cols = [
            {q: jnp.broadcast_to(parts[q][:, j + a : j + a + 1], full) for q in live}
            for a in range(STEP)
        ]
        rows = [jnp.broadcast_to(parts[home][at + a : at + a + 1], full) for a in range(STEP)]
        entry = {
            (a, b): jnp.broadcast_to(cols[b][home][at + a : at + a + 1], full)
            for a in range(STEP)
            for b in range(a + 1)
        }
        for a in range(STEP):
            over = 1.0 / entry[a, a]
            ratio = {c: entry[c, a] * over for c in range(a + 1, STEP)}
            for c in range(a + 1, STEP):
                for d in range(a + 1, c + 1):
                    entry[c, d] = entry[c, d] - ratio[c] * entry[d, a]
            for c in range(a + 1, STEP):
                rows[c] = rows[c] - ratio[c] * rows[a]
                for q in live:
                    cols[c][q] = cols[c][q] - ratio[c] * cols[a][q]
            root = 1.0 / jnp.sqrt(entry[a, a])
            scales[home] = jnp.where(sub == at + a, root, scales[home])
            for q in live:
                factor = cols[a][q] * over
                if q == home:
                    factor = jnp.where(sub > at + a, factor, 0.0)
                parts[q] = parts[q] - factor * rows[a]
    done = jnp.concatenate([p * s for p, s in zip(parts, scales)], axis=0)
    return done[:, n : 2 * n]


def apply_matrix(inverse):
    high, mid, low = (t.astype(F32) for t in split3(inverse))
    zero = jnp.zeros_like(high)
    full = jnp.concatenate(
        [
            jnp.concatenate([high, high, high], axis=1),
            jnp.concatenate([mid, mid, zero], axis=1),
            jnp.concatenate([low, zero, zero], axis=1),
        ],
        axis=0,
    )
    return full.astype(BF16)


def applied(matrix, stacked):
    n = matrix.shape[0] // 3
    terms = jnp.dot(matrix, stacked, preferred_element_type=F32)
    return terms[:n] + (terms[n : 2 * n] + terms[2 * n :])


def packed(square):
    n = square.shape[0]
    count = LANES // n
    step = n // count
    return jnp.concatenate([square[q * step : (q + 1) * step] for q in range(count)], axis=1)


def unpacked(wide):
    step = wide.shape[0]
    n = LANES // PACK
    count = n // step
    return jnp.concatenate([wide[:, q * n : (q + 1) * n] for q in range(count)], axis=0)


def gram_of(parts, total_states):
    return unpacked(paired_sum(parts)) / total_states


def transposed_into(source, rows_ref):
    for g in range(rows_ref.shape[0] // LANES):
        pieces = [
            source[:, (PACK * g + b) * LANES : (PACK * g + b + 1) * LANES].astype(F32)
            for b in range(PACK)
        ]
        rows_ref[g * LANES : (g + 1) * LANES, :] = jnp.concatenate(pieces, axis=0).T


def gathered_into(unroll, row_ref, part_ref, rows_ref, picked, outs):
    count = picked.shape[0]
    columns = outs[0].shape[0]

    def pick(i, carry):
        for u in range(unroll):
            m = i * unroll + u
            picked[pl.ds(m, 1), :] = rows_ref[pl.ds(row_ref[m], 1), :]
        return carry

    lax.fori_loop(0, count // unroll, pick, 0)
    tiles_out = outs[0].shape[1] // LANES
    for g in range(count // LANES):
        y = picked[g * LANES : (g + 1) * LANES, :].T
        part = jnp.broadcast_to(part_ref[g : g + 1, :], (columns, LANES))
        value = y[:columns]
        for b in range(1, PACK):
            value = jnp.where(part == b, y[b * columns : (b + 1) * columns], value)
        out, t = outs[g // tiles_out], g % tiles_out
        out[:, t * LANES : (t + 1) * LANES] = value.astype(out.dtype)


def gather_kernel(row_ref, part_ref, rows_ref, *rest):
    gathered_into(64, row_ref, part_ref, rows_ref, rest[-1], rest[:-1])


def gather_colours(rows, row_list, part_list, count):
    indices = row_list.shape[0]
    columns = LANES // PACK
    return pl.pallas_call(
        gather_kernel,
        out_shape=[vmem_out((columns, indices // count), F32)] * count,
        in_specs=[SMEM, VMEM, VMEM],
        out_specs=[VMEM] * count,
        scratch_shapes=[pltpu.VMEM((indices, LANES), F32)],
        compiler_params=PARAMS,
        cost_estimate=CHEAP,
        name="gather_rows",
    )(row_list, in_vmem(part_list), in_vmem(rows))


def start_kernel(count, first, make_rows, row_ref, part_ref, source_ref, tiles_ref, *refs):
    outs, kept_ref, refs = refs[:count], refs[count], refs[count + 1 :]
    picked, sems = refs[-2:]
    size = kept_ref.shape[0] // COPIES
    copies = [
        pltpu.make_async_copy(
            tiles_ref.at[pl.ds(first + c * size, size)],
            kept_ref.at[pl.ds(c * size, size)],
            sems.at[c],
        )
        for c in range(COPIES)
    ]
    if make_rows:
        block_ref = refs[1]
        block_copy = pltpu.make_async_copy(source_ref, block_ref, sems.at[COPIES])
        block_copy.start()
    for copy in copies:
        copy.start()
    if make_rows:
        block_copy.wait()
    rows_ref = source_ref
    if make_rows:
        rows_ref = refs[0]
        transposed_into(block_ref, rows_ref)
    gathered_into(64, row_ref, part_ref, rows_ref, picked, outs)
    for copy in copies:
        copy.wait()


def start_gather(source, row_list, part_list, count, tiles, first, kept, make_rows):
    indices = row_list.shape[0]
    columns = LANES // PACK
    outs = [vmem_out((columns, indices // count), BF16)] * count
    outs.append(vmem_out((kept, *tiles.shape[1:]), tiles.dtype))
    if make_rows:
        outs.append(vmem_out((source.shape[1] // PACK, LANES), F32))
        outs.append(vmem_out(source.shape, source.dtype))
    source = in_hbm(source) if make_rows else in_vmem(source)
    return pl.pallas_call(
        functools.partial(start_kernel, count, first, make_rows),
        out_shape=outs,
        in_specs=[SMEM, VMEM, HBM if make_rows else VMEM, HBM],
        out_specs=[VMEM] * len(outs),
        scratch_shapes=[pltpu.VMEM((indices, LANES), F32), pltpu.SemaphoreType.DMA((COPIES + 1,))],
        compiler_params=PARAMS,
        cost_estimate=CHEAP,
        name="start_gather",
    )(row_list, in_vmem(part_list), source, in_hbm(tiles))


def own_slots(block_ref, tiles_ref, own_ref):
    tile_size = tiles_ref.shape[1]
    for t in range(own_ref.shape[1] // tile_size):
        at = slice(t * tile_size, (t + 1) * tile_size)
        own_ref[:, at] = jnp.dot(block_ref[:, at], tiles_ref[t], preferred_element_type=F32)


def first_own_kernel(block_ref, tiles_ref, own_ref):
    own_slots(block_ref, tiles_ref, own_ref)


def first_own(block, tiles):
    return pl.pallas_call(
        first_own_kernel,
        out_shape=vmem_out(block.shape, F32),
        in_specs=[VMEM] * 2,
        out_specs=VMEM,
        compiler_params=PARAMS,
        cost_estimate=CHEAP,
        name="first_own",
    )(in_vmem(block), in_vmem(tiles))


def later_own_kernel(total_states, *refs):
    grams, stacked, tiles_ref = refs[:4], refs[4], refs[5]
    block_ref, matrix_ref, own_ref = refs[6:]
    matrix = apply_matrix(inverse_factor(gram_of([r[...] for r in grams], total_states)))
    matrix_ref[...] = matrix
    for c in range(0, block_ref.shape[1], CHUNK):
        block_ref[:, c : c + CHUNK] = applied(matrix, stacked[:, c : c + CHUNK]).astype(BF16)
    own_slots(block_ref, tiles_ref, own_ref)


def later_own(grams, stacked, tiles, total_states):
    columns, states = stacked.shape[0] // 3, stacked.shape[1]
    return pl.pallas_call(
        functools.partial(later_own_kernel, total_states),
        out_shape=[
            vmem_out((columns, states), BF16),
            vmem_out((3 * columns, 3 * columns), BF16),
            vmem_out((columns, states), F32),
        ],
        in_specs=[VMEM] * 6,
        out_specs=[VMEM] * 3,
        compiler_params=PARAMS,
        cost_estimate=CHEAP,
        name="later_own",
    )(*[in_vmem(g) for g in grams], in_vmem(stacked), in_vmem(tiles))


def product_kernel(colours, group, with_rows, *refs):
    src_ref, dst_ref, count_ref, block_ref, own_ref = refs[:5]
    ghosts, refs = refs[5 : 5 + colours], refs[5 + colours :]
    matrix_ref = None
    if ghosts[0].dtype == F32:
        matrix_ref, refs = refs[0], refs[1:]
    tiles_ref, refs = refs[0], refs[1:]
    stacked_ref, gram_ref, refs = refs[0], refs[1], refs[2:]
    if with_rows:
        rows_ref, refs = refs[0], refs[1:]
    source, total = refs
    columns, states = block_ref.shape
    tile_size = tiles_ref.shape[1]
    first = states // tile_size
    live = count_ref[0]

    source[:, :states] = block_ref[...]
    at = states
    for ghost in ghosts:
        width = ghost.shape[1]
        value = ghost[...]
        if matrix_ref is not None:
            value = applied(matrix_ref[...], stack3(value)).astype(BF16)
        source[:, at : at + width] = value
        at += width
    source[:, at:] = jnp.zeros((columns, tile_size), BF16)
    nothing = at // tile_size
    total[...] = own_ref[...]

    def tile_at(s):
        index = jnp.where(s < live, src_ref[s], nothing)
        return source[:, pl.ds(pl.multiple_of(index * tile_size, tile_size), tile_size)]

    zero = jnp.zeros((columns, tile_size), BF16)

    def body(i, carry):
        base = first + i * group
        terms = []
        for u in range(0, group, 2):
            pair = jnp.concatenate(
                [
                    jnp.concatenate([tile_at(base + u), zero], axis=1),
                    jnp.concatenate([zero, tile_at(base + u + 1)], axis=1),
                ],
                axis=0,
            )
            weights = tiles_ref[pl.ds(base + u - first, 2)].reshape(2 * tile_size, tile_size)
            both = jnp.dot(pair, weights, preferred_element_type=F32)
            terms += [both[:columns], both[columns:]]
        for u in range(group):
            where = pl.multiple_of(dst_ref[base + u] * tile_size, tile_size)
            total[:, pl.ds(where, tile_size)] += terms[u]
        return carry

    lax.fori_loop(0, (live - first + group - 1) // group, body, 0)

    gram = jnp.zeros((3 * columns, 3 * columns), F32)
    for c in range(0, states, CHUNK):
        part = stack3(total[:, c : c + CHUNK])
        stacked_ref[:, c : c + CHUNK] = part
        gram += lax.dot_general(part, part, (((1,), (1,)), ((), ())), preferred_element_type=F32)
    blocks = [
        gram[a * columns : (a + 1) * columns, b * columns : (b + 1) * columns]
        for a in range(3)
        for b in range(3)
    ]
    small = blocks[8] + (blocks[5] + blocks[7])
    middle = blocks[4] + (blocks[2] + blocks[6])
    gram_ref[...] = packed(blocks[0] + ((blocks[1] + blocks[3]) + (middle + small)))
    if with_rows:
        transposed_into(total, rows_ref)


def product(src, dst, count, block, own, ghosts, matrix, tiles, with_rows):
    columns, states = block.shape
    rest, tile_size, _ = tiles.shape
    group = 64
    while rest % group:
        group //= 2
    outs = [vmem_out((3 * columns, states), BF16), vmem_out((columns * columns // LANES, LANES), F32)]
    if with_rows:
        outs.append(vmem_out((states // PACK, LANES), F32))
    operands = [block, own, *ghosts] + ([] if matrix is None else [matrix]) + [tiles]
    width = states + sum(g.shape[1] for g in ghosts) + tile_size
    return pl.pallas_call(
        functools.partial(product_kernel, len(ghosts), group, with_rows),
        out_shape=outs,
        in_specs=[SMEM] * 3 + [VMEM] * len(operands),
        out_specs=[VMEM] * len(outs),
        scratch_shapes=[pltpu.VMEM((columns, width), BF16), pltpu.VMEM((columns, states), F32)],
        compiler_params=PARAMS,
        cost_estimate=CHEAP,
        name="product",
    )(src, dst, count, *[in_vmem(x) for x in operands])


def final_kernel(total_states, *refs):
    grams, stacked, out_ref, ready, sems = refs[:4], *refs[4:]
    matrix = apply_matrix(inverse_factor(gram_of([r[...] for r in grams], total_states)))
    copies = []
    for n, c in enumerate(range(0, out_ref.shape[1], CHUNK)):
        at = pl.ds(c, CHUNK)
        ready[:, at] = applied(matrix, stacked[:, at])
        copies.append(pltpu.make_async_copy(ready.at[:, at], out_ref.at[:, at], sems.at[n]))
        copies[-1].start()
    for copy in copies:
        copy.wait()


def final(grams, stacked, total_states):
    columns, states = stacked.shape[0] // 3, stacked.shape[1]
    return pl.pallas_call(
        functools.partial(final_kernel, total_states),
        out_shape=jax.ShapeDtypeStruct((columns, states), F32),
        in_specs=[VMEM] * 5,
        out_specs=HBM,
        scratch_shapes=[
            pltpu.VMEM((columns, states), F32),
            pltpu.SemaphoreType.DMA((states // CHUNK,)),
        ],
        compiler_params=PARAMS,
        cost_estimate=CHEAP,
        name="final",
    )(*[in_vmem(g) for g in grams], in_vmem(stacked))


def dom_rounds(size):
    rounds, step = [], 1
    while step < size:
        span = min(4, size // step)
        rounds.append([step * k for k in range(1, span)])
        step *= span
    return rounds[::-1]


def paired_sum(parts):
    return (parts[0] + parts[1]) + (parts[2] + parts[3])


def gram_round(gram, masks):
    parts = [gram] + [swapped(gram, mask) for mask in masks]
    return parts + [jnp.zeros_like(gram)] * (4 - len(parts))


def on_device(start_block, tiles, tile_src, tile_dst, slot_count, send_rows):
    size = lax.axis_size("dom")
    masks = [1, 2, 4, 1 << (size.bit_length() - 2)]
    columns, states = start_block.shape
    total_states = states * size
    rounds = dom_rounds(size)
    lists = send_rows[0]
    pack_states = PACK * LANES
    row_lists = lists // pack_states * LANES + lists % LANES
    part_lists = lists // LANES % PACK
    far = (3, 2)
    near = (1, 0)

    def lists_of(colours):
        rows = jnp.concatenate([row_lists[c] for c in colours])
        parts = jnp.concatenate([part_lists[c] for c in colours]).reshape(-1, LANES)
        return rows, parts

    listed = [lists_of(far), lists_of(near)]

    def sent(ghosts, colours, picked):
        for colour, x in zip(colours, picked):
            ghosts[colour] = swapped(x, masks[colour])

    own_count = states // tiles.shape[1]
    ghosts = [None] * len(masks)
    *picked, rest_tiles, start_rows, block = start_gather(
        start_block, *listed[0], len(far), tiles, own_count, tiles.shape[0] - own_count, True
    )
    sent(ghosts, far, picked)
    *picked, own_tiles = start_gather(
        start_rows, *listed[1], len(near), tiles, 0, own_count, False
    )
    sent(ghosts, near, picked)
    matrix = None
    own = first_own(block, own_tiles)
    for turn in range(ITERS):
        last = turn == ITERS - 1
        stacked, gram, *rows = product(
            tile_src, tile_dst, slot_count, block, own, ghosts, matrix, rest_tiles, not last
        )
        for masks_now in rounds[:-1]:
            gram = paired_sum(gram_round(gram, masks_now))
        if last:
            return final(gram_round(gram, rounds[-1]), stacked, total_states)
        ghosts = [None] * len(masks)
        picked = gather_colours(rows[0], *listed[0], len(far))
        gram, *picked = lax.optimization_barrier((gram, *picked))
        parts = gram_round(gram, rounds[-1])
        sent(ghosts, far, picked)
        near_rows, *parts = lax.optimization_barrier((rows[0], *parts))
        sent(ghosts, near, gather_colours(near_rows, *listed[1], len(near)))
        block, matrix, own = later_own(parts, stacked, own_tiles, total_states)


def solution(mesh):
    return jax.shard_map(
        on_device,
        mesh=mesh,
        in_specs=(
            P(None, ("groups", "dom")),
            P(("groups", "dom"), None, None),
            P(("groups", "dom")),
            P(("groups", "dom")),
            P(("groups", "dom")),
            P(("groups", "dom"), None, None),
        ),
        out_specs=P(None, ("groups", "dom")),
        check_vma=False,
    )
```

```python
import functools

import jax
import jax.numpy as jnp
from jax import lax
from jax.experimental import pallas as pl
from jax.experimental.pallas import tpu as pltpu
from jax.sharding import PartitionSpec as P

ITERS = 3
LANES = 128
PACK = 4
CHUNK = 1024
SUBLANES = 8
STEP = 4
COPIES = 8
F32 = jnp.float32
BF16 = jnp.bfloat16
VMEM = pl.BlockSpec(memory_space=pltpu.VMEM)
SMEM = pl.BlockSpec(memory_space=pltpu.SMEM)
HBM = pl.BlockSpec(memory_space=pltpu.HBM)
CHEAP = pl.CostEstimate(flops=0, bytes_accessed=1024, transcendentals=0)
PARAMS = pltpu.CompilerParams(vmem_limit_bytes=32 << 20)


def in_vmem(x):
    return pltpu.with_memory_space_constraint(x, pltpu.VMEM)


def in_hbm(x):
    return pltpu.with_memory_space_constraint(x, pltpu.HBM)


def vmem_out(shape, dtype):
    return pltpu.VMEM(shape, dtype)


def swapped(x, mask):
    size = lax.axis_size("dom")
    return lax.ppermute(x, "dom", [(i, i ^ mask) for i in range(size)])


def split3(x):
    high = x.astype(BF16)
    rest = x - high.astype(F32)
    mid = rest.astype(BF16)
    low = (rest - mid.astype(F32)).astype(BF16)
    return high, mid, low


def stack3(x):
    return jnp.concatenate(split3(x), axis=0)


def inverse_factor(gram):
    n = gram.shape[0]
    row = lax.broadcasted_iota(jnp.int32, (n, n), 0)
    col = lax.broadcasted_iota(jnp.int32, (n, n), 1)
    eye = (row == col).astype(F32)
    both = jnp.concatenate([gram, eye, jnp.zeros((n, LANES - 2 * n), F32)], axis=1)
    full = (SUBLANES, LANES)
    parts = [both[q : q + SUBLANES] for q in range(0, n, SUBLANES)]
    sub = lax.broadcasted_iota(jnp.int32, full, 0)
    scales = [jnp.zeros(full, F32) for _ in parts]
    for j in range(0, n, STEP):
        home, at = j // SUBLANES, j % SUBLANES
        live = range(home, len(parts))
        cols = [
            {q: jnp.broadcast_to(parts[q][:, j + a : j + a + 1], full) for q in live}
            for a in range(STEP)
        ]
        rows = [jnp.broadcast_to(parts[home][at + a : at + a + 1], full) for a in range(STEP)]
        entry = {
            (a, b): jnp.broadcast_to(cols[b][home][at + a : at + a + 1], full)
            for a in range(STEP)
            for b in range(a + 1)
        }
        for a in range(STEP):
            over = 1.0 / entry[a, a]
            ratio = {c: entry[c, a] * over for c in range(a + 1, STEP)}
            for c in range(a + 1, STEP):
                for d in range(a + 1, c + 1):
                    entry[c, d] = entry[c, d] - ratio[c] * entry[d, a]
            for c in range(a + 1, STEP):
                rows[c] = rows[c] - ratio[c] * rows[a]
                for q in live:
                    cols[c][q] = cols[c][q] - ratio[c] * cols[a][q]
            root = 1.0 / jnp.sqrt(entry[a, a])
            scales[home] = jnp.where(sub == at + a, root, scales[home])
            for q in live:
                factor = cols[a][q] * over
                if q == home:
                    factor = jnp.where(sub > at + a, factor, 0.0)
                parts[q] = parts[q] - factor * rows[a]
    done = jnp.concatenate([p * s for p, s in zip(parts, scales)], axis=0)
    return done[:, n : 2 * n]


def apply_matrix(inverse):
    high, mid, low = (t.astype(F32) for t in split3(inverse))
    zero = jnp.zeros_like(high)
    full = jnp.concatenate(
        [
            jnp.concatenate([high, high, high], axis=1),
            jnp.concatenate([mid, mid, zero], axis=1),
            jnp.concatenate([low, zero, zero], axis=1),
        ],
        axis=0,
    )
    return full.astype(BF16)


def applied(matrix, stacked):
    n = matrix.shape[0] // 3
    terms = jnp.dot(matrix, stacked, preferred_element_type=F32)
    return terms[:n] + (terms[n : 2 * n] + terms[2 * n :])


def packed(square):
    n = square.shape[0]
    count = LANES // n
    step = n // count
    return jnp.concatenate([square[q * step : (q + 1) * step] for q in range(count)], axis=1)


def unpacked(wide):
    step = wide.shape[0]
    n = LANES // PACK
    count = n // step
    return jnp.concatenate([wide[:, q * n : (q + 1) * n] for q in range(count)], axis=0)


def gram_of(parts, total_states):
    return unpacked(paired_sum(parts)) / total_states


def transposed_into(source, rows_ref):
    for g in range(rows_ref.shape[0] // LANES):
        pieces = [
            source[:, (PACK * g + b) * LANES : (PACK * g + b + 1) * LANES].astype(F32)
            for b in range(PACK)
        ]
        rows_ref[g * LANES : (g + 1) * LANES, :] = jnp.concatenate(pieces, axis=0).T


def gathered_into(unroll, row_ref, part_ref, rows_ref, picked, outs):
    count = picked.shape[0]
    columns = outs[0].shape[0]

    def pick(i, carry):
        for u in range(unroll):
            m = i * unroll + u
            picked[pl.ds(m, 1), :] = rows_ref[pl.ds(row_ref[m], 1), :]
        return carry

    lax.fori_loop(0, count // unroll, pick, 0)
    tiles_out = outs[0].shape[1] // LANES
    for g in range(count // LANES):
        y = picked[g * LANES : (g + 1) * LANES, :].T
        part = jnp.broadcast_to(part_ref[g : g + 1, :], (columns, LANES))
        value = y[:columns]
        for b in range(1, PACK):
            value = jnp.where(part == b, y[b * columns : (b + 1) * columns], value)
        out, t = outs[g // tiles_out], g % tiles_out
        out[:, t * LANES : (t + 1) * LANES] = value.astype(out.dtype)


def gather_kernel(row_ref, part_ref, rows_ref, *rest):
    gathered_into(64, row_ref, part_ref, rows_ref, rest[-1], rest[:-1])


def gather_colours(rows, row_list, part_list, count):
    indices = row_list.shape[0]
    columns = LANES // PACK
    return pl.pallas_call(
        gather_kernel,
        out_shape=[vmem_out((columns, indices // count), F32)] * count,
        in_specs=[SMEM, VMEM, VMEM],
        out_specs=[VMEM] * count,
        scratch_shapes=[pltpu.VMEM((indices, LANES), F32)],
        compiler_params=PARAMS,
        cost_estimate=CHEAP,
        name="gather_rows",
    )(row_list, in_vmem(part_list), in_vmem(rows))


def start_kernel(count, first, make_rows, row_ref, part_ref, source_ref, tiles_ref, *refs):
    outs, kept_ref, refs = refs[:count], refs[count], refs[count + 1 :]
    picked, sems = refs[-2:]
    size = kept_ref.shape[0] // COPIES
    copies = [
        pltpu.make_async_copy(
            tiles_ref.at[pl.ds(first + c * size, size)],
            kept_ref.at[pl.ds(c * size, size)],
            sems.at[c],
        )
        for c in range(COPIES)
    ]
    if make_rows:
        block_ref = refs[1]
        block_copy = pltpu.make_async_copy(source_ref, block_ref, sems.at[COPIES])
        block_copy.start()
    for copy in copies:
        copy.start()
    if make_rows:
        block_copy.wait()
    rows_ref = source_ref
    if make_rows:
        rows_ref = refs[0]
        transposed_into(block_ref, rows_ref)
    gathered_into(64, row_ref, part_ref, rows_ref, picked, outs)
    for copy in copies:
        copy.wait()


def start_gather(source, row_list, part_list, count, tiles, first, kept, make_rows):
    indices = row_list.shape[0]
    columns = LANES // PACK
    outs = [vmem_out((columns, indices // count), BF16)] * count
    outs.append(vmem_out((kept, *tiles.shape[1:]), tiles.dtype))
    if make_rows:
        outs.append(vmem_out((source.shape[1] // PACK, LANES), F32))
        outs.append(vmem_out(source.shape, source.dtype))
    source = in_hbm(source) if make_rows else in_vmem(source)
    return pl.pallas_call(
        functools.partial(start_kernel, count, first, make_rows),
        out_shape=outs,
        in_specs=[SMEM, VMEM, HBM if make_rows else VMEM, HBM],
        out_specs=[VMEM] * len(outs),
        scratch_shapes=[pltpu.VMEM((indices, LANES), F32), pltpu.SemaphoreType.DMA((COPIES + 1,))],
        compiler_params=PARAMS,
        cost_estimate=CHEAP,
        name="start_gather",
    )(row_list, in_vmem(part_list), source, in_hbm(tiles))


def own_slots(block_ref, tiles_ref, own_ref):
    tile_size = tiles_ref.shape[1]
    for t in range(own_ref.shape[1] // tile_size):
        at = slice(t * tile_size, (t + 1) * tile_size)
        own_ref[:, at] = jnp.dot(block_ref[:, at], tiles_ref[t], preferred_element_type=F32)


def first_own_kernel(block_ref, tiles_ref, own_ref):
    own_slots(block_ref, tiles_ref, own_ref)


def first_own(block, tiles):
    return pl.pallas_call(
        first_own_kernel,
        out_shape=vmem_out(block.shape, F32),
        in_specs=[VMEM] * 2,
        out_specs=VMEM,
        compiler_params=PARAMS,
        cost_estimate=CHEAP,
        name="first_own",
    )(in_vmem(block), in_vmem(tiles))


def later_own_kernel(total_states, *refs):
    grams, stacked, tiles_ref = refs[:4], refs[4], refs[5]
    block_ref, matrix_ref, own_ref = refs[6:]
    matrix = apply_matrix(inverse_factor(gram_of([r[...] for r in grams], total_states)))
    matrix_ref[...] = matrix
    for c in range(0, block_ref.shape[1], CHUNK):
        block_ref[:, c : c + CHUNK] = applied(matrix, stacked[:, c : c + CHUNK]).astype(BF16)
    own_slots(block_ref, tiles_ref, own_ref)


def later_own(grams, stacked, tiles, total_states):
    columns, states = stacked.shape[0] // 3, stacked.shape[1]
    return pl.pallas_call(
        functools.partial(later_own_kernel, total_states),
        out_shape=[
            vmem_out((columns, states), BF16),
            vmem_out((3 * columns, 3 * columns), BF16),
            vmem_out((columns, states), F32),
        ],
        in_specs=[VMEM] * 6,
        out_specs=[VMEM] * 3,
        compiler_params=PARAMS,
        cost_estimate=CHEAP,
        name="later_own",
    )(*[in_vmem(g) for g in grams], in_vmem(stacked), in_vmem(tiles))


def product_kernel(colours, group, with_rows, *refs):
    src_ref, dst_ref, count_ref, block_ref, own_ref = refs[:5]
    ghosts, refs = refs[5 : 5 + colours], refs[5 + colours :]
    matrix_ref = None
    if ghosts[0].dtype == F32:
        matrix_ref, refs = refs[0], refs[1:]
    tiles_ref, refs = refs[0], refs[1:]
    stacked_ref, gram_ref, refs = refs[0], refs[1], refs[2:]
    if with_rows:
        rows_ref, refs = refs[0], refs[1:]
    source, total = refs
    columns, states = block_ref.shape
    tile_size = tiles_ref.shape[1]
    first = states // tile_size
    live = count_ref[0]

    source[:, :states] = block_ref[...]
    width = ghosts[0].shape[1]
    for n, ghost in enumerate(ghosts):
        at = states + (len(ghosts) - 1 - n) * width
        value = ghost[...]
        if matrix_ref is not None:
            value = applied(matrix_ref[...], stack3(value)).astype(BF16)
        source[:, at : at + width] = value
    at = states + len(ghosts) * width
    source[:, at:] = jnp.zeros((columns, tile_size), BF16)
    nothing = at // tile_size
    total[...] = own_ref[...]

    def tile_at(s):
        index = jnp.where(s < live, src_ref[s], nothing)
        return source[:, pl.ds(pl.multiple_of(index * tile_size, tile_size), tile_size)]

    zero = jnp.zeros((columns, tile_size), BF16)

    def body(i, carry):
        base = first + i * group
        terms = []
        for u in range(0, group, 2):
            pair = jnp.concatenate(
                [
                    jnp.concatenate([tile_at(base + u), zero], axis=1),
                    jnp.concatenate([zero, tile_at(base + u + 1)], axis=1),
                ],
                axis=0,
            )
            weights = tiles_ref[pl.ds(base + u - first, 2)].reshape(2 * tile_size, tile_size)
            both = jnp.dot(pair, weights, preferred_element_type=F32)
            terms += [both[:columns], both[columns:]]
        for u in range(group):
            where = pl.multiple_of(dst_ref[base + u] * tile_size, tile_size)
            total[:, pl.ds(where, tile_size)] += terms[u]
        return carry

    lax.fori_loop(0, (live - first + group - 1) // group, body, 0)

    gram = jnp.zeros((3 * columns, 3 * columns), F32)
    for c in range(0, states, CHUNK):
        part = stack3(total[:, c : c + CHUNK])
        stacked_ref[:, c : c + CHUNK] = part
        gram += lax.dot_general(part, part, (((1,), (1,)), ((), ())), preferred_element_type=F32)
    blocks = [
        gram[a * columns : (a + 1) * columns, b * columns : (b + 1) * columns]
        for a in range(3)
        for b in range(3)
    ]
    small = blocks[8] + (blocks[5] + blocks[7])
    middle = blocks[4] + (blocks[2] + blocks[6])
    gram_ref[...] = packed(blocks[0] + ((blocks[1] + blocks[3]) + (middle + small)))
    if with_rows:
        transposed_into(total, rows_ref)


def product(src, dst, count, block, own, ghosts, matrix, tiles, with_rows):
    columns, states = block.shape
    rest, tile_size, _ = tiles.shape
    group = 64
    while rest % group:
        group //= 2
    outs = [vmem_out((3 * columns, states), BF16), vmem_out((columns * columns // LANES, LANES), F32)]
    if with_rows:
        outs.append(vmem_out((states // PACK, LANES), F32))
    operands = [block, own, *ghosts[::-1]] + ([] if matrix is None else [matrix]) + [tiles]
    width = states + sum(g.shape[1] for g in ghosts) + tile_size
    return pl.pallas_call(
        functools.partial(product_kernel, len(ghosts), group, with_rows),
        out_shape=outs,
        in_specs=[SMEM] * 3 + [VMEM] * len(operands),
        out_specs=[VMEM] * len(outs),
        scratch_shapes=[pltpu.VMEM((columns, width), BF16), pltpu.VMEM((columns, states), F32)],
        compiler_params=PARAMS,
        cost_estimate=CHEAP,
        name="product",
    )(src, dst, count, *[in_vmem(x) for x in operands])


def final_kernel(total_states, *refs):
    grams, stacked, out_ref, ready, sems = refs[:4], *refs[4:]
    matrix = apply_matrix(inverse_factor(gram_of([r[...] for r in grams], total_states)))
    copies = []
    for n, c in enumerate(range(0, out_ref.shape[1], CHUNK)):
        at = pl.ds(c, CHUNK)
        ready[:, at] = applied(matrix, stacked[:, at])
        copies.append(pltpu.make_async_copy(ready.at[:, at], out_ref.at[:, at], sems.at[n]))
        copies[-1].start()
    for copy in copies:
        copy.wait()


def final(grams, stacked, total_states):
    columns, states = stacked.shape[0] // 3, stacked.shape[1]
    return pl.pallas_call(
        functools.partial(final_kernel, total_states),
        out_shape=jax.ShapeDtypeStruct((columns, states), F32),
        in_specs=[VMEM] * 5,
        out_specs=HBM,
        scratch_shapes=[
            pltpu.VMEM((columns, states), F32),
            pltpu.SemaphoreType.DMA((states // CHUNK,)),
        ],
        compiler_params=PARAMS,
        cost_estimate=CHEAP,
        name="final",
    )(*[in_vmem(g) for g in grams], in_vmem(stacked))


def dom_rounds(size):
    rounds, step = [], 1
    while step < size:
        span = min(4, size // step)
        rounds.append([step * k for k in range(1, span)])
        step *= span
    return rounds[::-1]


def paired_sum(parts):
    return (parts[0] + parts[1]) + (parts[2] + parts[3])


def gram_round(gram, masks):
    parts = [gram] + [swapped(gram, mask) for mask in masks]
    return parts + [jnp.zeros_like(gram)] * (4 - len(parts))


def on_device(start_block, tiles, tile_src, tile_dst, slot_count, send_rows):
    size = lax.axis_size("dom")
    masks = [1, 2, 4, 1 << (size.bit_length() - 2)]
    columns, states = start_block.shape
    total_states = states * size
    rounds = dom_rounds(size)
    lists = send_rows[0]
    pack_states = PACK * LANES
    row_lists = lists // pack_states * LANES + lists % LANES
    part_lists = lists // LANES % PACK
    far = (3, 2)
    near = (1, 0)

    def lists_of(colours):
        rows = jnp.concatenate([row_lists[c] for c in colours])
        parts = jnp.concatenate([part_lists[c] for c in colours]).reshape(-1, LANES)
        return rows, parts

    listed = [lists_of(far), lists_of(near)]

    def sent(ghosts, colours, picked):
        for colour, x in zip(colours, picked):
            ghosts[colour] = swapped(x, masks[colour])

    own_count = states // tiles.shape[1]
    ghosts = [None] * len(masks)
    *picked, rest_tiles, start_rows, block = start_gather(
        start_block, *listed[0], len(far), tiles, own_count, tiles.shape[0] - own_count, True
    )
    sent(ghosts, far, picked)
    *picked, own_tiles = start_gather(
        start_rows, *listed[1], len(near), tiles, 0, own_count, False
    )
    sent(ghosts, near, picked)
    matrix = None
    own = first_own(block, own_tiles)
    for turn in range(ITERS):
        last = turn == ITERS - 1
        stacked, gram, *rows = product(
            tile_src, tile_dst, slot_count, block, own, ghosts, matrix, rest_tiles, not last
        )
        for masks_now in rounds[:-1]:
            gram = paired_sum(gram_round(gram, masks_now))
        if last:
            return final(gram_round(gram, rounds[-1]), stacked, total_states)
        ghosts = [None] * len(masks)
        picked = gather_colours(rows[0], *listed[0], len(far))
        gram, *picked = lax.optimization_barrier((gram, *picked))
        parts = gram_round(gram, rounds[-1])
        sent(ghosts, far, picked)
        near_rows, *parts = lax.optimization_barrier((rows[0], *parts))
        sent(ghosts, near, gather_colours(near_rows, *listed[1], len(near)))
        block, matrix, own = later_own(parts, stacked, own_tiles, total_states)


def solution(mesh):
    return jax.shard_map(
        on_device,
        mesh=mesh,
        in_specs=(
            P(None, ("groups", "dom")),
            P(("groups", "dom"), None, None),
            P(("groups", "dom")),
            P(("groups", "dom")),
            P(("groups", "dom")),
            P(("groups", "dom"), None, None),
        ),
        out_specs=P(None, ("groups", "dom")),
        check_vma=False,
    )
```

```python
import functools

import jax
import jax.numpy as jnp
from jax import lax
from jax.experimental import pallas as pl
from jax.experimental.pallas import tpu as pltpu
from jax.sharding import PartitionSpec as P

ITERS = 3
LANES = 128
PACK = 4
CHUNK = 1024
SUBLANES = 8
STEP = 4
COPIES = 8
LARGE = 64
SMALL = 16
F32 = jnp.float32
BF16 = jnp.bfloat16
VMEM = pl.BlockSpec(memory_space=pltpu.VMEM)
SMEM = pl.BlockSpec(memory_space=pltpu.SMEM)
HBM = pl.BlockSpec(memory_space=pltpu.HBM)
CHEAP = pl.CostEstimate(flops=0, bytes_accessed=1024, transcendentals=0)
PARAMS = pltpu.CompilerParams(vmem_limit_bytes=32 << 20)


def in_vmem(x):
    return pltpu.with_memory_space_constraint(x, pltpu.VMEM)


def in_hbm(x):
    return pltpu.with_memory_space_constraint(x, pltpu.HBM)


def vmem_out(shape, dtype):
    return pltpu.VMEM(shape, dtype)


def swapped(x, mask):
    size = lax.axis_size("dom")
    return lax.ppermute(x, "dom", [(i, i ^ mask) for i in range(size)])


def split3(x):
    high = x.astype(BF16)
    rest = x - high.astype(F32)
    mid = rest.astype(BF16)
    low = (rest - mid.astype(F32)).astype(BF16)
    return high, mid, low


def stack3(x):
    return jnp.concatenate(split3(x), axis=0)


def inverse_factor(gram):
    n = gram.shape[0]
    row = lax.broadcasted_iota(jnp.int32, (n, n), 0)
    col = lax.broadcasted_iota(jnp.int32, (n, n), 1)
    eye = (row == col).astype(F32)
    both = jnp.concatenate([gram, eye, jnp.zeros((n, LANES - 2 * n), F32)], axis=1)
    full = (SUBLANES, LANES)
    parts = [both[q : q + SUBLANES] for q in range(0, n, SUBLANES)]
    sub = lax.broadcasted_iota(jnp.int32, full, 0)
    scales = [jnp.zeros(full, F32) for _ in parts]
    for j in range(0, n, STEP):
        home, at = j // SUBLANES, j % SUBLANES
        live = range(home, len(parts))
        cols = [
            {q: jnp.broadcast_to(parts[q][:, j + a : j + a + 1], full) for q in live}
            for a in range(STEP)
        ]
        rows = [jnp.broadcast_to(parts[home][at + a : at + a + 1], full) for a in range(STEP)]
        entry = {
            (a, b): jnp.broadcast_to(cols[b][home][at + a : at + a + 1], full)
            for a in range(STEP)
            for b in range(a + 1)
        }
        for a in range(STEP):
            over = 1.0 / entry[a, a]
            ratio = {c: entry[c, a] * over for c in range(a + 1, STEP)}
            for c in range(a + 1, STEP):
                for d in range(a + 1, c + 1):
                    entry[c, d] = entry[c, d] - ratio[c] * entry[d, a]
            for c in range(a + 1, STEP):
                rows[c] = rows[c] - ratio[c] * rows[a]
                for q in live:
                    cols[c][q] = cols[c][q] - ratio[c] * cols[a][q]
            root = 1.0 / jnp.sqrt(entry[a, a])
            scales[home] = jnp.where(sub == at + a, root, scales[home])
            for q in live:
                factor = cols[a][q] * over
                if q == home:
                    factor = jnp.where(sub > at + a, factor, 0.0)
                parts[q] = parts[q] - factor * rows[a]
    done = jnp.concatenate([p * s for p, s in zip(parts, scales)], axis=0)
    return done[:, n : 2 * n]


def apply_matrix(inverse):
    high, mid, low = (t.astype(F32) for t in split3(inverse))
    zero = jnp.zeros_like(high)
    full = jnp.concatenate(
        [
            jnp.concatenate([high, high, high], axis=1),
            jnp.concatenate([mid, mid, zero], axis=1),
            jnp.concatenate([low, zero, zero], axis=1),
        ],
        axis=0,
    )
    return full.astype(BF16)


def applied(matrix, stacked):
    n = matrix.shape[0] // 3
    terms = jnp.dot(matrix, stacked, preferred_element_type=F32)
    return terms[:n] + (terms[n : 2 * n] + terms[2 * n :])


def packed(square):
    n = square.shape[0]
    count = LANES // n
    step = n // count
    return jnp.concatenate([square[q * step : (q + 1) * step] for q in range(count)], axis=1)


def unpacked(wide):
    step = wide.shape[0]
    n = LANES // PACK
    count = n // step
    return jnp.concatenate([wide[:, q * n : (q + 1) * n] for q in range(count)], axis=0)


def gram_of(parts, total_states):
    return unpacked(paired_sum(parts)) / total_states


def transposed_into(source, rows_ref):
    for g in range(rows_ref.shape[0] // LANES):
        pieces = [
            source[:, (PACK * g + b) * LANES : (PACK * g + b + 1) * LANES].astype(F32)
            for b in range(PACK)
        ]
        rows_ref[g * LANES : (g + 1) * LANES, :] = jnp.concatenate(pieces, axis=0).T


def gathered_into(unroll, row_ref, part_ref, rows_ref, picked, outs):
    count = picked.shape[0]
    columns = outs[0].shape[0]

    def pick(i, carry):
        for u in range(unroll):
            m = i * unroll + u
            picked[pl.ds(m, 1), :] = rows_ref[pl.ds(row_ref[m], 1), :]
        return carry

    lax.fori_loop(0, count // unroll, pick, 0)
    tiles_out = outs[0].shape[1] // LANES
    for g in range(count // LANES):
        y = picked[g * LANES : (g + 1) * LANES, :].T
        part = jnp.broadcast_to(part_ref[g : g + 1, :], (columns, LANES))
        value = y[:columns]
        for b in range(1, PACK):
            value = jnp.where(part == b, y[b * columns : (b + 1) * columns], value)
        out, t = outs[g // tiles_out], g % tiles_out
        out[:, t * LANES : (t + 1) * LANES] = value.astype(out.dtype)


def gather_kernel(row_ref, part_ref, rows_ref, *rest):
    gathered_into(64, row_ref, part_ref, rows_ref, rest[-1], rest[:-1])


def gather_colours(rows, row_list, part_list, count):
    indices = row_list.shape[0]
    columns = LANES // PACK
    return pl.pallas_call(
        gather_kernel,
        out_shape=[vmem_out((columns, indices // count), F32)] * count,
        in_specs=[SMEM, VMEM, VMEM],
        out_specs=[VMEM] * count,
        scratch_shapes=[pltpu.VMEM((indices, LANES), F32)],
        compiler_params=PARAMS,
        cost_estimate=CHEAP,
        name="gather_rows",
    )(row_list, in_vmem(part_list), in_vmem(rows))


def start_kernel(count, first, make_rows, row_ref, part_ref, source_ref, tiles_ref, *refs):
    outs, kept_ref, refs = refs[:count], refs[count], refs[count + 1 :]
    picked, sems = refs[-2:]
    size = kept_ref.shape[0] // COPIES
    copies = [
        pltpu.make_async_copy(
            tiles_ref.at[pl.ds(first + c * size, size)],
            kept_ref.at[pl.ds(c * size, size)],
            sems.at[c],
        )
        for c in range(COPIES)
    ]
    if make_rows:
        block_ref = refs[1]
        block_copy = pltpu.make_async_copy(source_ref, block_ref, sems.at[COPIES])
        block_copy.start()
    for copy in copies:
        copy.start()
    if make_rows:
        block_copy.wait()
    rows_ref = source_ref
    if make_rows:
        rows_ref = refs[0]
        transposed_into(block_ref, rows_ref)
    gathered_into(64, row_ref, part_ref, rows_ref, picked, outs)
    for copy in copies:
        copy.wait()


def start_gather(source, row_list, part_list, count, tiles, first, kept, make_rows):
    indices = row_list.shape[0]
    columns = LANES // PACK
    outs = [vmem_out((columns, indices // count), BF16)] * count
    outs.append(vmem_out((kept, *tiles.shape[1:]), tiles.dtype))
    if make_rows:
        outs.append(vmem_out((source.shape[1] // PACK, LANES), F32))
        outs.append(vmem_out(source.shape, source.dtype))
    source = in_hbm(source) if make_rows else in_vmem(source)
    return pl.pallas_call(
        functools.partial(start_kernel, count, first, make_rows),
        out_shape=outs,
        in_specs=[SMEM, VMEM, HBM if make_rows else VMEM, HBM],
        out_specs=[VMEM] * len(outs),
        scratch_shapes=[pltpu.VMEM((indices, LANES), F32), pltpu.SemaphoreType.DMA((COPIES + 1,))],
        compiler_params=PARAMS,
        cost_estimate=CHEAP,
        name="start_gather",
    )(row_list, in_vmem(part_list), source, in_hbm(tiles))


def own_slots(block_ref, tiles_ref, own_ref):
    tile_size = tiles_ref.shape[1]
    for t in range(tiles_ref.shape[0]):
        at = slice(t * tile_size, (t + 1) * tile_size)
        own_ref[:, at] = jnp.dot(block_ref[:, at], tiles_ref[t], preferred_element_type=F32)


def order_slots(src_ref, dst_ref, count_ref, order_ref, first):
    rest = order_ref.shape[0] // 4
    used = jnp.minimum(count_ref[0] - first, rest)

    def place(i, placed):
        src = src_ref[first + i]
        local = src < first
        at = jnp.where(local, placed, used - 1 - (i - placed))
        order_ref[at] = i
        order_ref[rest + at] = jnp.where(local, src, src - first)
        order_ref[2 * rest + at] = dst_ref[first + i]
        return placed + local.astype(jnp.int32)

    order_ref[3 * rest] = lax.fori_loop(0, used, place, jnp.int32(0))
    order_ref[3 * rest + 1] = used


def add_slots(order_ref, start, stop, source, tiles_ref, total):
    rest = order_ref.shape[0] // 4
    tile_size = tiles_ref.shape[1]
    columns = source.shape[0]
    spare = total.shape[1] // tile_size - 1
    zero = jnp.zeros((columns, tile_size), BF16)

    def tile_of(index):
        return pl.ds(pl.multiple_of(index * tile_size, tile_size), tile_size)

    def chunk(base, size, whole):
        slots = []
        for u in range(size):
            at = base + u
            if whole:
                slots.append([order_ref[k * rest + at] for k in range(3)])
            else:
                there = at < stop
                at = jnp.minimum(at, rest - 1)
                other = (0, 0, spare)
                slots.append([jnp.where(there, order_ref[k * rest + at], other[k]) for k in range(3)])
        terms = []
        for u in range(0, size, 2):
            (slot_a, src_a, _), (slot_b, src_b, _) = slots[u : u + 2]
            pair = jnp.concatenate(
                [
                    jnp.concatenate([source[:, tile_of(src_a)], zero], axis=1),
                    jnp.concatenate([zero, source[:, tile_of(src_b)]], axis=1),
                ],
                axis=0,
            )
            weights = jnp.concatenate([tiles_ref[slot_a], tiles_ref[slot_b]], axis=0)
            both = jnp.dot(pair, weights, preferred_element_type=F32)
            terms += [both[:columns], both[columns:]]
        for (_, _, dst), term in zip(slots, terms):
            total[:, tile_of(dst)] += term

    def large(i, carry):
        chunk(start + i * LARGE, LARGE, True)
        return carry

    wholes = (stop - start) // LARGE
    lax.fori_loop(0, wholes, large, 0)
    after = start + wholes * LARGE

    def small(i, carry):
        chunk(after + i * SMALL, SMALL, False)
        return carry

    lax.fori_loop(0, (stop - after + SMALL - 1) // SMALL, small, 0)


def local_slots(order_ref, block_ref, own_tiles, rest_tiles, own_ref):
    rest = order_ref.shape[0] // 4
    own_slots(block_ref, own_tiles, own_ref)
    states = block_ref.shape[1]
    own_ref[:, states:] = jnp.zeros((own_ref.shape[0], own_ref.shape[1] - states), F32)
    add_slots(order_ref, 0, order_ref[3 * rest], block_ref, rest_tiles, own_ref)


def first_own_kernel(src_ref, dst_ref, count_ref, block_ref, own_tiles, rest_tiles, own_ref, order_ref):
    order_slots(src_ref, dst_ref, count_ref, order_ref, own_tiles.shape[0])
    local_slots(order_ref, block_ref, own_tiles, rest_tiles, own_ref)


def own_shape(columns, tiles):
    count, tile_size, _ = tiles.shape
    return vmem_out((columns, (count + 1) * tile_size), F32)


def first_own(src, dst, count, block, own_tiles, rest_tiles):
    return pl.pallas_call(
        first_own_kernel,
        out_shape=[
            own_shape(block.shape[0], own_tiles),
            jax.ShapeDtypeStruct((4 * rest_tiles.shape[0],), jnp.int32),
        ],
        in_specs=[SMEM] * 3 + [VMEM] * 3,
        out_specs=[VMEM, SMEM],
        compiler_params=PARAMS,
        cost_estimate=CHEAP,
        name="first_own",
    )(src, dst, count, in_vmem(block), in_vmem(own_tiles), in_vmem(rest_tiles))


def later_own_kernel(total_states, order_ref, *refs):
    grams, (stacked, own_tiles, rest_tiles) = refs[:4], refs[4:7]
    matrix_ref, own_ref, block_ref = refs[7:]
    matrix = apply_matrix(inverse_factor(gram_of([r[...] for r in grams], total_states)))
    matrix_ref[...] = matrix
    for c in range(0, block_ref.shape[1], CHUNK):
        block_ref[:, c : c + CHUNK] = applied(matrix, stacked[:, c : c + CHUNK]).astype(BF16)
    local_slots(order_ref, block_ref, own_tiles, rest_tiles, own_ref)


def later_own(order, grams, stacked, own_tiles, rest_tiles, total_states):
    columns, states = stacked.shape[0] // 3, stacked.shape[1]
    operands = [*grams, stacked, own_tiles, rest_tiles]
    return pl.pallas_call(
        functools.partial(later_own_kernel, total_states),
        out_shape=[vmem_out((3 * columns, 3 * columns), BF16), own_shape(columns, own_tiles)],
        in_specs=[SMEM] + [VMEM] * len(operands),
        out_specs=[VMEM] * 2,
        scratch_shapes=[pltpu.VMEM((columns, states), BF16)],
        compiler_params=PARAMS,
        cost_estimate=CHEAP,
        name="later_own",
    )(order, *[in_vmem(x) for x in operands])


def product_kernel(colours, with_rows, order_ref, own_ref, *refs):
    ghosts, refs = refs[:colours], refs[colours:]
    matrix_ref = None
    if ghosts[0].dtype == F32:
        matrix_ref, refs = refs[0], refs[1:]
    tiles_ref, stacked_ref, gram_ref, *refs = refs
    if with_rows:
        rows_ref, *refs = refs
    source, total = refs
    columns, states = stacked_ref.shape[0] // 3, stacked_ref.shape[1]
    rest = order_ref.shape[0] // 4

    width = ghosts[0].shape[1]
    for n, ghost in enumerate(ghosts):
        at = (len(ghosts) - 1 - n) * width
        value = ghost[...]
        if matrix_ref is not None:
            value = applied(matrix_ref[...], stack3(value)).astype(BF16)
        source[:, at : at + width] = value
    total[...] = own_ref[...]
    add_slots(order_ref, order_ref[3 * rest], order_ref[3 * rest + 1], source, tiles_ref, total)

    gram = jnp.zeros((3 * columns, 3 * columns), F32)
    for c in range(0, states, CHUNK):
        part = stack3(total[:, c : c + CHUNK])
        stacked_ref[:, c : c + CHUNK] = part
        gram += lax.dot_general(part, part, (((1,), (1,)), ((), ())), preferred_element_type=F32)
    blocks = [
        gram[a * columns : (a + 1) * columns, b * columns : (b + 1) * columns]
        for a in range(3)
        for b in range(3)
    ]
    small = blocks[8] + (blocks[5] + blocks[7])
    middle = blocks[4] + (blocks[2] + blocks[6])
    gram_ref[...] = packed(blocks[0] + ((blocks[1] + blocks[3]) + (middle + small)))
    if with_rows:
        transposed_into(total, rows_ref)


def product(order, own, ghosts, matrix, tiles, with_rows):
    tile_size = tiles.shape[1]
    columns, states = own.shape[0], own.shape[1] - tile_size
    outs = [
        vmem_out((3 * columns, states), BF16),
        vmem_out((columns * columns // LANES, LANES), F32),
    ]
    if with_rows:
        outs.append(vmem_out((states // PACK, LANES), F32))
    operands = [own, *ghosts[::-1]] + ([] if matrix is None else [matrix]) + [tiles]
    width = sum(g.shape[1] for g in ghosts)
    return pl.pallas_call(
        functools.partial(product_kernel, len(ghosts), with_rows),
        out_shape=outs,
        in_specs=[SMEM] + [VMEM] * len(operands),
        out_specs=[VMEM] * len(outs),
        scratch_shapes=[pltpu.VMEM((columns, width), BF16), pltpu.VMEM(own.shape, F32)],
        compiler_params=PARAMS,
        cost_estimate=CHEAP,
        name="product",
    )(order, *[in_vmem(x) for x in operands])


def final_kernel(total_states, *refs):
    grams, stacked, out_ref, ready, sems = refs[:4], *refs[4:]
    matrix = apply_matrix(inverse_factor(gram_of([r[...] for r in grams], total_states)))
    copies = []
    for n, c in enumerate(range(0, out_ref.shape[1], CHUNK)):
        at = pl.ds(c, CHUNK)
        ready[:, at] = applied(matrix, stacked[:, at])
        copies.append(pltpu.make_async_copy(ready.at[:, at], out_ref.at[:, at], sems.at[n]))
        copies[-1].start()
    for copy in copies:
        copy.wait()


def final(grams, stacked, total_states):
    columns, states = stacked.shape[0] // 3, stacked.shape[1]
    return pl.pallas_call(
        functools.partial(final_kernel, total_states),
        out_shape=jax.ShapeDtypeStruct((columns, states), F32),
        in_specs=[VMEM] * 5,
        out_specs=HBM,
        scratch_shapes=[
            pltpu.VMEM((columns, states), F32),
            pltpu.SemaphoreType.DMA((states // CHUNK,)),
        ],
        compiler_params=PARAMS,
        cost_estimate=CHEAP,
        name="final",
    )(*[in_vmem(g) for g in grams], in_vmem(stacked))


def dom_rounds(size):
    rounds, step = [], 1
    while step < size:
        span = min(4, size // step)
        rounds.append([step * k for k in range(1, span)])
        step *= span
    return rounds[::-1]


def paired_sum(parts):
    return (parts[0] + parts[1]) + (parts[2] + parts[3])


def gram_round(gram, masks):
    parts = [gram] + [swapped(gram, mask) for mask in masks]
    return parts + [jnp.zeros_like(gram)] * (4 - len(parts))


def on_device(start_block, tiles, tile_src, tile_dst, slot_count, send_rows):
    size = lax.axis_size("dom")
    masks = [1, 2, 4, 1 << (size.bit_length() - 2)]
    columns, states = start_block.shape
    total_states = states * size
    rounds = dom_rounds(size)
    lists = send_rows[0]
    pack_states = PACK * LANES
    row_lists = lists // pack_states * LANES + lists % LANES
    part_lists = lists // LANES % PACK
    far = (3, 2)
    near = (1, 0)

    def lists_of(colours):
        rows = jnp.concatenate([row_lists[c] for c in colours])
        parts = jnp.concatenate([part_lists[c] for c in colours]).reshape(-1, LANES)
        return rows, parts

    listed = [lists_of(far), lists_of(near)]

    def sent(ghosts, colours, picked):
        for colour, x in zip(colours, picked):
            ghosts[colour] = swapped(x, masks[colour])

    own_count = states // tiles.shape[1]
    ghosts = [None] * len(masks)
    *picked, rest_tiles, start_rows, block = start_gather(
        start_block, *listed[0], len(far), tiles, own_count, tiles.shape[0] - own_count, True
    )
    sent(ghosts, far, picked)
    *picked, own_tiles = start_gather(
        start_rows, *listed[1], len(near), tiles, 0, own_count, False
    )
    sent(ghosts, near, picked)
    matrix = None
    own, order = first_own(tile_src, tile_dst, slot_count, block, own_tiles, rest_tiles)
    for turn in range(ITERS):
        last = turn == ITERS - 1
        stacked, gram, *rows = product(order, own, ghosts, matrix, rest_tiles, not last)
        for masks_now in rounds[:-1]:
            gram = paired_sum(gram_round(gram, masks_now))
        if last:
            return final(gram_round(gram, rounds[-1]), stacked, total_states)
        ghosts = [None] * len(masks)
        picked = gather_colours(rows[0], *listed[0], len(far))
        gram, *picked = lax.optimization_barrier((gram, *picked))
        parts = gram_round(gram, rounds[-1])
        sent(ghosts, far, picked)
        near_rows, *parts = lax.optimization_barrier((rows[0], *parts))
        sent(ghosts, near, gather_colours(near_rows, *listed[1], len(near)))
        matrix, own = later_own(order, parts, stacked, own_tiles, rest_tiles, total_states)


def solution(mesh):
    return jax.shard_map(
        on_device,
        mesh=mesh,
        in_specs=(
            P(None, ("groups", "dom")),
            P(("groups", "dom"), None, None),
            P(("groups", "dom")),
            P(("groups", "dom")),
            P(("groups", "dom")),
            P(("groups", "dom"), None, None),
        ),
        out_specs=P(None, ("groups", "dom")),
        check_vma=False,
    )
```

```python
import functools

import jax
import jax.numpy as jnp
from jax import lax
from jax.experimental import pallas as pl
from jax.experimental.pallas import tpu as pltpu
from jax.sharding import PartitionSpec as P

ITERS = 3
LANES = 128
PACK = 4
CHUNK = 1024
SUBLANES = 8
STEP = 8
COPIES = 8
GROUP = 128
F32 = jnp.float32
BF16 = jnp.bfloat16
VMEM = pl.BlockSpec(memory_space=pltpu.VMEM)
SMEM = pl.BlockSpec(memory_space=pltpu.SMEM)
HBM = pl.BlockSpec(memory_space=pltpu.HBM)
CHEAP = pl.CostEstimate(flops=0, bytes_accessed=1024, transcendentals=0)
PARAMS = pltpu.CompilerParams(vmem_limit_bytes=32 << 20)


def in_vmem(x):
    return pltpu.with_memory_space_constraint(x, pltpu.VMEM)


def in_hbm(x):
    return pltpu.with_memory_space_constraint(x, pltpu.HBM)


def vmem_out(shape, dtype):
    return pltpu.VMEM(shape, dtype)


def swapped(x, mask):
    size = lax.axis_size("dom")
    return lax.ppermute(x, "dom", [(i, i ^ mask) for i in range(size)])


def split3(x):
    high = x.astype(BF16)
    rest = x - high.astype(F32)
    mid = rest.astype(BF16)
    low = (rest - mid.astype(F32)).astype(BF16)
    return high, mid, low


def stack3(x):
    return jnp.concatenate(split3(x), axis=0)


def inverse_factor(gram):
    n = gram.shape[0]
    row = lax.broadcasted_iota(jnp.int32, (n, n), 0)
    col = lax.broadcasted_iota(jnp.int32, (n, n), 1)
    eye = (row == col).astype(F32)
    both = jnp.concatenate([gram, eye, jnp.zeros((n, LANES - 2 * n), F32)], axis=1)
    full = (SUBLANES, LANES)
    parts = [both[q : q + SUBLANES] for q in range(0, n, SUBLANES)]
    sub = lax.broadcasted_iota(jnp.int32, full, 0)
    scales = [jnp.zeros(full, F32) for _ in parts]
    for j in range(0, n, STEP):
        home, at = j // SUBLANES, j % SUBLANES
        live = range(home, len(parts))
        cols = [
            {q: jnp.broadcast_to(parts[q][:, j + a : j + a + 1], full) for q in live}
            for a in range(STEP)
        ]
        rows = [jnp.broadcast_to(parts[home][at + a : at + a + 1], full) for a in range(STEP)]
        entry = {
            (a, b): jnp.broadcast_to(cols[b][home][at + a : at + a + 1], full)
            for a in range(STEP)
            for b in range(a + 1)
        }
        for a in range(STEP):
            over = 1.0 / entry[a, a]
            ratio = {c: entry[c, a] * over for c in range(a + 1, STEP)}
            for c in range(a + 1, STEP):
                for d in range(a + 1, c + 1):
                    entry[c, d] = entry[c, d] - ratio[c] * entry[d, a]
            for c in range(a + 1, STEP):
                rows[c] = rows[c] - ratio[c] * rows[a]
                for q in live:
                    cols[c][q] = cols[c][q] - ratio[c] * cols[a][q]
            root = 1.0 / jnp.sqrt(entry[a, a])
            scales[home] = jnp.where(sub == at + a, root, scales[home])
            for q in live:
                factor = cols[a][q] * over
                if q == home:
                    factor = jnp.where(sub > at + a, factor, 0.0)
                parts[q] = parts[q] - factor * rows[a]
    done = jnp.concatenate([p * s for p, s in zip(parts, scales)], axis=0)
    return done[:, n : 2 * n]


def apply_matrix(inverse):
    high, mid, low = (t.astype(F32) for t in split3(inverse))
    zero = jnp.zeros_like(high)
    full = jnp.concatenate(
        [
            jnp.concatenate([high, high, high], axis=1),
            jnp.concatenate([mid, mid, zero], axis=1),
            jnp.concatenate([low, zero, zero], axis=1),
        ],
        axis=0,
    )
    return full.astype(BF16)


def applied(matrix, stacked):
    n = matrix.shape[0] // 3
    terms = jnp.dot(matrix, stacked, preferred_element_type=F32)
    return terms[:n] + (terms[n : 2 * n] + terms[2 * n :])


def packed(square):
    n = square.shape[0]
    count = LANES // n
    step = n // count
    return jnp.concatenate([square[q * step : (q + 1) * step] for q in range(count)], axis=1)


def unpacked(wide):
    step = wide.shape[0]
    n = LANES // PACK
    count = n // step
    return jnp.concatenate([wide[:, q * n : (q + 1) * n] for q in range(count)], axis=0)


def gram_of(parts, total_states):
    while len(parts) > 1:
        parts = [a + b for a, b in zip(parts[::2], parts[1::2])] + parts[len(parts) // 2 * 2 :]
    return unpacked(parts[0]) / total_states


def transposed_into(source, rows_ref):
    for g in range(rows_ref.shape[0] // LANES):
        pieces = [
            source[:, (PACK * g + b) * LANES : (PACK * g + b + 1) * LANES].astype(F32)
            for b in range(PACK)
        ]
        rows_ref[g * LANES : (g + 1) * LANES, :] = jnp.concatenate(pieces, axis=0).T


def gathered_into(unroll, row_ref, part_ref, rows_ref, picked, outs):
    count = picked.shape[0]
    columns = outs[0].shape[0]

    def pick(i, carry):
        for u in range(unroll):
            m = i * unroll + u
            picked[pl.ds(m, 1), :] = rows_ref[pl.ds(row_ref[m], 1), :]
        return carry

    lax.fori_loop(0, count // unroll, pick, 0)
    tiles_out = outs[0].shape[1] // LANES
    for g in range(count // LANES):
        y = picked[g * LANES : (g + 1) * LANES, :].T
        part = jnp.broadcast_to(part_ref[g : g + 1, :], (columns, LANES))
        value = y[:columns]
        for b in range(1, PACK):
            value = jnp.where(part == b, y[b * columns : (b + 1) * columns], value)
        out, t = outs[g // tiles_out], g % tiles_out
        out[:, t * LANES : (t + 1) * LANES] = value.astype(out.dtype)


def gather_kernel(row_ref, part_ref, rows_ref, *rest):
    gathered_into(64, row_ref, part_ref, rows_ref, rest[-1], rest[:-1])


def gather_colours(rows, row_list, part_list, count):
    indices = row_list.shape[0]
    columns = LANES // PACK
    return pl.pallas_call(
        gather_kernel,
        out_shape=[vmem_out((columns, indices // count), F32)] * count,
        in_specs=[SMEM, VMEM, VMEM],
        out_specs=[VMEM] * count,
        scratch_shapes=[pltpu.VMEM((indices, LANES), F32)],
        compiler_params=PARAMS,
        cost_estimate=CHEAP,
        name="gather_rows",
    )(row_list, in_vmem(part_list), in_vmem(rows))


def start_kernel(count, first, make_rows, row_ref, part_ref, source_ref, tiles_ref, *refs):
    outs, kept_ref, refs = refs[:count], refs[count], refs[count + 1 :]
    picked, sems = refs[-2:]
    size = kept_ref.shape[0] // COPIES
    copies = [
        pltpu.make_async_copy(
            tiles_ref.at[pl.ds(first + c * size, size)],
            kept_ref.at[pl.ds(c * size, size)],
            sems.at[c],
        )
        for c in range(COPIES)
    ]
    if make_rows:
        block_ref = refs[1]
        block_copy = pltpu.make_async_copy(source_ref, block_ref, sems.at[COPIES])
        block_copy.start()
    for copy in copies:
        copy.start()
    if make_rows:
        block_copy.wait()
    rows_ref = source_ref
    if make_rows:
        rows_ref = refs[0]
        transposed_into(block_ref, rows_ref)
    gathered_into(64, row_ref, part_ref, rows_ref, picked, outs)
    for copy in copies:
        copy.wait()


def start_gather(source, row_list, part_list, count, tiles, first, kept, make_rows):
    indices = row_list.shape[0]
    columns = LANES // PACK
    outs = [vmem_out((columns, indices // count), BF16)] * count
    outs.append(vmem_out((kept, *tiles.shape[1:]), tiles.dtype))
    if make_rows:
        outs.append(vmem_out((source.shape[1] // PACK, LANES), F32))
        outs.append(vmem_out(source.shape, source.dtype))
    source = in_hbm(source) if make_rows else in_vmem(source)
    return pl.pallas_call(
        functools.partial(start_kernel, count, first, make_rows),
        out_shape=outs,
        in_specs=[SMEM, VMEM, HBM if make_rows else VMEM, HBM],
        out_specs=[VMEM] * len(outs),
        scratch_shapes=[pltpu.VMEM((indices, LANES), F32), pltpu.SemaphoreType.DMA((COPIES + 1,))],
        compiler_params=PARAMS,
        cost_estimate=CHEAP,
        name="start_gather",
    )(row_list, in_vmem(part_list), source, in_hbm(tiles))


def own_slots(block_ref, tiles_ref, own_ref):
    tile_size = tiles_ref.shape[1]
    for t in range(own_ref.shape[1] // tile_size):
        at = slice(t * tile_size, (t + 1) * tile_size)
        own_ref[:, at] = jnp.dot(block_ref[:, at], tiles_ref[t], preferred_element_type=F32)


def first_own_kernel(block_ref, tiles_ref, own_ref):
    own_slots(block_ref, tiles_ref, own_ref)


def first_own(block, tiles):
    return pl.pallas_call(
        first_own_kernel,
        out_shape=vmem_out(block.shape, F32),
        in_specs=[VMEM] * 2,
        out_specs=VMEM,
        compiler_params=PARAMS,
        cost_estimate=CHEAP,
        name="first_own",
    )(in_vmem(block), in_vmem(tiles))


def later_own_kernel(total_states, *refs):
    grams, stacked, tiles_ref = refs[:4], refs[4], refs[5]
    block_ref, matrix_ref, own_ref = refs[6:]
    matrix = apply_matrix(inverse_factor(gram_of([r[...] for r in grams], total_states)))
    matrix_ref[...] = matrix
    for c in range(0, block_ref.shape[1], CHUNK):
        block_ref[:, c : c + CHUNK] = applied(matrix, stacked[:, c : c + CHUNK]).astype(BF16)
    own_slots(block_ref, tiles_ref, own_ref)


def later_own(grams, stacked, tiles, total_states):
    columns, states = stacked.shape[0] // 3, stacked.shape[1]
    return pl.pallas_call(
        functools.partial(later_own_kernel, total_states),
        out_shape=[
            vmem_out((columns, states), BF16),
            vmem_out((3 * columns, 3 * columns), BF16),
            vmem_out((columns, states), F32),
        ],
        in_specs=[VMEM] * 6,
        out_specs=[VMEM] * 3,
        compiler_params=PARAMS,
        cost_estimate=CHEAP,
        name="later_own",
    )(*[in_vmem(g) for g in grams], in_vmem(stacked), in_vmem(tiles))


def product_kernel(colours, group, with_rows, *refs):
    src_ref, dst_ref, count_ref, block_ref, own_ref = refs[:5]
    ghosts, refs = refs[5 : 5 + colours], refs[5 + colours :]
    matrix_ref = None
    if ghosts[0].dtype == F32:
        matrix_ref, refs = refs[0], refs[1:]
    tiles_ref, refs = refs[0], refs[1:]
    stacked_ref, gram_ref, refs = refs[0], refs[1], refs[2:]
    if with_rows:
        rows_ref, refs = refs[0], refs[1:]
    source, total = refs
    columns, states = block_ref.shape
    tile_size = tiles_ref.shape[1]
    first = states // tile_size
    live = count_ref[0]

    source[:, :states] = block_ref[...]
    width = ghosts[0].shape[1]
    for n, ghost in enumerate(ghosts):
        at = states + (len(ghosts) - 1 - n) * width
        value = ghost[...]
        if matrix_ref is not None:
            value = applied(matrix_ref[...], stack3(value)).astype(BF16)
        source[:, at : at + width] = value
    at = states + len(ghosts) * width
    source[:, at:] = jnp.zeros((columns, tile_size), BF16)
    nothing = at // tile_size
    total[...] = own_ref[...]

    def tile_at(s):
        index = jnp.where(s < live, src_ref[s], nothing)
        return source[:, pl.ds(pl.multiple_of(index * tile_size, tile_size), tile_size)]

    zero = jnp.zeros((columns, tile_size), BF16)

    def body(i, carry):
        base = first + i * group
        terms = []
        for u in range(0, group, 2):
            pair = jnp.concatenate(
                [
                    jnp.concatenate([tile_at(base + u), zero], axis=1),
                    jnp.concatenate([zero, tile_at(base + u + 1)], axis=1),
                ],
                axis=0,
            )
            weights = tiles_ref[pl.ds(base + u - first, 2)].reshape(2 * tile_size, tile_size)
            both = jnp.dot(pair, weights, preferred_element_type=F32)
            terms += [both[:columns], both[columns:]]
        for u in range(group):
            where = pl.multiple_of(dst_ref[base + u] * tile_size, tile_size)
            total[:, pl.ds(where, tile_size)] += terms[u]
        return carry

    lax.fori_loop(0, (live - first + group - 1) // group, body, 0)

    gram = jnp.zeros((3 * columns, 3 * columns), F32)
    for c in range(0, states, CHUNK):
        part = stack3(total[:, c : c + CHUNK])
        stacked_ref[:, c : c + CHUNK] = part
        gram += lax.dot_general(part, part, (((1,), (1,)), ((), ())), preferred_element_type=F32)
    blocks = [
        gram[a * columns : (a + 1) * columns, b * columns : (b + 1) * columns]
        for a in range(3)
        for b in range(3)
    ]
    small = blocks[8] + (blocks[5] + blocks[7])
    middle = blocks[4] + (blocks[2] + blocks[6])
    gram = packed(blocks[0] + ((blocks[1] + blocks[3]) + (middle + small)))
    if with_rows:
        gram_ref[...] = gram
    else:
        for n in range(gram_ref.shape[0]):
            gram_ref[n] = gram
    if with_rows:
        transposed_into(total, rows_ref)


def product(src, dst, count, block, own, ghosts, matrix, tiles, with_rows):
    columns, states = block.shape
    rest, tile_size, _ = tiles.shape
    group = GROUP
    while rest % group:
        group //= 2
    gram_shape = (columns * columns // LANES, LANES)
    if not with_rows:
        gram_shape = (lax.axis_size("dom"), *gram_shape)
    outs = [vmem_out((3 * columns, states), BF16), vmem_out(gram_shape, F32)]
    if with_rows:
        outs.append(vmem_out((states // PACK, LANES), F32))
    operands = [block, own, *ghosts[::-1]] + ([] if matrix is None else [matrix]) + [tiles]
    width = states + sum(g.shape[1] for g in ghosts) + tile_size
    return pl.pallas_call(
        functools.partial(product_kernel, len(ghosts), group, with_rows),
        out_shape=outs,
        in_specs=[SMEM] * 3 + [VMEM] * len(operands),
        out_specs=[VMEM] * len(outs),
        scratch_shapes=[pltpu.VMEM((columns, width), BF16), pltpu.VMEM((columns, states), F32)],
        compiler_params=PARAMS,
        cost_estimate=CHEAP,
        name="product",
    )(src, dst, count, *[in_vmem(x) for x in operands])


def final_kernel(total_states, *refs):
    grams, stacked, out_ref, ready, sems = refs
    parts = [grams[n] for n in range(grams.shape[0])]
    matrix = apply_matrix(inverse_factor(gram_of(parts, total_states)))
    copies = []
    for n, c in enumerate(range(0, out_ref.shape[1], CHUNK)):
        at = pl.ds(c, CHUNK)
        ready[:, at] = applied(matrix, stacked[:, at])
        copies.append(pltpu.make_async_copy(ready.at[:, at], out_ref.at[:, at], sems.at[n]))
        copies[-1].start()
    for copy in copies:
        copy.wait()


def final(grams, stacked, total_states):
    columns, states = stacked.shape[0] // 3, stacked.shape[1]
    return pl.pallas_call(
        functools.partial(final_kernel, total_states),
        out_shape=jax.ShapeDtypeStruct((columns, states), F32),
        in_specs=[VMEM] * 2,
        out_specs=HBM,
        scratch_shapes=[
            pltpu.VMEM((columns, states), F32),
            pltpu.SemaphoreType.DMA((states // CHUNK,)),
        ],
        compiler_params=PARAMS,
        cost_estimate=CHEAP,
        name="final",
    )(in_vmem(grams), in_vmem(stacked))


def dom_rounds(size):
    rounds, step = [], 1
    while step < size:
        span = min(4, size // step)
        rounds.append([step * k for k in range(1, span)])
        step *= span
    return rounds[::-1]


def paired_sum(parts):
    return (parts[0] + parts[1]) + (parts[2] + parts[3])


def gram_round(gram, masks):
    parts = [gram] + [swapped(gram, mask) for mask in masks]
    return parts + [jnp.zeros_like(gram)] * (4 - len(parts))


def on_device(start_block, tiles, tile_src, tile_dst, slot_count, send_rows):
    size = lax.axis_size("dom")
    masks = [1, 2, 4, 1 << (size.bit_length() - 2)]
    columns, states = start_block.shape
    total_states = states * size
    rounds = dom_rounds(size)
    lists = send_rows[0]
    pack_states = PACK * LANES
    row_lists = lists // pack_states * LANES + lists % LANES
    part_lists = lists // LANES % PACK
    far = (3, 2)
    near = (1, 0)

    def lists_of(colours):
        rows = jnp.concatenate([row_lists[c] for c in colours])
        parts = jnp.concatenate([part_lists[c] for c in colours]).reshape(-1, LANES)
        return rows, parts

    listed = [lists_of(far), lists_of(near)]

    def sent(ghosts, colours, picked):
        for colour, x in zip(colours, picked):
            ghosts[colour] = swapped(x, masks[colour])

    own_count = states // tiles.shape[1]
    ghosts = [None] * len(masks)
    *picked, rest_tiles, start_rows, block = start_gather(
        start_block, *listed[0], len(far), tiles, own_count, tiles.shape[0] - own_count, True
    )
    sent(ghosts, far, picked)
    *picked, own_tiles = start_gather(
        start_rows, *listed[1], len(near), tiles, 0, own_count, False
    )
    sent(ghosts, near, picked)
    matrix = None
    own = first_own(block, own_tiles)
    for turn in range(ITERS):
        last = turn == ITERS - 1
        stacked, gram, *rows = product(
            tile_src, tile_dst, slot_count, block, own, ghosts, matrix, rest_tiles, not last
        )
        if last:
            return final(lax.all_to_all(gram, "dom", 0, 0), stacked, total_states)
        for masks_now in rounds[:-1]:
            gram = paired_sum(gram_round(gram, masks_now))
        ghosts = [None] * len(masks)
        picked = gather_colours(rows[0], *listed[0], len(far))
        gram, *picked = lax.optimization_barrier((gram, *picked))
        parts = gram_round(gram, rounds[-1])
        sent(ghosts, far, picked)
        near_rows, *parts = lax.optimization_barrier((rows[0], *parts))
        sent(ghosts, near, gather_colours(near_rows, *listed[1], len(near)))
        block, matrix, own = later_own(parts, stacked, own_tiles, total_states)


def solution(mesh):
    return jax.shard_map(
        on_device,
        mesh=mesh,
        in_specs=(
            P(None, ("groups", "dom")),
            P(("groups", "dom"), None, None),
            P(("groups", "dom")),
            P(("groups", "dom")),
            P(("groups", "dom")),
            P(("groups", "dom"), None, None),
        ),
        out_specs=P(None, ("groups", "dom")),
        check_vma=False,
    )
```

```python
import functools

import jax
import jax.numpy as jnp
from jax import lax
from jax.experimental import pallas as pl
from jax.experimental.pallas import tpu as pltpu
from jax.sharding import PartitionSpec as P

ITERS = 3
LANES = 128
PACK = 4
CHUNK = 1024
SUBLANES = 8
STEP = 8
COPIES = 8
GROUP = 128
F32 = jnp.float32
BF16 = jnp.bfloat16
VMEM = pl.BlockSpec(memory_space=pltpu.VMEM)
SMEM = pl.BlockSpec(memory_space=pltpu.SMEM)
HBM = pl.BlockSpec(memory_space=pltpu.HBM)
CHEAP = pl.CostEstimate(flops=0, bytes_accessed=1024, transcendentals=0)
PARAMS = pltpu.CompilerParams(vmem_limit_bytes=32 << 20)


def in_vmem(x):
    return pltpu.with_memory_space_constraint(x, pltpu.VMEM)


def in_hbm(x):
    return pltpu.with_memory_space_constraint(x, pltpu.HBM)


def vmem_out(shape, dtype):
    return pltpu.VMEM(shape, dtype)


def swapped(x, mask):
    size = lax.axis_size("dom")
    return lax.ppermute(x, "dom", [(i, i ^ mask) for i in range(size)])


def split3(x):
    high = x.astype(BF16)
    rest = x - high.astype(F32)
    mid = rest.astype(BF16)
    low = (rest - mid.astype(F32)).astype(BF16)
    return high, mid, low


def stack3(x):
    return jnp.concatenate(split3(x), axis=0)


def inverse_factor(gram):
    n = gram.shape[0]
    row = lax.broadcasted_iota(jnp.int32, (n, n), 0)
    col = lax.broadcasted_iota(jnp.int32, (n, n), 1)
    eye = (row == col).astype(F32)
    both = jnp.concatenate([gram, eye, jnp.zeros((n, LANES - 2 * n), F32)], axis=1)
    full = (SUBLANES, LANES)
    parts = [both[q : q + SUBLANES] for q in range(0, n, SUBLANES)]
    sub = lax.broadcasted_iota(jnp.int32, full, 0)
    scales = [jnp.zeros(full, F32) for _ in parts]
    for j in range(0, n, STEP):
        home, at = j // SUBLANES, j % SUBLANES
        live = range(home, len(parts))
        cols = [
            {q: jnp.broadcast_to(parts[q][:, j + a : j + a + 1], full) for q in live}
            for a in range(STEP)
        ]
        rows = [jnp.broadcast_to(parts[home][at + a : at + a + 1], full) for a in range(STEP)]
        entry = {
            (a, b): jnp.broadcast_to(cols[b][home][at + a : at + a + 1], full)
            for a in range(STEP)
            for b in range(a + 1)
        }
        for a in range(STEP):
            over = 1.0 / entry[a, a]
            ratio = {c: entry[c, a] * over for c in range(a + 1, STEP)}
            for c in range(a + 1, STEP):
                for d in range(a + 1, c + 1):
                    entry[c, d] = entry[c, d] - ratio[c] * entry[d, a]
            for c in range(a + 1, STEP):
                rows[c] = rows[c] - ratio[c] * rows[a]
                for q in live:
                    cols[c][q] = cols[c][q] - ratio[c] * cols[a][q]
            root = 1.0 / jnp.sqrt(entry[a, a])
            scales[home] = jnp.where(sub == at + a, root, scales[home])
            for q in live:
                factor = cols[a][q] * over
                if q == home:
                    factor = jnp.where(sub > at + a, factor, 0.0)
                parts[q] = parts[q] - factor * rows[a]
    done = jnp.concatenate([p * s for p, s in zip(parts, scales)], axis=0)
    return done[:, n : 2 * n]


def apply_matrix(inverse):
    high, mid, low = (t.astype(F32) for t in split3(inverse))
    zero = jnp.zeros_like(high)
    full = jnp.concatenate(
        [
            jnp.concatenate([high, high, high], axis=1),
            jnp.concatenate([mid, mid, zero], axis=1),
            jnp.concatenate([low, zero, zero], axis=1),
        ],
        axis=0,
    )
    return full.astype(BF16)


def applied(matrix, stacked):
    n = matrix.shape[0] // 3
    terms = jnp.dot(matrix, stacked, preferred_element_type=F32)
    return terms[:n] + (terms[n : 2 * n] + terms[2 * n :])


def packed(square):
    n = square.shape[0]
    count = LANES // n
    step = n // count
    return jnp.concatenate([square[q * step : (q + 1) * step] for q in range(count)], axis=1)


def unpacked(wide):
    step = wide.shape[0]
    n = LANES // PACK
    count = n // step
    return jnp.concatenate([wide[:, q * n : (q + 1) * n] for q in range(count)], axis=0)


def gram_of(parts, total_states):
    return unpacked(paired_sum(parts)) / total_states


def transposed_into(source, rows_ref):
    for g in range(rows_ref.shape[0] // LANES):
        pieces = [
            source[:, (PACK * g + b) * LANES : (PACK * g + b + 1) * LANES].astype(F32)
            for b in range(PACK)
        ]
        rows_ref[g * LANES : (g + 1) * LANES, :] = jnp.concatenate(pieces, axis=0).T


def gathered_into(unroll, row_ref, part_ref, rows_ref, picked, outs):
    count = picked.shape[0]
    columns = outs[0].shape[0]

    def pick(i, carry):
        for u in range(unroll):
            m = i * unroll + u
            picked[pl.ds(m, 1), :] = rows_ref[pl.ds(row_ref[m], 1), :]
        return carry

    lax.fori_loop(0, count // unroll, pick, 0)
    tiles_out = outs[0].shape[1] // LANES
    for g in range(count // LANES):
        y = picked[g * LANES : (g + 1) * LANES, :].T
        part = jnp.broadcast_to(part_ref[g : g + 1, :], (columns, LANES))
        value = y[:columns]
        for b in range(1, PACK):
            value = jnp.where(part == b, y[b * columns : (b + 1) * columns], value)
        out, t = outs[g // tiles_out], g % tiles_out
        out[:, t * LANES : (t + 1) * LANES] = value.astype(out.dtype)


def gather_kernel(row_ref, part_ref, rows_ref, *rest):
    gathered_into(64, row_ref, part_ref, rows_ref, rest[-1], rest[:-1])


def gather_colours(rows, row_list, part_list, count):
    indices = row_list.shape[0]
    columns = LANES // PACK
    return pl.pallas_call(
        gather_kernel,
        out_shape=[vmem_out((columns, indices // count), F32)] * count,
        in_specs=[SMEM, VMEM, VMEM],
        out_specs=[VMEM] * count,
        scratch_shapes=[pltpu.VMEM((indices, LANES), F32)],
        compiler_params=PARAMS,
        cost_estimate=CHEAP,
        name="gather_rows",
    )(row_list, in_vmem(part_list), in_vmem(rows))


def start_kernel(count, first, make_rows, row_ref, part_ref, source_ref, tiles_ref, *refs):
    outs, kept_ref, refs = refs[:count], refs[count], refs[count + 1 :]
    picked, sems = refs[-2:]
    size = kept_ref.shape[0] // COPIES
    copies = [
        pltpu.make_async_copy(
            tiles_ref.at[pl.ds(first + c * size, size)],
            kept_ref.at[pl.ds(c * size, size)],
            sems.at[c],
        )
        for c in range(COPIES)
    ]
    if make_rows:
        block_ref = refs[1]
        block_copy = pltpu.make_async_copy(source_ref, block_ref, sems.at[COPIES])
        block_copy.start()
    for copy in copies:
        copy.start()
    if make_rows:
        block_copy.wait()
    rows_ref = source_ref
    if make_rows:
        rows_ref = refs[0]
        transposed_into(block_ref, rows_ref)
    gathered_into(64, row_ref, part_ref, rows_ref, picked, outs)
    for copy in copies:
        copy.wait()


def start_gather(source, row_list, part_list, count, tiles, first, kept, make_rows):
    indices = row_list.shape[0]
    columns = LANES // PACK
    outs = [vmem_out((columns, indices // count), BF16)] * count
    outs.append(vmem_out((kept, *tiles.shape[1:]), tiles.dtype))
    if make_rows:
        outs.append(vmem_out((source.shape[1] // PACK, LANES), F32))
        outs.append(vmem_out(source.shape, source.dtype))
    source = in_hbm(source) if make_rows else in_vmem(source)
    return pl.pallas_call(
        functools.partial(start_kernel, count, first, make_rows),
        out_shape=outs,
        in_specs=[SMEM, VMEM, HBM if make_rows else VMEM, HBM],
        out_specs=[VMEM] * len(outs),
        scratch_shapes=[pltpu.VMEM((indices, LANES), F32), pltpu.SemaphoreType.DMA((COPIES + 1,))],
        compiler_params=PARAMS,
        cost_estimate=CHEAP,
        name="start_gather",
    )(row_list, in_vmem(part_list), source, in_hbm(tiles))


def own_slots(block_ref, tiles_ref, own_ref):
    tile_size = tiles_ref.shape[1]
    for t in range(own_ref.shape[1] // tile_size):
        at = slice(t * tile_size, (t + 1) * tile_size)
        own_ref[:, at] = jnp.dot(block_ref[:, at], tiles_ref[t], preferred_element_type=F32)


def first_own_kernel(block_ref, tiles_ref, own_ref):
    own_slots(block_ref, tiles_ref, own_ref)


def first_own(block, tiles):
    return pl.pallas_call(
        first_own_kernel,
        out_shape=vmem_out(block.shape, F32),
        in_specs=[VMEM] * 2,
        out_specs=VMEM,
        compiler_params=PARAMS,
        cost_estimate=CHEAP,
        name="first_own",
    )(in_vmem(block), in_vmem(tiles))


def later_own_kernel(total_states, *refs):
    grams, stacked, tiles_ref = refs[:4], refs[4], refs[5]
    block_ref, matrix_ref, own_ref = refs[6:]
    matrix = apply_matrix(inverse_factor(gram_of([r[...] for r in grams], total_states)))
    matrix_ref[...] = matrix
    for c in range(0, block_ref.shape[1], CHUNK):
        block_ref[:, c : c + CHUNK] = applied(matrix, stacked[:, c : c + CHUNK]).astype(BF16)
    own_slots(block_ref, tiles_ref, own_ref)


def later_own(grams, stacked, tiles, total_states):
    columns, states = stacked.shape[0] // 3, stacked.shape[1]
    return pl.pallas_call(
        functools.partial(later_own_kernel, total_states),
        out_shape=[
            vmem_out((columns, states), BF16),
            vmem_out((3 * columns, 3 * columns), BF16),
            vmem_out((columns, states), F32),
        ],
        in_specs=[VMEM] * 6,
        out_specs=[VMEM] * 3,
        compiler_params=PARAMS,
        cost_estimate=CHEAP,
        name="later_own",
    )(*[in_vmem(g) for g in grams], in_vmem(stacked), in_vmem(tiles))


def product_kernel(colours, group, with_rows, *refs):
    src_ref, dst_ref, count_ref, block_ref, own_ref = refs[:5]
    ghosts, refs = refs[5 : 5 + colours], refs[5 + colours :]
    matrix_ref = None
    if ghosts[0].dtype == F32:
        matrix_ref, refs = refs[0], refs[1:]
    tiles_ref, refs = refs[0], refs[1:]
    stacked_ref, gram_ref, refs = refs[0], refs[1], refs[2:]
    if with_rows:
        rows_ref, refs = refs[0], refs[1:]
    source, total = refs
    columns, states = block_ref.shape
    tile_size = tiles_ref.shape[1]
    first = states // tile_size
    live = count_ref[0]

    source[:, :states] = block_ref[...]
    width = ghosts[0].shape[1]
    for n, ghost in enumerate(ghosts):
        at = states + (len(ghosts) - 1 - n) * width
        value = ghost[...]
        if matrix_ref is not None:
            value = applied(matrix_ref[...], stack3(value)).astype(BF16)
        source[:, at : at + width] = value
    at = states + len(ghosts) * width
    source[:, at:] = jnp.zeros((columns, tile_size), BF16)
    nothing = at // tile_size
    total[...] = own_ref[...]

    def tile_at(s):
        index = jnp.where(s < live, src_ref[s], nothing)
        return source[:, pl.ds(pl.multiple_of(index * tile_size, tile_size), tile_size)]

    zero = jnp.zeros((columns, tile_size), BF16)

    def body(i, carry):
        base = first + i * group
        terms = []
        for u in range(0, group, 2):
            pair = jnp.concatenate(
                [
                    jnp.concatenate([tile_at(base + u), zero], axis=1),
                    jnp.concatenate([zero, tile_at(base + u + 1)], axis=1),
                ],
                axis=0,
            )
            weights = tiles_ref[pl.ds(base + u - first, 2)].reshape(2 * tile_size, tile_size)
            both = jnp.dot(pair, weights, preferred_element_type=F32)
            terms += [both[:columns], both[columns:]]
        for u in range(group):
            where = pl.multiple_of(dst_ref[base + u] * tile_size, tile_size)
            total[:, pl.ds(where, tile_size)] += terms[u]
        return carry

    lax.fori_loop(0, (live - first + group - 1) // group, body, 0)

    gram = jnp.zeros((3 * columns, 3 * columns), F32)
    for c in range(0, states, CHUNK):
        part = stack3(total[:, c : c + CHUNK])
        stacked_ref[:, c : c + CHUNK] = part
        gram += lax.dot_general(part, part, (((1,), (1,)), ((), ())), preferred_element_type=F32)
    blocks = [
        gram[a * columns : (a + 1) * columns, b * columns : (b + 1) * columns]
        for a in range(3)
        for b in range(3)
    ]
    small = blocks[8] + (blocks[5] + blocks[7])
    middle = blocks[4] + (blocks[2] + blocks[6])
    gram_ref[...] = packed(blocks[0] + ((blocks[1] + blocks[3]) + (middle + small)))
    if with_rows:
        transposed_into(total, rows_ref)


def product(src, dst, count, block, own, ghosts, matrix, tiles, with_rows):
    columns, states = block.shape
    rest, tile_size, _ = tiles.shape
    group = GROUP
    while rest % group:
        group //= 2
    outs = [vmem_out((3 * columns, states), BF16), vmem_out((columns * columns // LANES, LANES), F32)]
    if with_rows:
        outs.append(vmem_out((states // PACK, LANES), F32))
    operands = [block, own, *ghosts[::-1]] + ([] if matrix is None else [matrix]) + [tiles]
    width = states + sum(g.shape[1] for g in ghosts) + tile_size
    return pl.pallas_call(
        functools.partial(product_kernel, len(ghosts), group, with_rows),
        out_shape=outs,
        in_specs=[SMEM] * 3 + [VMEM] * len(operands),
        out_specs=[VMEM] * len(outs),
        scratch_shapes=[pltpu.VMEM((columns, width), BF16), pltpu.VMEM((columns, states), F32)],
        compiler_params=PARAMS,
        cost_estimate=CHEAP,
        name="product",
    )(src, dst, count, *[in_vmem(x) for x in operands])


def final_kernel(total_states, *refs):
    grams, stacked, out_ref, ready, sems = refs[:4], *refs[4:]
    matrix = apply_matrix(inverse_factor(gram_of([r[...] for r in grams], total_states)))
    copies = []
    for n, c in enumerate(range(0, out_ref.shape[1], CHUNK)):
        at = pl.ds(c, CHUNK)
        ready[:, at] = applied(matrix, stacked[:, at])
        copies.append(pltpu.make_async_copy(ready.at[:, at], out_ref.at[:, at], sems.at[n]))
        copies[-1].start()
    for copy in copies:
        copy.wait()


def final(grams, stacked, total_states):
    columns, states = stacked.shape[0] // 3, stacked.shape[1]
    return pl.pallas_call(
        functools.partial(final_kernel, total_states),
        out_shape=jax.ShapeDtypeStruct((columns, states), F32),
        in_specs=[VMEM] * 5,
        out_specs=HBM,
        scratch_shapes=[
            pltpu.VMEM((columns, states), F32),
            pltpu.SemaphoreType.DMA((states // CHUNK,)),
        ],
        compiler_params=PARAMS,
        cost_estimate=CHEAP,
        name="final",
    )(*[in_vmem(g) for g in grams], in_vmem(stacked))


def dom_rounds(size):
    rounds, step = [], 1
    while step < size:
        span = min(4, size // step)
        rounds.append([step * k for k in range(1, span)])
        step *= span
    return rounds[::-1]


def paired_sum(parts):
    return (parts[0] + parts[1]) + (parts[2] + parts[3])


def gram_round(gram, masks):
    parts = [gram] + [swapped(gram, mask) for mask in masks]
    return parts + [jnp.zeros_like(gram)] * (4 - len(parts))


def on_device(start_block, tiles, tile_src, tile_dst, slot_count, send_rows):
    size = lax.axis_size("dom")
    masks = [1, 2, 4, 1 << (size.bit_length() - 2)]
    columns, states = start_block.shape
    total_states = states * size
    rounds = dom_rounds(size)
    lists = send_rows[0]
    pack_states = PACK * LANES
    row_lists = lists // pack_states * LANES + lists % LANES
    part_lists = lists // LANES % PACK
    far = (3, 2)
    near = (1, 0)

    def lists_of(colours):
        rows = jnp.concatenate([row_lists[c] for c in colours])
        parts = jnp.concatenate([part_lists[c] for c in colours]).reshape(-1, LANES)
        return rows, parts

    listed = [lists_of(far), lists_of(near)]

    def sent(ghosts, colours, picked):
        for colour, x in zip(colours, picked):
            ghosts[colour] = swapped(x, masks[colour])

    own_count = states // tiles.shape[1]
    ghosts = [None] * len(masks)
    *picked, rest_tiles, start_rows, block = start_gather(
        start_block, *listed[0], len(far), tiles, own_count, tiles.shape[0] - own_count, True
    )
    sent(ghosts, far, picked)
    *picked, own_tiles = start_gather(
        start_rows, *listed[1], len(near), tiles, 0, own_count, False
    )
    sent(ghosts, near, picked)
    matrix = None
    own = first_own(block, own_tiles)
    for turn in range(ITERS):
        last = turn == ITERS - 1
        stacked, gram, *rows = product(
            tile_src, tile_dst, slot_count, block, own, ghosts, matrix, rest_tiles, not last
        )
        for masks_now in rounds[:-1]:
            gram = paired_sum(gram_round(gram, masks_now))
        if last:
            return final(gram_round(gram, rounds[-1]), stacked, total_states)
        ghosts = [None] * len(masks)
        picked = gather_colours(rows[0], *listed[0], len(far))
        gram, *picked = lax.optimization_barrier((gram, *picked))
        parts = gram_round(gram, rounds[-1])
        sent(ghosts, far, picked)
        near_rows, *parts = lax.optimization_barrier((rows[0], *parts))
        sent(ghosts, near, gather_colours(near_rows, *listed[1], len(near)))
        block, matrix, own = later_own(parts, stacked, own_tiles, total_states)


def solution(mesh):
    return jax.shard_map(
        on_device,
        mesh=mesh,
        in_specs=(
            P(None, ("groups", "dom")),
            P(("groups", "dom"), None, None),
            P(("groups", "dom")),
            P(("groups", "dom")),
            P(("groups", "dom")),
            P(("groups", "dom"), None, None),
        ),
        out_specs=P(None, ("groups", "dom")),
        check_vma=False,
    )
```

```python
import functools

import jax
import jax.numpy as jnp
from jax import lax
from jax.experimental import pallas as pl
from jax.experimental.pallas import tpu as pltpu
from jax.sharding import PartitionSpec as P

ITERS = 3
LANES = 128
PACK = 4
CHUNK = 1024
SUBLANES = 8
STEP = 8
COPIES = 8
GROUP = 128
F32 = jnp.float32
BF16 = jnp.bfloat16
VMEM = pl.BlockSpec(memory_space=pltpu.VMEM)
SMEM = pl.BlockSpec(memory_space=pltpu.SMEM)
HBM = pl.BlockSpec(memory_space=pltpu.HBM)
CHEAP = pl.CostEstimate(flops=0, bytes_accessed=1024, transcendentals=0)
PARAMS = pltpu.CompilerParams(vmem_limit_bytes=32 << 20)


def in_vmem(x):
    return pltpu.with_memory_space_constraint(x, pltpu.VMEM)


def in_hbm(x):
    return pltpu.with_memory_space_constraint(x, pltpu.HBM)


def vmem_out(shape, dtype):
    return pltpu.VMEM(shape, dtype)


def swapped(x, mask):
    size = lax.axis_size("dom")
    return lax.ppermute(x, "dom", [(i, i ^ mask) for i in range(size)])


def split3(x):
    high = x.astype(BF16)
    rest = x - high.astype(F32)
    mid = rest.astype(BF16)
    low = (rest - mid.astype(F32)).astype(BF16)
    return high, mid, low


def stack3(x):
    return jnp.concatenate(split3(x), axis=0)


def inverse_factor(gram):
    n = gram.shape[0]
    row = lax.broadcasted_iota(jnp.int32, (n, n), 0)
    col = lax.broadcasted_iota(jnp.int32, (n, n), 1)
    eye = (row == col).astype(F32)
    both = jnp.concatenate([gram, eye, jnp.zeros((n, LANES - 2 * n), F32)], axis=1)
    full = (SUBLANES, LANES)
    parts = [both[q : q + SUBLANES] for q in range(0, n, SUBLANES)]
    sub = lax.broadcasted_iota(jnp.int32, full, 0)
    scales = [jnp.zeros(full, F32) for _ in parts]
    for j in range(0, n, STEP):
        home, at = j // SUBLANES, j % SUBLANES
        live = range(home, len(parts))
        cols = [
            {q: jnp.broadcast_to(parts[q][:, j + a : j + a + 1], full) for q in live}
            for a in range(STEP)
        ]
        rows = [jnp.broadcast_to(parts[home][at + a : at + a + 1], full) for a in range(STEP)]
        entry = {
            (a, b): jnp.broadcast_to(cols[b][home][at + a : at + a + 1], full)
            for a in range(STEP)
            for b in range(a + 1)
        }
        for a in range(STEP):
            over = 1.0 / entry[a, a]
            ratio = {c: entry[c, a] * over for c in range(a + 1, STEP)}
            for c in range(a + 1, STEP):
                for d in range(a + 1, c + 1):
                    entry[c, d] = entry[c, d] - ratio[c] * entry[d, a]
            for c in range(a + 1, STEP):
                rows[c] = rows[c] - ratio[c] * rows[a]
                for q in live:
                    cols[c][q] = cols[c][q] - ratio[c] * cols[a][q]
            root = 1.0 / jnp.sqrt(entry[a, a])
            scales[home] = jnp.where(sub == at + a, root, scales[home])
            for q in live:
                factor = cols[a][q] * over
                if q == home:
                    factor = jnp.where(sub > at + a, factor, 0.0)
                parts[q] = parts[q] - factor * rows[a]
    done = jnp.concatenate([p * s for p, s in zip(parts, scales)], axis=0)
    return done[:, n : 2 * n]


def apply_matrix(inverse):
    high, mid, low = (t.astype(F32) for t in split3(inverse))
    zero = jnp.zeros_like(high)
    full = jnp.concatenate(
        [
            jnp.concatenate([high, high, high], axis=1),
            jnp.concatenate([mid, mid, zero], axis=1),
            jnp.concatenate([low, zero, zero], axis=1),
        ],
        axis=0,
    )
    return full.astype(BF16)


def applied(matrix, stacked):
    n = matrix.shape[0] // 3
    terms = jnp.dot(matrix, stacked, preferred_element_type=F32)
    return terms[:n] + (terms[n : 2 * n] + terms[2 * n :])


def packed(square):
    n = square.shape[0]
    count = LANES // n
    step = n // count
    return jnp.concatenate([square[q * step : (q + 1) * step] for q in range(count)], axis=1)


def unpacked(wide):
    step = wide.shape[0]
    n = LANES // PACK
    count = n // step
    return jnp.concatenate([wide[:, q * n : (q + 1) * n] for q in range(count)], axis=0)


def gram_of(parts, total_states):
    return unpacked(paired_sum(parts)) / total_states


def transposed_into(source, rows_ref):
    for g in range(rows_ref.shape[0] // LANES):
        pieces = [
            source[:, (PACK * g + b) * LANES : (PACK * g + b + 1) * LANES].astype(F32)
            for b in range(PACK)
        ]
        rows_ref[g * LANES : (g + 1) * LANES, :] = jnp.concatenate(pieces, axis=0).T


def gathered_into(unroll, row_ref, part_ref, rows_ref, picked, outs):
    count = picked.shape[0]
    columns = outs[0].shape[0]

    def pick(i, carry):
        for u in range(unroll):
            m = i * unroll + u
            picked[pl.ds(m, 1), :] = rows_ref[pl.ds(row_ref[m], 1), :]
        return carry

    lax.fori_loop(0, count // unroll, pick, 0)
    tiles_out = outs[0].shape[1] // LANES
    for g in range(count // LANES):
        y = picked[g * LANES : (g + 1) * LANES, :].T
        part = jnp.broadcast_to(part_ref[g : g + 1, :], (columns, LANES))
        value = y[:columns]
        for b in range(1, PACK):
            value = jnp.where(part == b, y[b * columns : (b + 1) * columns], value)
        out, t = outs[g // tiles_out], g % tiles_out
        out[:, t * LANES : (t + 1) * LANES] = value.astype(out.dtype)


def gather_kernel(row_ref, part_ref, rows_ref, *rest):
    gathered_into(128, row_ref, part_ref, rows_ref, rest[-1], rest[:-1])


def gather_colours(rows, row_list, part_list, count):
    indices = row_list.shape[0]
    columns = LANES // PACK
    return pl.pallas_call(
        gather_kernel,
        out_shape=[vmem_out((columns, indices // count), F32)] * count,
        in_specs=[SMEM, VMEM, VMEM],
        out_specs=[VMEM] * count,
        scratch_shapes=[pltpu.VMEM((indices, LANES), F32)],
        compiler_params=PARAMS,
        cost_estimate=CHEAP,
        name="gather_rows",
    )(row_list, in_vmem(part_list), in_vmem(rows))


def start_kernel(count, first, make_rows, row_ref, part_ref, source_ref, tiles_ref, *refs):
    outs, kept_ref, refs = refs[:count], refs[count], refs[count + 1 :]
    picked, sems = refs[-2:]
    size = kept_ref.shape[0] // COPIES
    copies = [
        pltpu.make_async_copy(
            tiles_ref.at[pl.ds(first + c * size, size)],
            kept_ref.at[pl.ds(c * size, size)],
            sems.at[c],
        )
        for c in range(COPIES)
    ]
    if make_rows:
        block_ref = refs[1]
        block_copy = pltpu.make_async_copy(source_ref, block_ref, sems.at[COPIES])
        block_copy.start()
    for copy in copies:
        copy.start()
    if make_rows:
        block_copy.wait()
    rows_ref = source_ref
    if make_rows:
        rows_ref = refs[0]
        transposed_into(block_ref, rows_ref)
    gathered_into(128, row_ref, part_ref, rows_ref, picked, outs)
    for copy in copies:
        copy.wait()


def start_gather(source, row_list, part_list, count, tiles, first, kept, make_rows):
    indices = row_list.shape[0]
    columns = LANES // PACK
    outs = [vmem_out((columns, indices // count), BF16)] * count
    outs.append(vmem_out((kept, *tiles.shape[1:]), tiles.dtype))
    if make_rows:
        outs.append(vmem_out((source.shape[1] // PACK, LANES), F32))
        outs.append(vmem_out(source.shape, source.dtype))
    source = in_hbm(source) if make_rows else in_vmem(source)
    return pl.pallas_call(
        functools.partial(start_kernel, count, first, make_rows),
        out_shape=outs,
        in_specs=[SMEM, VMEM, HBM if make_rows else VMEM, HBM],
        out_specs=[VMEM] * len(outs),
        scratch_shapes=[pltpu.VMEM((indices, LANES), F32), pltpu.SemaphoreType.DMA((COPIES + 1,))],
        compiler_params=PARAMS,
        cost_estimate=CHEAP,
        name="start_gather",
    )(row_list, in_vmem(part_list), source, in_hbm(tiles))


def own_slots(block_ref, tiles_ref, own_ref):
    tile_size = tiles_ref.shape[1]
    for t in range(own_ref.shape[1] // tile_size):
        at = slice(t * tile_size, (t + 1) * tile_size)
        own_ref[:, at] = jnp.dot(block_ref[:, at], tiles_ref[t], preferred_element_type=F32)


def first_own_kernel(block_ref, tiles_ref, own_ref):
    own_slots(block_ref, tiles_ref, own_ref)


def first_own(block, tiles):
    return pl.pallas_call(
        first_own_kernel,
        out_shape=vmem_out(block.shape, F32),
        in_specs=[VMEM] * 2,
        out_specs=VMEM,
        compiler_params=PARAMS,
        cost_estimate=CHEAP,
        name="first_own",
    )(in_vmem(block), in_vmem(tiles))


def later_own_kernel(total_states, *refs):
    grams, stacked, tiles_ref = refs[:4], refs[4], refs[5]
    block_ref, matrix_ref, own_ref = refs[6:]
    matrix = apply_matrix(inverse_factor(gram_of([r[...] for r in grams], total_states)))
    matrix_ref[...] = matrix
    for c in range(0, block_ref.shape[1], CHUNK):
        block_ref[:, c : c + CHUNK] = applied(matrix, stacked[:, c : c + CHUNK]).astype(BF16)
    own_slots(block_ref, tiles_ref, own_ref)


def later_own(grams, stacked, tiles, total_states):
    columns, states = stacked.shape[0] // 3, stacked.shape[1]
    return pl.pallas_call(
        functools.partial(later_own_kernel, total_states),
        out_shape=[
            vmem_out((columns, states), BF16),
            vmem_out((3 * columns, 3 * columns), BF16),
            vmem_out((columns, states), F32),
        ],
        in_specs=[VMEM] * 6,
        out_specs=[VMEM] * 3,
        compiler_params=PARAMS,
        cost_estimate=CHEAP,
        name="later_own",
    )(*[in_vmem(g) for g in grams], in_vmem(stacked), in_vmem(tiles))


def product_kernel(colours, group, with_rows, *refs):
    src_ref, dst_ref, count_ref, block_ref, own_ref = refs[:5]
    ghosts, refs = refs[5 : 5 + colours], refs[5 + colours :]
    matrix_ref = None
    if ghosts[0].dtype == F32:
        matrix_ref, refs = refs[0], refs[1:]
    tiles_ref, refs = refs[0], refs[1:]
    stacked_ref, gram_ref, refs = refs[0], refs[1], refs[2:]
    if with_rows:
        rows_ref, refs = refs[0], refs[1:]
    source, total = refs
    columns, states = block_ref.shape
    tile_size = tiles_ref.shape[1]
    first = states // tile_size
    live = count_ref[0]

    source[:, :states] = block_ref[...]
    width = ghosts[0].shape[1]
    for n, ghost in enumerate(ghosts):
        at = states + (len(ghosts) - 1 - n) * width
        value = ghost[...]
        if matrix_ref is not None:
            value = applied(matrix_ref[...], stack3(value)).astype(BF16)
        source[:, at : at + width] = value
    at = states + len(ghosts) * width
    source[:, at:] = jnp.zeros((columns, tile_size), BF16)
    nothing = at // tile_size
    total[...] = own_ref[...]

    def tile_at(s):
        index = jnp.where(s < live, src_ref[s], nothing)
        return source[:, pl.ds(pl.multiple_of(index * tile_size, tile_size), tile_size)]

    zero = jnp.zeros((columns, tile_size), BF16)

    def body(i, carry):
        base = first + i * group
        terms = []
        for u in range(0, group, 2):
            pair = jnp.concatenate(
                [
                    jnp.concatenate([tile_at(base + u), zero], axis=1),
                    jnp.concatenate([zero, tile_at(base + u + 1)], axis=1),
                ],
                axis=0,
            )
            weights = tiles_ref[pl.ds(base + u - first, 2)].reshape(2 * tile_size, tile_size)
            both = jnp.dot(pair, weights, preferred_element_type=F32)
            terms += [both[:columns], both[columns:]]
        for u in range(group):
            where = pl.multiple_of(dst_ref[base + u] * tile_size, tile_size)
            total[:, pl.ds(where, tile_size)] += terms[u]
        return carry

    lax.fori_loop(0, (live - first + group - 1) // group, body, 0)

    gram = jnp.zeros((3 * columns, 3 * columns), F32)
    for c in range(0, states, CHUNK):
        part = stack3(total[:, c : c + CHUNK])
        stacked_ref[:, c : c + CHUNK] = part
        gram += lax.dot_general(part, part, (((1,), (1,)), ((), ())), preferred_element_type=F32)
    blocks = [
        gram[a * columns : (a + 1) * columns, b * columns : (b + 1) * columns]
        for a in range(3)
        for b in range(3)
    ]
    small = blocks[8] + (blocks[5] + blocks[7])
    middle = blocks[4] + (blocks[2] + blocks[6])
    gram_ref[...] = packed(blocks[0] + ((blocks[1] + blocks[3]) + (middle + small)))
    if with_rows:
        transposed_into(total, rows_ref)


def product(src, dst, count, block, own, ghosts, matrix, tiles, with_rows):
    columns, states = block.shape
    rest, tile_size, _ = tiles.shape
    group = GROUP
    while rest % group:
        group //= 2
    outs = [vmem_out((3 * columns, states), BF16), vmem_out((columns * columns // LANES, LANES), F32)]
    if with_rows:
        outs.append(vmem_out((states // PACK, LANES), F32))
    operands = [block, own, *ghosts[::-1]] + ([] if matrix is None else [matrix]) + [tiles]
    width = states + sum(g.shape[1] for g in ghosts) + tile_size
    return pl.pallas_call(
        functools.partial(product_kernel, len(ghosts), group, with_rows),
        out_shape=outs,
        in_specs=[SMEM] * 3 + [VMEM] * len(operands),
        out_specs=[VMEM] * len(outs),
        scratch_shapes=[pltpu.VMEM((columns, width), BF16), pltpu.VMEM((columns, states), F32)],
        compiler_params=PARAMS,
        cost_estimate=CHEAP,
        name="product",
    )(src, dst, count, *[in_vmem(x) for x in operands])


def final_kernel(total_states, *refs):
    grams, stacked, out_ref, ready, sems = refs[:4], *refs[4:]
    matrix = apply_matrix(inverse_factor(gram_of([r[...] for r in grams], total_states)))
    copies = []
    for n, c in enumerate(range(0, out_ref.shape[1], CHUNK)):
        at = pl.ds(c, CHUNK)
        ready[:, at] = applied(matrix, stacked[:, at])
        copies.append(pltpu.make_async_copy(ready.at[:, at], out_ref.at[:, at], sems.at[n]))
        copies[-1].start()
    for copy in copies:
        copy.wait()


def final(grams, stacked, total_states):
    columns, states = stacked.shape[0] // 3, stacked.shape[1]
    return pl.pallas_call(
        functools.partial(final_kernel, total_states),
        out_shape=jax.ShapeDtypeStruct((columns, states), F32),
        in_specs=[VMEM] * 5,
        out_specs=HBM,
        scratch_shapes=[
            pltpu.VMEM((columns, states), F32),
            pltpu.SemaphoreType.DMA((states // CHUNK,)),
        ],
        compiler_params=PARAMS,
        cost_estimate=CHEAP,
        name="final",
    )(*[in_vmem(g) for g in grams], in_vmem(stacked))


def dom_rounds(size):
    rounds, step = [], 1
    while step < size:
        span = min(4, size // step)
        rounds.append([step * k for k in range(1, span)])
        step *= span
    return rounds[::-1]


def paired_sum(parts):
    return (parts[0] + parts[1]) + (parts[2] + parts[3])


def gram_round(gram, masks):
    parts = [gram] + [swapped(gram, mask) for mask in masks]
    return parts + [jnp.zeros_like(gram)] * (4 - len(parts))


def on_device(start_block, tiles, tile_src, tile_dst, slot_count, send_rows):
    size = lax.axis_size("dom")
    masks = [1, 2, 4, 1 << (size.bit_length() - 2)]
    columns, states = start_block.shape
    total_states = states * size
    rounds = dom_rounds(size)
    lists = send_rows[0]
    pack_states = PACK * LANES
    row_lists = lists // pack_states * LANES + lists % LANES
    part_lists = lists // LANES % PACK
    far = (3, 2)
    near = (1, 0)

    def lists_of(colours):
        rows = jnp.concatenate([row_lists[c] for c in colours])
        parts = jnp.concatenate([part_lists[c] for c in colours]).reshape(-1, LANES)
        return rows, parts

    listed = [lists_of(far), lists_of(near)]

    def sent(ghosts, colours, picked):
        for colour, x in zip(colours, picked):
            ghosts[colour] = swapped(x, masks[colour])

    own_count = states // tiles.shape[1]
    ghosts = [None] * len(masks)
    *picked, rest_tiles, start_rows, block = start_gather(
        start_block, *listed[0], len(far), tiles, own_count, tiles.shape[0] - own_count, True
    )
    sent(ghosts, far, picked)
    *picked, own_tiles = start_gather(
        start_rows, *listed[1], len(near), tiles, 0, own_count, False
    )
    sent(ghosts, near, picked)
    matrix = None
    own = first_own(block, own_tiles)
    for turn in range(ITERS):
        last = turn == ITERS - 1
        stacked, gram, *rows = product(
            tile_src, tile_dst, slot_count, block, own, ghosts, matrix, rest_tiles, not last
        )
        for masks_now in rounds[:-1]:
            gram = paired_sum(gram_round(gram, masks_now))
        if last:
            return final(gram_round(gram, rounds[-1]), stacked, total_states)
        ghosts = [None] * len(masks)
        picked = gather_colours(rows[0], *listed[0], len(far))
        gram, *picked = lax.optimization_barrier((gram, *picked))
        parts = gram_round(gram, rounds[-1])
        sent(ghosts, far, picked)
        near_rows, *parts = lax.optimization_barrier((rows[0], *parts))
        sent(ghosts, near, gather_colours(near_rows, *listed[1], len(near)))
        block, matrix, own = later_own(parts, stacked, own_tiles, total_states)


def solution(mesh):
    return jax.shard_map(
        on_device,
        mesh=mesh,
        in_specs=(
            P(None, ("groups", "dom")),
            P(("groups", "dom"), None, None),
            P(("groups", "dom")),
            P(("groups", "dom")),
            P(("groups", "dom")),
            P(("groups", "dom"), None, None),
        ),
        out_specs=P(None, ("groups", "dom")),
        check_vma=False,
    )
```

```python
import functools

import jax
import jax.numpy as jnp
from jax import lax
from jax.experimental import pallas as pl
from jax.experimental.pallas import tpu as pltpu
from jax.sharding import PartitionSpec as P

ITERS = 3
LANES = 128
PACK = 4
CHUNK = 1024
SUBLANES = 8
STEP = 8
COPIES = 8
GROUP = 128
F32 = jnp.float32
BF16 = jnp.bfloat16
VMEM = pl.BlockSpec(memory_space=pltpu.VMEM)
SMEM = pl.BlockSpec(memory_space=pltpu.SMEM)
HBM = pl.BlockSpec(memory_space=pltpu.HBM)
CHEAP = pl.CostEstimate(flops=0, bytes_accessed=1024, transcendentals=0)
PARAMS = pltpu.CompilerParams(vmem_limit_bytes=32 << 20)


def in_vmem(x):
    return pltpu.with_memory_space_constraint(x, pltpu.VMEM)


def in_hbm(x):
    return pltpu.with_memory_space_constraint(x, pltpu.HBM)


def vmem_out(shape, dtype):
    return pltpu.VMEM(shape, dtype)


def swapped(x, mask):
    size = lax.axis_size("dom")
    return lax.ppermute(x, "dom", [(i, i ^ mask) for i in range(size)])


def split3(x):
    high = x.astype(BF16)
    rest = x - high.astype(F32)
    mid = rest.astype(BF16)
    low = (rest - mid.astype(F32)).astype(BF16)
    return high, mid, low


def stack3(x):
    return jnp.concatenate(split3(x), axis=0)


def inverse_factor(gram):
    n = gram.shape[0]
    row = lax.broadcasted_iota(jnp.int32, (n, n), 0)
    col = lax.broadcasted_iota(jnp.int32, (n, n), 1)
    eye = (row == col).astype(F32)
    both = jnp.concatenate([gram, eye, jnp.zeros((n, LANES - 2 * n), F32)], axis=1)
    full = (SUBLANES, LANES)
    parts = [both[q : q + SUBLANES] for q in range(0, n, SUBLANES)]
    sub = lax.broadcasted_iota(jnp.int32, full, 0)
    scales = [jnp.zeros(full, F32) for _ in parts]
    for j in range(0, n, STEP):
        home, at = j // SUBLANES, j % SUBLANES
        live = range(home, len(parts))
        cols = [
            {q: jnp.broadcast_to(parts[q][:, j + a : j + a + 1], full) for q in live}
            for a in range(STEP)
        ]
        rows = [jnp.broadcast_to(parts[home][at + a : at + a + 1], full) for a in range(STEP)]
        entry = {
            (a, b): jnp.broadcast_to(cols[b][home][at + a : at + a + 1], full)
            for a in range(STEP)
            for b in range(a + 1)
        }
        for a in range(STEP):
            over = 1.0 / entry[a, a]
            ratio = {c: entry[c, a] * over for c in range(a + 1, STEP)}
            for c in range(a + 1, STEP):
                for d in range(a + 1, c + 1):
                    entry[c, d] = entry[c, d] - ratio[c] * entry[d, a]
            for c in range(a + 1, STEP):
                rows[c] = rows[c] - ratio[c] * rows[a]
                for q in live:
                    cols[c][q] = cols[c][q] - ratio[c] * cols[a][q]
            root = 1.0 / jnp.sqrt(entry[a, a])
            scales[home] = jnp.where(sub == at + a, root, scales[home])
            for q in live:
                factor = cols[a][q] * over
                if q == home:
                    factor = jnp.where(sub > at + a, factor, 0.0)
                parts[q] = parts[q] - factor * rows[a]
    done = jnp.concatenate([p * s for p, s in zip(parts, scales)], axis=0)
    return done[:, n : 2 * n]


def apply_matrix(inverse):
    high, mid, low = (t.astype(F32) for t in split3(inverse))
    zero = jnp.zeros_like(high)
    full = jnp.concatenate(
        [
            jnp.concatenate([high, high, high], axis=1),
            jnp.concatenate([mid, mid, zero], axis=1),
            jnp.concatenate([low, zero, zero], axis=1),
        ],
        axis=0,
    )
    return full.astype(BF16)


def applied(matrix, stacked):
    n = matrix.shape[0] // 3
    terms = jnp.dot(matrix, stacked, preferred_element_type=F32)
    return terms[:n] + (terms[n : 2 * n] + terms[2 * n :])


def packed(square):
    n = square.shape[0]
    count = LANES // n
    step = n // count
    return jnp.concatenate([square[q * step : (q + 1) * step] for q in range(count)], axis=1)


def unpacked(wide):
    step = wide.shape[0]
    n = LANES // PACK
    count = n // step
    return jnp.concatenate([wide[:, q * n : (q + 1) * n] for q in range(count)], axis=0)


def gram_of(parts, total_states):
    return unpacked(paired_sum(parts)) / total_states


def transposed_into(source, rows_ref):
    for g in range(rows_ref.shape[0] // LANES):
        pieces = [
            source[:, (PACK * g + b) * LANES : (PACK * g + b + 1) * LANES].astype(F32)
            for b in range(PACK)
        ]
        rows_ref[g * LANES : (g + 1) * LANES, :] = jnp.concatenate(pieces, axis=0).T


def gathered_into(row_ref, part_ref, rows_ref, picked, outs):
    columns, width = outs[0].shape
    tiles_out = width // LANES

    def turn(g, t, out):
        y = picked[pl.ds(pl.multiple_of(g * LANES, LANES), LANES), :].T
        part = jnp.broadcast_to(part_ref[pl.ds(g, 1), :], (columns, LANES))
        value = y[:columns]
        for b in range(1, PACK):
            value = jnp.where(part == b, y[b * columns : (b + 1) * columns], value)
        at = pl.ds(pl.multiple_of(t * LANES, LANES), LANES)
        out[:, at] = value.astype(out.dtype)

    for n, out in enumerate(outs):
        first = n * tiles_out

        def step(i, carry, first=first, out=out):
            before = jnp.maximum(i - 1, 0)
            turn(first + before, before, out)
            base = (first + i) * LANES
            for u in range(LANES):
                picked[pl.ds(base + u, 1), :] = rows_ref[pl.ds(row_ref[base + u], 1), :]
            return carry

        lax.fori_loop(0, tiles_out, step, 0)
        turn(first + tiles_out - 1, tiles_out - 1, out)


def gather_kernel(row_ref, part_ref, rows_ref, *rest):
    gathered_into(row_ref, part_ref, rows_ref, rest[-1], rest[:-1])


def gather_colours(rows, row_list, part_list, count):
    indices = row_list.shape[0]
    columns = LANES // PACK
    return pl.pallas_call(
        gather_kernel,
        out_shape=[vmem_out((columns, indices // count), F32)] * count,
        in_specs=[SMEM, VMEM, VMEM],
        out_specs=[VMEM] * count,
        scratch_shapes=[pltpu.VMEM((indices, LANES), F32)],
        compiler_params=PARAMS,
        cost_estimate=CHEAP,
        name="gather_rows",
    )(row_list, in_vmem(part_list), in_vmem(rows))


def start_kernel(count, first, make_rows, row_ref, part_ref, source_ref, tiles_ref, *refs):
    outs, kept_ref, refs = refs[:count], refs[count], refs[count + 1 :]
    picked, sems = refs[-2:]
    size = kept_ref.shape[0] // COPIES
    copies = [
        pltpu.make_async_copy(
            tiles_ref.at[pl.ds(first + c * size, size)],
            kept_ref.at[pl.ds(c * size, size)],
            sems.at[c],
        )
        for c in range(COPIES)
    ]
    if make_rows:
        block_ref = refs[1]
        block_copy = pltpu.make_async_copy(source_ref, block_ref, sems.at[COPIES])
        block_copy.start()
    for copy in copies:
        copy.start()
    if make_rows:
        block_copy.wait()
    rows_ref = source_ref
    if make_rows:
        rows_ref = refs[0]
        transposed_into(block_ref, rows_ref)
    gathered_into(row_ref, part_ref, rows_ref, picked, outs)
    for copy in copies:
        copy.wait()


def start_gather(source, row_list, part_list, count, tiles, first, kept, make_rows):
    indices = row_list.shape[0]
    columns = LANES // PACK
    outs = [vmem_out((columns, indices // count), BF16)] * count
    outs.append(vmem_out((kept, *tiles.shape[1:]), tiles.dtype))
    if make_rows:
        outs.append(vmem_out((source.shape[1] // PACK, LANES), F32))
        outs.append(vmem_out(source.shape, source.dtype))
    source = in_hbm(source) if make_rows else in_vmem(source)
    return pl.pallas_call(
        functools.partial(start_kernel, count, first, make_rows),
        out_shape=outs,
        in_specs=[SMEM, VMEM, HBM if make_rows else VMEM, HBM],
        out_specs=[VMEM] * len(outs),
        scratch_shapes=[pltpu.VMEM((indices, LANES), F32), pltpu.SemaphoreType.DMA((COPIES + 1,))],
        compiler_params=PARAMS,
        cost_estimate=CHEAP,
        name="start_gather",
    )(row_list, in_vmem(part_list), source, in_hbm(tiles))


def own_slots(block_ref, tiles_ref, own_ref):
    tile_size = tiles_ref.shape[1]
    for t in range(own_ref.shape[1] // tile_size):
        at = slice(t * tile_size, (t + 1) * tile_size)
        own_ref[:, at] = jnp.dot(block_ref[:, at], tiles_ref[t], preferred_element_type=F32)


def first_own_kernel(block_ref, tiles_ref, own_ref):
    own_slots(block_ref, tiles_ref, own_ref)


def first_own(block, tiles):
    return pl.pallas_call(
        first_own_kernel,
        out_shape=vmem_out(block.shape, F32),
        in_specs=[VMEM] * 2,
        out_specs=VMEM,
        compiler_params=PARAMS,
        cost_estimate=CHEAP,
        name="first_own",
    )(in_vmem(block), in_vmem(tiles))


def later_own_kernel(total_states, *refs):
    grams, stacked, tiles_ref = refs[:4], refs[4], refs[5]
    block_ref, matrix_ref, own_ref = refs[6:]
    matrix = apply_matrix(inverse_factor(gram_of([r[...] for r in grams], total_states)))
    matrix_ref[...] = matrix
    for c in range(0, block_ref.shape[1], CHUNK):
        block_ref[:, c : c + CHUNK] = applied(matrix, stacked[:, c : c + CHUNK]).astype(BF16)
    own_slots(block_ref, tiles_ref, own_ref)


def later_own(grams, stacked, tiles, total_states):
    columns, states = stacked.shape[0] // 3, stacked.shape[1]
    return pl.pallas_call(
        functools.partial(later_own_kernel, total_states),
        out_shape=[
            vmem_out((columns, states), BF16),
            vmem_out((3 * columns, 3 * columns), BF16),
            vmem_out((columns, states), F32),
        ],
        in_specs=[VMEM] * 6,
        out_specs=[VMEM] * 3,
        compiler_params=PARAMS,
        cost_estimate=CHEAP,
        name="later_own",
    )(*[in_vmem(g) for g in grams], in_vmem(stacked), in_vmem(tiles))


def product_kernel(colours, group, with_rows, *refs):
    src_ref, dst_ref, count_ref, block_ref, own_ref = refs[:5]
    ghosts, refs = refs[5 : 5 + colours], refs[5 + colours :]
    matrix_ref = None
    if ghosts[0].dtype == F32:
        matrix_ref, refs = refs[0], refs[1:]
    tiles_ref, refs = refs[0], refs[1:]
    stacked_ref, gram_ref, refs = refs[0], refs[1], refs[2:]
    if with_rows:
        rows_ref, refs = refs[0], refs[1:]
    source, total = refs
    columns, states = block_ref.shape
    tile_size = tiles_ref.shape[1]
    first = states // tile_size
    live = count_ref[0]

    source[:, :states] = block_ref[...]
    width = ghosts[0].shape[1]
    for n, ghost in enumerate(ghosts):
        at = states + (len(ghosts) - 1 - n) * width
        value = ghost[...]
        if matrix_ref is not None:
            value = applied(matrix_ref[...], stack3(value)).astype(BF16)
        source[:, at : at + width] = value
    at = states + len(ghosts) * width
    source[:, at:] = jnp.zeros((columns, tile_size), BF16)
    nothing = at // tile_size
    total[...] = own_ref[...]

    def tile_at(s):
        index = jnp.where(s < live, src_ref[s], nothing)
        return source[:, pl.ds(pl.multiple_of(index * tile_size, tile_size), tile_size)]

    zero = jnp.zeros((columns, tile_size), BF16)

    def body(i, carry):
        base = first + i * group
        terms = []
        for u in range(0, group, 2):
            pair = jnp.concatenate(
                [
                    jnp.concatenate([tile_at(base + u), zero], axis=1),
                    jnp.concatenate([zero, tile_at(base + u + 1)], axis=1),
                ],
                axis=0,
            )
            weights = tiles_ref[pl.ds(base + u - first, 2)].reshape(2 * tile_size, tile_size)
            both = jnp.dot(pair, weights, preferred_element_type=F32)
            terms += [both[:columns], both[columns:]]
        for u in range(group):
            where = pl.multiple_of(dst_ref[base + u] * tile_size, tile_size)
            total[:, pl.ds(where, tile_size)] += terms[u]
        return carry

    lax.fori_loop(0, (live - first + group - 1) // group, body, 0)

    gram = jnp.zeros((3 * columns, 3 * columns), F32)
    for c in range(0, states, CHUNK):
        part = stack3(total[:, c : c + CHUNK])
        stacked_ref[:, c : c + CHUNK] = part
        gram += lax.dot_general(part, part, (((1,), (1,)), ((), ())), preferred_element_type=F32)
    blocks = [
        gram[a * columns : (a + 1) * columns, b * columns : (b + 1) * columns]
        for a in range(3)
        for b in range(3)
    ]
    small = blocks[8] + (blocks[5] + blocks[7])
    middle = blocks[4] + (blocks[2] + blocks[6])
    gram_ref[...] = packed(blocks[0] + ((blocks[1] + blocks[3]) + (middle + small)))
    if with_rows:
        transposed_into(total, rows_ref)


def product(src, dst, count, block, own, ghosts, matrix, tiles, with_rows):
    columns, states = block.shape
    rest, tile_size, _ = tiles.shape
    group = GROUP
    while rest % group:
        group //= 2
    outs = [vmem_out((3 * columns, states), BF16), vmem_out((columns * columns // LANES, LANES), F32)]
    if with_rows:
        outs.append(vmem_out((states // PACK, LANES), F32))
    operands = [block, own, *ghosts[::-1]] + ([] if matrix is None else [matrix]) + [tiles]
    width = states + sum(g.shape[1] for g in ghosts) + tile_size
    return pl.pallas_call(
        functools.partial(product_kernel, len(ghosts), group, with_rows),
        out_shape=outs,
        in_specs=[SMEM] * 3 + [VMEM] * len(operands),
        out_specs=[VMEM] * len(outs),
        scratch_shapes=[pltpu.VMEM((columns, width), BF16), pltpu.VMEM((columns, states), F32)],
        compiler_params=PARAMS,
        cost_estimate=CHEAP,
        name="product",
    )(src, dst, count, *[in_vmem(x) for x in operands])


def final_kernel(total_states, *refs):
    grams, stacked, out_ref, ready, sems = refs[:4], *refs[4:]
    matrix = apply_matrix(inverse_factor(gram_of([r[...] for r in grams], total_states)))
    copies = []
    for n, c in enumerate(range(0, out_ref.shape[1], CHUNK)):
        at = pl.ds(c, CHUNK)
        ready[:, at] = applied(matrix, stacked[:, at])
        copies.append(pltpu.make_async_copy(ready.at[:, at], out_ref.at[:, at], sems.at[n]))
        copies[-1].start()
    for copy in copies:
        copy.wait()


def final(grams, stacked, total_states):
    columns, states = stacked.shape[0] // 3, stacked.shape[1]
    return pl.pallas_call(
        functools.partial(final_kernel, total_states),
        out_shape=jax.ShapeDtypeStruct((columns, states), F32),
        in_specs=[VMEM] * 5,
        out_specs=HBM,
        scratch_shapes=[
            pltpu.VMEM((columns, states), F32),
            pltpu.SemaphoreType.DMA((states // CHUNK,)),
        ],
        compiler_params=PARAMS,
        cost_estimate=CHEAP,
        name="final",
    )(*[in_vmem(g) for g in grams], in_vmem(stacked))


def dom_rounds(size):
    rounds, step = [], 1
    while step < size:
        span = min(4, size // step)
        rounds.append([step * k for k in range(1, span)])
        step *= span
    return rounds[::-1]


def paired_sum(parts):
    return (parts[0] + parts[1]) + (parts[2] + parts[3])


def gram_round(gram, masks):
    parts = [gram] + [swapped(gram, mask) for mask in masks]
    return parts + [jnp.zeros_like(gram)] * (4 - len(parts))


def on_device(start_block, tiles, tile_src, tile_dst, slot_count, send_rows):
    size = lax.axis_size("dom")
    masks = [1, 2, 4, 1 << (size.bit_length() - 2)]
    columns, states = start_block.shape
    total_states = states * size
    rounds = dom_rounds(size)
    lists = send_rows[0]
    pack_states = PACK * LANES
    row_lists = lists // pack_states * LANES + lists % LANES
    part_lists = lists // LANES % PACK
    far = (3, 2)
    near = (1, 0)

    def lists_of(colours):
        rows = jnp.concatenate([row_lists[c] for c in colours])
        parts = jnp.concatenate([part_lists[c] for c in colours]).reshape(-1, LANES)
        return rows, parts

    listed = [lists_of(far), lists_of(near)]

    def sent(ghosts, colours, picked):
        for colour, x in zip(colours, picked):
            ghosts[colour] = swapped(x, masks[colour])

    own_count = states // tiles.shape[1]
    ghosts = [None] * len(masks)
    *picked, rest_tiles, start_rows, block = start_gather(
        start_block, *listed[0], len(far), tiles, own_count, tiles.shape[0] - own_count, True
    )
    sent(ghosts, far, picked)
    *picked, own_tiles = start_gather(
        start_rows, *listed[1], len(near), tiles, 0, own_count, False
    )
    sent(ghosts, near, picked)
    matrix = None
    own = first_own(block, own_tiles)
    for turn in range(ITERS):
        last = turn == ITERS - 1
        stacked, gram, *rows = product(
            tile_src, tile_dst, slot_count, block, own, ghosts, matrix, rest_tiles, not last
        )
        for masks_now in rounds[:-1]:
            gram = paired_sum(gram_round(gram, masks_now))
        if last:
            return final(gram_round(gram, rounds[-1]), stacked, total_states)
        ghosts = [None] * len(masks)
        picked = gather_colours(rows[0], *listed[0], len(far))
        gram, *picked = lax.optimization_barrier((gram, *picked))
        parts = gram_round(gram, rounds[-1])
        sent(ghosts, far, picked)
        near_rows, *parts = lax.optimization_barrier((rows[0], *parts))
        sent(ghosts, near, gather_colours(near_rows, *listed[1], len(near)))
        block, matrix, own = later_own(parts, stacked, own_tiles, total_states)


def solution(mesh):
    return jax.shard_map(
        on_device,
        mesh=mesh,
        in_specs=(
            P(None, ("groups", "dom")),
            P(("groups", "dom"), None, None),
            P(("groups", "dom")),
            P(("groups", "dom")),
            P(("groups", "dom")),
            P(("groups", "dom"), None, None),
        ),
        out_specs=P(None, ("groups", "dom")),
        check_vma=False,
    )
```

```python
import functools

import jax
import jax.numpy as jnp
from jax import lax
from jax.experimental import pallas as pl
from jax.experimental.pallas import tpu as pltpu
from jax.sharding import PartitionSpec as P

ITERS = 3
LANES = 128
PACK = 4
CHUNK = 2048
SUBLANES = 8
STEP = 8
COPIES = 8
GROUP = 128
F32 = jnp.float32
BF16 = jnp.bfloat16
VMEM = pl.BlockSpec(memory_space=pltpu.VMEM)
SMEM = pl.BlockSpec(memory_space=pltpu.SMEM)
HBM = pl.BlockSpec(memory_space=pltpu.HBM)
CHEAP = pl.CostEstimate(flops=0, bytes_accessed=1024, transcendentals=0)
PARAMS = pltpu.CompilerParams(vmem_limit_bytes=32 << 20)


def in_vmem(x):
    return pltpu.with_memory_space_constraint(x, pltpu.VMEM)


def in_hbm(x):
    return pltpu.with_memory_space_constraint(x, pltpu.HBM)


def vmem_out(shape, dtype):
    return pltpu.VMEM(shape, dtype)


def swapped(x, mask):
    size = lax.axis_size("dom")
    return lax.ppermute(x, "dom", [(i, i ^ mask) for i in range(size)])


def split3(x):
    high = x.astype(BF16)
    rest = x - high.astype(F32)
    mid = rest.astype(BF16)
    low = (rest - mid.astype(F32)).astype(BF16)
    return high, mid, low


def stack3(x):
    return jnp.concatenate(split3(x), axis=0)


def inverse_factor(gram):
    n = gram.shape[0]
    row = lax.broadcasted_iota(jnp.int32, (n, n), 0)
    col = lax.broadcasted_iota(jnp.int32, (n, n), 1)
    eye = (row == col).astype(F32)
    both = jnp.concatenate([gram, eye, jnp.zeros((n, LANES - 2 * n), F32)], axis=1)
    full = (SUBLANES, LANES)
    parts = [both[q : q + SUBLANES] for q in range(0, n, SUBLANES)]
    sub = lax.broadcasted_iota(jnp.int32, full, 0)
    scales = [jnp.zeros(full, F32) for _ in parts]
    for j in range(0, n, STEP):
        home, at = j // SUBLANES, j % SUBLANES
        live = range(home, len(parts))
        cols = [
            {q: jnp.broadcast_to(parts[q][:, j + a : j + a + 1], full) for q in live}
            for a in range(STEP)
        ]
        rows = [jnp.broadcast_to(parts[home][at + a : at + a + 1], full) for a in range(STEP)]
        entry = {
            (a, b): jnp.broadcast_to(cols[b][home][at + a : at + a + 1], full)
            for a in range(STEP)
            for b in range(a + 1)
        }
        for a in range(STEP):
            over = 1.0 / entry[a, a]
            ratio = {c: entry[c, a] * over for c in range(a + 1, STEP)}
            for c in range(a + 1, STEP):
                for d in range(a + 1, c + 1):
                    entry[c, d] = entry[c, d] - ratio[c] * entry[d, a]
            for c in range(a + 1, STEP):
                rows[c] = rows[c] - ratio[c] * rows[a]
                for q in live:
                    cols[c][q] = cols[c][q] - ratio[c] * cols[a][q]
            root = 1.0 / jnp.sqrt(entry[a, a])
            scales[home] = jnp.where(sub == at + a, root, scales[home])
            for q in live:
                factor = cols[a][q] * over
                if q == home:
                    factor = jnp.where(sub > at + a, factor, 0.0)
                parts[q] = parts[q] - factor * rows[a]
    done = jnp.concatenate([p * s for p, s in zip(parts, scales)], axis=0)
    return done[:, n : 2 * n]


def apply_matrix(inverse):
    high, mid, low = (t.astype(F32) for t in split3(inverse))
    zero = jnp.zeros_like(high)
    full = jnp.concatenate(
        [
            jnp.concatenate([high, high, high], axis=1),
            jnp.concatenate([mid, mid, zero], axis=1),
            jnp.concatenate([low, zero, zero], axis=1),
        ],
        axis=0,
    )
    return full.astype(BF16)


def applied(matrix, stacked):
    n = matrix.shape[0] // 3
    terms = jnp.dot(matrix, stacked, preferred_element_type=F32)
    return terms[:n] + (terms[n : 2 * n] + terms[2 * n :])


def packed(square):
    n = square.shape[0]
    count = LANES // n
    step = n // count
    return jnp.concatenate([square[q * step : (q + 1) * step] for q in range(count)], axis=1)


def unpacked(wide):
    step = wide.shape[0]
    n = LANES // PACK
    count = n // step
    return jnp.concatenate([wide[:, q * n : (q + 1) * n] for q in range(count)], axis=0)


def gram_of(parts, total_states):
    return unpacked(paired_sum(parts)) / total_states


def transposed_into(source, rows_ref):
    for g in range(rows_ref.shape[0] // LANES):
        pieces = [
            source[:, (PACK * g + b) * LANES : (PACK * g + b + 1) * LANES].astype(F32)
            for b in range(PACK)
        ]
        rows_ref[g * LANES : (g + 1) * LANES, :] = jnp.concatenate(pieces, axis=0).T


def gathered_into(row_ref, part_ref, rows_ref, picked, outs):
    columns, width = outs[0].shape
    tiles_out = width // LANES

    def turn(g, t, out):
        y = picked[pl.ds(pl.multiple_of(g * LANES, LANES), LANES), :].T
        part = jnp.broadcast_to(part_ref[pl.ds(g, 1), :], (columns, LANES))
        value = y[:columns]
        for b in range(1, PACK):
            value = jnp.where(part == b, y[b * columns : (b + 1) * columns], value)
        at = pl.ds(pl.multiple_of(t * LANES, LANES), LANES)
        out[:, at] = value.astype(out.dtype)

    for n, out in enumerate(outs):
        first = n * tiles_out

        def step(i, carry, first=first, out=out):
            before = jnp.maximum(i - 1, 0)
            turn(first + before, before, out)
            base = (first + i) * LANES
            for u in range(LANES):
                picked[pl.ds(base + u, 1), :] = rows_ref[pl.ds(row_ref[base + u], 1), :]
            return carry

        lax.fori_loop(0, tiles_out, step, 0)
        turn(first + tiles_out - 1, tiles_out - 1, out)


def gather_kernel(row_ref, part_ref, rows_ref, *rest):
    gathered_into(row_ref, part_ref, rows_ref, rest[-1], rest[:-1])


def gather_colours(rows, row_list, part_list, count):
    indices = row_list.shape[0]
    columns = LANES // PACK
    return pl.pallas_call(
        gather_kernel,
        out_shape=[vmem_out((columns, indices // count), F32)] * count,
        in_specs=[SMEM, VMEM, VMEM],
        out_specs=[VMEM] * count,
        scratch_shapes=[pltpu.VMEM((indices, LANES), F32)],
        compiler_params=PARAMS,
        cost_estimate=CHEAP,
        name="gather_rows",
    )(row_list, in_vmem(part_list), in_vmem(rows))


def start_kernel(count, first, make_rows, row_ref, part_ref, source_ref, tiles_ref, *refs):
    outs, kept_ref, refs = refs[:count], refs[count], refs[count + 1 :]
    picked, sems = refs[-2:]
    size = kept_ref.shape[0] // COPIES
    copies = [
        pltpu.make_async_copy(
            tiles_ref.at[pl.ds(first + c * size, size)],
            kept_ref.at[pl.ds(c * size, size)],
            sems.at[c],
        )
        for c in range(COPIES)
    ]
    if make_rows:
        block_ref = refs[1]
        block_copy = pltpu.make_async_copy(source_ref, block_ref, sems.at[COPIES])
        block_copy.start()
    for copy in copies:
        copy.start()
    if make_rows:
        block_copy.wait()
    rows_ref = source_ref
    if make_rows:
        rows_ref = refs[0]
        transposed_into(block_ref, rows_ref)
    gathered_into(row_ref, part_ref, rows_ref, picked, outs)
    for copy in copies:
        copy.wait()


def start_gather(source, row_list, part_list, count, tiles, first, kept, make_rows):
    indices = row_list.shape[0]
    columns = LANES // PACK
    outs = [vmem_out((columns, indices // count), BF16)] * count
    outs.append(vmem_out((kept, *tiles.shape[1:]), tiles.dtype))
    if make_rows:
        outs.append(vmem_out((source.shape[1] // PACK, LANES), F32))
        outs.append(vmem_out(source.shape, source.dtype))
    source = in_hbm(source) if make_rows else in_vmem(source)
    return pl.pallas_call(
        functools.partial(start_kernel, count, first, make_rows),
        out_shape=outs,
        in_specs=[SMEM, VMEM, HBM if make_rows else VMEM, HBM],
        out_specs=[VMEM] * len(outs),
        scratch_shapes=[pltpu.VMEM((indices, LANES), F32), pltpu.SemaphoreType.DMA((COPIES + 1,))],
        compiler_params=PARAMS,
        cost_estimate=CHEAP,
        name="start_gather",
    )(row_list, in_vmem(part_list), source, in_hbm(tiles))


def own_slots(block_ref, tiles_ref, own_ref):
    tile_size = tiles_ref.shape[1]
    for t in range(own_ref.shape[1] // tile_size):
        at = slice(t * tile_size, (t + 1) * tile_size)
        own_ref[:, at] = jnp.dot(block_ref[:, at], tiles_ref[t], preferred_element_type=F32)


def first_own_kernel(block_ref, tiles_ref, own_ref):
    own_slots(block_ref, tiles_ref, own_ref)


def first_own(block, tiles):
    return pl.pallas_call(
        first_own_kernel,
        out_shape=vmem_out(block.shape, F32),
        in_specs=[VMEM] * 2,
        out_specs=VMEM,
        compiler_params=PARAMS,
        cost_estimate=CHEAP,
        name="first_own",
    )(in_vmem(block), in_vmem(tiles))


def later_own_kernel(total_states, *refs):
    grams, stacked, tiles_ref = refs[:4], refs[4], refs[5]
    block_ref, matrix_ref, own_ref = refs[6:]
    matrix = apply_matrix(inverse_factor(gram_of([r[...] for r in grams], total_states)))
    matrix_ref[...] = matrix
    for c in range(0, block_ref.shape[1], CHUNK):
        block_ref[:, c : c + CHUNK] = applied(matrix, stacked[:, c : c + CHUNK]).astype(BF16)
    own_slots(block_ref, tiles_ref, own_ref)


def later_own(grams, stacked, tiles, total_states):
    columns, states = stacked.shape[0] // 3, stacked.shape[1]
    return pl.pallas_call(
        functools.partial(later_own_kernel, total_states),
        out_shape=[
            vmem_out((columns, states), BF16),
            vmem_out((3 * columns, 3 * columns), BF16),
            vmem_out((columns, states), F32),
        ],
        in_specs=[VMEM] * 6,
        out_specs=[VMEM] * 3,
        compiler_params=PARAMS,
        cost_estimate=CHEAP,
        name="later_own",
    )(*[in_vmem(g) for g in grams], in_vmem(stacked), in_vmem(tiles))


def product_kernel(colours, group, with_rows, *refs):
    src_ref, dst_ref, count_ref, block_ref, own_ref = refs[:5]
    ghosts, refs = refs[5 : 5 + colours], refs[5 + colours :]
    matrix_ref = None
    if ghosts[0].dtype == F32:
        matrix_ref, refs = refs[0], refs[1:]
    tiles_ref, refs = refs[0], refs[1:]
    stacked_ref, gram_ref, refs = refs[0], refs[1], refs[2:]
    if with_rows:
        rows_ref, refs = refs[0], refs[1:]
    source, total = refs
    columns, states = block_ref.shape
    tile_size = tiles_ref.shape[1]
    first = states // tile_size
    live = count_ref[0]

    source[:, :states] = block_ref[...]
    width = ghosts[0].shape[1]
    for n, ghost in enumerate(ghosts):
        at = states + (len(ghosts) - 1 - n) * width
        value = ghost[...]
        if matrix_ref is not None:
            value = applied(matrix_ref[...], stack3(value)).astype(BF16)
        source[:, at : at + width] = value
    at = states + len(ghosts) * width
    source[:, at:] = jnp.zeros((columns, tile_size), BF16)
    nothing = at // tile_size
    total[...] = own_ref[...]

    def tile_at(s):
        index = jnp.where(s < live, src_ref[s], nothing)
        return source[:, pl.ds(pl.multiple_of(index * tile_size, tile_size), tile_size)]

    zero = jnp.zeros((columns, tile_size), BF16)

    def body(i, carry):
        base = first + i * group
        terms = []
        for u in range(0, group, 2):
            pair = jnp.concatenate(
                [
                    jnp.concatenate([tile_at(base + u), zero], axis=1),
                    jnp.concatenate([zero, tile_at(base + u + 1)], axis=1),
                ],
                axis=0,
            )
            weights = tiles_ref[pl.ds(base + u - first, 2)].reshape(2 * tile_size, tile_size)
            both = jnp.dot(pair, weights, preferred_element_type=F32)
            terms += [both[:columns], both[columns:]]
        for u in range(group):
            where = pl.multiple_of(dst_ref[base + u] * tile_size, tile_size)
            total[:, pl.ds(where, tile_size)] += terms[u]
        return carry

    lax.fori_loop(0, (live - first + group - 1) // group, body, 0)

    gram = jnp.zeros((3 * columns, 3 * columns), F32)
    for c in range(0, states, CHUNK):
        part = stack3(total[:, c : c + CHUNK])
        stacked_ref[:, c : c + CHUNK] = part
        gram += lax.dot_general(part, part, (((1,), (1,)), ((), ())), preferred_element_type=F32)
    blocks = [
        gram[a * columns : (a + 1) * columns, b * columns : (b + 1) * columns]
        for a in range(3)
        for b in range(3)
    ]
    small = blocks[8] + (blocks[5] + blocks[7])
    middle = blocks[4] + (blocks[2] + blocks[6])
    gram_ref[...] = packed(blocks[0] + ((blocks[1] + blocks[3]) + (middle + small)))
    if with_rows:
        transposed_into(total, rows_ref)


def product(src, dst, count, block, own, ghosts, matrix, tiles, with_rows):
    columns, states = block.shape
    rest, tile_size, _ = tiles.shape
    group = GROUP
    while rest % group:
        group //= 2
    outs = [vmem_out((3 * columns, states), BF16), vmem_out((columns * columns // LANES, LANES), F32)]
    if with_rows:
        outs.append(vmem_out((states // PACK, LANES), F32))
    operands = [block, own, *ghosts[::-1]] + ([] if matrix is None else [matrix]) + [tiles]
    width = states + sum(g.shape[1] for g in ghosts) + tile_size
    return pl.pallas_call(
        functools.partial(product_kernel, len(ghosts), group, with_rows),
        out_shape=outs,
        in_specs=[SMEM] * 3 + [VMEM] * len(operands),
        out_specs=[VMEM] * len(outs),
        scratch_shapes=[pltpu.VMEM((columns, width), BF16), pltpu.VMEM((columns, states), F32)],
        compiler_params=PARAMS,
        cost_estimate=CHEAP,
        name="product",
    )(src, dst, count, *[in_vmem(x) for x in operands])


def final_kernel(total_states, *refs):
    grams, stacked, out_ref, ready, sems = refs[:4], *refs[4:]
    matrix = apply_matrix(inverse_factor(gram_of([r[...] for r in grams], total_states)))
    copies = []
    for n, c in enumerate(range(0, out_ref.shape[1], CHUNK)):
        at = pl.ds(c, CHUNK)
        ready[:, at] = applied(matrix, stacked[:, at])
        copies.append(pltpu.make_async_copy(ready.at[:, at], out_ref.at[:, at], sems.at[n]))
        copies[-1].start()
    for copy in copies:
        copy.wait()


def final(grams, stacked, total_states):
    columns, states = stacked.shape[0] // 3, stacked.shape[1]
    return pl.pallas_call(
        functools.partial(final_kernel, total_states),
        out_shape=jax.ShapeDtypeStruct((columns, states), F32),
        in_specs=[VMEM] * 5,
        out_specs=HBM,
        scratch_shapes=[
            pltpu.VMEM((columns, states), F32),
            pltpu.SemaphoreType.DMA((states // CHUNK,)),
        ],
        compiler_params=PARAMS,
        cost_estimate=CHEAP,
        name="final",
    )(*[in_vmem(g) for g in grams], in_vmem(stacked))


def dom_rounds(size):
    rounds, step = [], 1
    while step < size:
        span = min(4, size // step)
        rounds.append([step * k for k in range(1, span)])
        step *= span
    return rounds[::-1]


def paired_sum(parts):
    return (parts[0] + parts[1]) + (parts[2] + parts[3])


def gram_round(gram, masks):
    parts = [gram] + [swapped(gram, mask) for mask in masks]
    return parts + [jnp.zeros_like(gram)] * (4 - len(parts))


def on_device(start_block, tiles, tile_src, tile_dst, slot_count, send_rows):
    size = lax.axis_size("dom")
    masks = [1, 2, 4, 1 << (size.bit_length() - 2)]
    columns, states = start_block.shape
    total_states = states * size
    rounds = dom_rounds(size)
    lists = send_rows[0]
    pack_states = PACK * LANES
    row_lists = lists // pack_states * LANES + lists % LANES
    part_lists = lists // LANES % PACK
    far = (3, 2)
    near = (1, 0)

    def lists_of(colours):
        rows = jnp.concatenate([row_lists[c] for c in colours])
        parts = jnp.concatenate([part_lists[c] for c in colours]).reshape(-1, LANES)
        return rows, parts

    listed = [lists_of(far), lists_of(near)]

    def sent(ghosts, colours, picked):
        for colour, x in zip(colours, picked):
            ghosts[colour] = swapped(x, masks[colour])

    own_count = states // tiles.shape[1]
    ghosts = [None] * len(masks)
    *picked, rest_tiles, start_rows, block = start_gather(
        start_block, *listed[0], len(far), tiles, own_count, tiles.shape[0] - own_count, True
    )
    sent(ghosts, far, picked)
    *picked, own_tiles = start_gather(
        start_rows, *listed[1], len(near), tiles, 0, own_count, False
    )
    sent(ghosts, near, picked)
    matrix = None
    own = first_own(block, own_tiles)
    for turn in range(ITERS):
        last = turn == ITERS - 1
        stacked, gram, *rows = product(
            tile_src, tile_dst, slot_count, block, own, ghosts, matrix, rest_tiles, not last
        )
        for masks_now in rounds[:-1]:
            gram = paired_sum(gram_round(gram, masks_now))
        if last:
            return final(gram_round(gram, rounds[-1]), stacked, total_states)
        ghosts = [None] * len(masks)
        picked = gather_colours(rows[0], *listed[0], len(far))
        gram, *picked = lax.optimization_barrier((gram, *picked))
        parts = gram_round(gram, rounds[-1])
        sent(ghosts, far, picked)
        near_rows, *parts = lax.optimization_barrier((rows[0], *parts))
        sent(ghosts, near, gather_colours(near_rows, *listed[1], len(near)))
        block, matrix, own = later_own(parts, stacked, own_tiles, total_states)


def solution(mesh):
    return jax.shard_map(
        on_device,
        mesh=mesh,
        in_specs=(
            P(None, ("groups", "dom")),
            P(("groups", "dom"), None, None),
            P(("groups", "dom")),
            P(("groups", "dom")),
            P(("groups", "dom")),
            P(("groups", "dom"), None, None),
        ),
        out_specs=P(None, ("groups", "dom")),
        check_vma=False,
    )
```
